32 devices in a mesh: dp: 8 (over z, x), rows: 4 (over y, core).
Axes of the slice: x: 2, y: 2, z: 4, core: 2. Of those that a mesh axis runs over, the one named last changes fastest.
Arguments:
- tokens: bfloat16 [4096, 1024], P(('dp', 'rows')), parts along dimension 0, may hold values from -6 to 6
- timestep: int32 [8], P('dp'), parts along dimension 0, may hold values from 0 to 999
- timestep_gain_map: float32 [256, 1024], replicated, may hold values from -0.25 to 0.25
- query_key_value_weight: bfloat16 [1024, 3072], P('rows'), may hold values from -0.1875 to 0.1875
- adapter_down_weight: bfloat16 [1024, 16], replicated, may hold values from -0.1875 to 0.1875
- adapter_up_weight: bfloat16 [16, 3072], replicated, may hold values from -1.5 to 1.5
- head_score_scale: float32 [16], P('rows'), may hold values from 4 to 12
- heads_output_grad: bfloat16 [4096, 1024], P(('dp', 'rows')), parts along dimension 0, may hold values from -6 to 6
Outputs:
- input_grad: bfloat16 [4096, 1024], P(('dp', 'rows')), parts along dimension 0
- down_grad: float32 [8192, 16], P('dp'), parts along dimension 0
- up_grad: float32 [128, 3072], P('dp'), parts along dimension 0
The draws below stay inside these ranges and needn't reach their ends.
There are 8 independent parts, one for each index of `dp`. The reference program is written for one: setup_inputs(seed, part) draws one part's arguments, and reference() takes and returns one part's arrays. A program takes and returns all parts, laid end to end along the dimension named above; an argument that names none is the same for every part. Nothing has to cross between parts.
All inputs are finite; a program needn't handle non-finite values.
Results may differ from the reference program's by a relative error of at most 0.012.
Values may be sent and summed in bfloat16 or wider, within the bound.
No kernel may reach another device: no remote copies, remote signals or barrier semaphores. Data moves between devices by JAX's collectives and lax.ppermute only.
A program may use at most 64 MiB of HBM per device.

```python
import math
import jax
import jax.numpy as jnp
from jax import lax

H = 16
HEAD = 64
MODEL_DIM = 1024
ADAPTER_RANK = 16
EMB = 256
TOKENS = 512


def shard_levels(own_key, dims, shards, low, high):
    def one(axis_at, shards_of):
        steps = jax.random.uniform(jax.random.fold_in(jax.random.fold_in(own_key, 6), axis_at), (shards_of,), jnp.float32, low / len(shards), high / len(shards))
        return jnp.repeat(jnp.exp(steps), dims[axis_at] // shards_of).reshape((-1,) + (1,) * (len(dims) - axis_at - 1))

    gain = one(*shards[0])
    for cut in shards[1:]:
        gain = gain * one(*cut)
    return gain


def noise(key, shape, spread, limit, pieces=(), kind=jnp.bfloat16):
    array = spread * jax.random.normal(key, shape, jnp.float32)
    if pieces:
        array = array * shard_levels(key, shape, pieces, -0.22, 0.18)
    return jnp.clip(array, -limit, limit).astype(kind)


def setup_inputs(seed: int = 0, part: int = 0) -> dict:
    key_list = jax.random.split(jax.random.key(seed), 9)
    part_splits = jax.random.split(jax.random.fold_in(key_list[8], part), 9)
    return {
        "tokens": noise(part_splits[0], (TOKENS, MODEL_DIM), 1.0, 6.0, ((0, 4),)),
        "timestep": jax.random.randint(part_splits[1], (1,), 0, 1000).astype(jnp.int32),
        "timestep_gain_map": noise(key_list[2], (EMB, MODEL_DIM), (2 * EMB) ** -0.5, 0.25, (), jnp.float32),
        "query_key_value_weight": noise(key_list[3], (MODEL_DIM, 3 * MODEL_DIM), MODEL_DIM ** -0.5, 0.1875, ((0, 4),)),
        "adapter_down_weight": noise(key_list[4], (MODEL_DIM, ADAPTER_RANK), MODEL_DIM ** -0.5, 0.1875),
        "adapter_up_weight": noise(key_list[5], (ADAPTER_RANK, 3 * MODEL_DIM), ADAPTER_RANK ** -0.5, 1.5),
        "head_score_scale": jnp.clip(jnp.exp(math.log(12.0) - 1.0986123 * jax.random.uniform(key_list[6], (H,), jnp.float32) ** shard_levels(key_list[6], (H,), ((0, 4),), -0.2, 0.2)), 4.0, 12.0),
        "heads_output_grad": noise(part_splits[7], (TOKENS, MODEL_DIM), 1.0, 6.0, ((0, 4),)),
    }


eps = 1e-06

def time_features(timestep):
    half_emb = EMB // 2
    frequency = jnp.exp(-math.log(10000.0) * jnp.arange(half_emb, dtype=jnp.float32) / half_emb)
    phases = timestep.astype(jnp.float32)[0] * frequency
    return jnp.concatenate([jnp.cos(phases), jnp.sin(phases)])

def head_backward(query_rows, key_rows, value_rows, grad_out, scaling):
    seq_len = query_rows.shape[0]
    block_rows = math.gcd(512, seq_len)
    query_f = query_rows.astype(jnp.float32)
    key_f = key_rows.astype(jnp.float32)
    query_inv = lax.rsqrt(lax.optimization_barrier(jnp.sum(query_f * query_f, -1, keepdims=True)) + eps)
    key_inv = lax.rsqrt(lax.optimization_barrier(jnp.sum(key_f * key_f, -1, keepdims=True)) + eps)
    query_unit = query_f * query_inv
    key_unit = key_f * key_inv
    query_low = query_unit.astype(jnp.bfloat16)
    key_low = key_unit.astype(jnp.bfloat16)

    def step_block(carry, block_index):
        key_acc, value_acc = carry
        row_start = block_index * block_rows
        query_block = lax.dynamic_slice_in_dim(query_low, row_start, block_rows, 0)
        grad_block = lax.dynamic_slice_in_dim(grad_out, row_start, block_rows, 0)
        scores = scaling * jnp.dot(query_block, key_low.T, preferred_element_type=jnp.float32)
        exponent = jnp.exp(scores)
        attention = exponent / lax.optimization_barrier(jnp.sum(exponent, -1, keepdims=True))
        value_acc = value_acc + jnp.dot(attention.astype(jnp.bfloat16).T, grad_block, preferred_element_type=jnp.float32)
        grad_probs = jnp.dot(grad_block, value_rows.T, preferred_element_type=jnp.float32)
        row_delta = lax.optimization_barrier(jnp.sum(attention * grad_probs, -1, keepdims=True))
        grad_scores = (attention * (grad_probs - row_delta)).astype(jnp.bfloat16)
        grad_qunit = scaling * jnp.dot(grad_scores, key_low, preferred_element_type=jnp.float32)
        key_acc = key_acc + scaling * jnp.dot(grad_scores.T, query_block, preferred_element_type=jnp.float32)
        unit_block = lax.dynamic_slice_in_dim(query_unit, row_start, block_rows, 0)
        inv_block = lax.dynamic_slice_in_dim(query_inv, row_start, block_rows, 0)
        grad_query = inv_block * (grad_qunit - unit_block * lax.optimization_barrier(jnp.sum(unit_block * grad_qunit, -1, keepdims=True)))
        return ((key_acc, value_acc), grad_query.astype(jnp.bfloat16))
    zeros_acc = jnp.zeros((seq_len, query_rows.shape[1]), jnp.float32)
    (key_acc, value_acc), query_blocks = lax.scan(step_block, (zeros_acc, zeros_acc), jnp.arange(seq_len // block_rows, dtype=jnp.int32))
    grad_query = query_blocks.reshape(seq_len, query_rows.shape[1])
    grad_key = key_inv * (key_acc - key_unit * lax.optimization_barrier(jnp.sum(key_unit * key_acc, -1, keepdims=True)))
    return (grad_query, grad_key.astype(jnp.bfloat16), value_acc.astype(jnp.bfloat16))

def reference(tokens, timestep, timestep_gain_map, query_key_value_weight, adapter_down_weight, adapter_up_weight, head_score_scale, heads_output_grad):
    features = time_features(timestep)
    ada_gain = 1.0 + jnp.dot(features, timestep_gain_map, precision=lax.Precision.HIGHEST)
    tokens_f = tokens.astype(jnp.float32)
    inv_rms = lax.rsqrt(lax.optimization_barrier(jnp.mean(tokens_f * tokens_f, -1, keepdims=True)) + eps)
    normalized_input = (tokens_f * inv_rms * ada_gain).astype(jnp.bfloat16)
    low_rank_output = jnp.dot(normalized_input, adapter_down_weight, preferred_element_type=jnp.float32).astype(jnp.bfloat16)
    projected_rows = (jnp.dot(normalized_input, query_key_value_weight, preferred_element_type=jnp.float32) + 0.5 * jnp.dot(low_rank_output, adapter_up_weight, preferred_element_type=jnp.float32)).astype(jnp.bfloat16)
    seq_len = tokens.shape[0]
    packed = jnp.concatenate([projected_rows.reshape(seq_len, H, 3 * HEAD), heads_output_grad.reshape(seq_len, H, HEAD)], axis=2)
    packed = jnp.transpose(packed, (1, 0, 2))

    def one_head(inputs):
        head_cols, scaling = inputs
        return head_backward(head_cols[:, :HEAD], head_cols[:, HEAD:2 * HEAD], head_cols[:, 2 * HEAD:3 * HEAD], head_cols[:, 3 * HEAD:], scaling)
    grad_q, grad_k, grad_v = lax.map(one_head, (packed, head_score_scale))
    grad_heads = jnp.concatenate([grad_q, grad_k, grad_v], axis=2)
    projected_grad = jnp.transpose(grad_heads, (1, 0, 2)).reshape(seq_len, 3 * MODEL_DIM)
    low_rank_grad = (0.5 * jnp.dot(projected_grad, adapter_up_weight.T, preferred_element_type=jnp.float32)).astype(jnp.bfloat16)
    normalized_grad = jnp.dot(projected_grad, query_key_value_weight.T, preferred_element_type=jnp.float32) + jnp.dot(low_rank_grad, adapter_down_weight.T, preferred_element_type=jnp.float32)
    up_grad = 0.5 * jnp.dot(low_rank_output.T, projected_grad, preferred_element_type=jnp.float32)
    down_grad = jnp.dot(normalized_input.T, low_rank_grad, preferred_element_type=jnp.float32)
    scaled = normalized_grad * ada_gain
    input_grad = inv_rms * (scaled - tokens_f * inv_rms * inv_rms * lax.optimization_barrier(jnp.mean(scaled * tokens_f, -1, keepdims=True)))
    return (input_grad.astype(jnp.bfloat16), down_grad, up_grad)
```

```python
import functools
import math

import jax
import jax.numpy as jnp
from jax import lax
from jax.experimental import pallas as pl
from jax.experimental.pallas import tpu as pltpu
from jax.sharding import PartitionSpec as P

HEAD = 64
EMB = 256
EPS = 1e-06
LOG2E = 1.4426950408889634
BF = jnp.bfloat16
F32 = jnp.float32


def time_features(timestep):
    half_emb = EMB // 2
    frequency = jnp.exp(-math.log(10000.0) * jnp.arange(half_emb, dtype=F32) / half_emb)
    phases = timestep.astype(F32)[0] * frequency
    return jnp.concatenate([jnp.cos(phases), jnp.sin(phases)])


def contract(a, b, a_dim, b_dim):
    return lax.dot_general(a, b, (((a_dim,), (b_dim,)), ((), ())), preferred_element_type=F32)


def attention_kernel(n, heads, piece_rows, *refs):
    pieces = len(piece_rows)
    refs = list(refs)
    bases, scale = refs.pop(0), refs.pop(0)
    normed_in = [refs.pop(0) for _ in range(n)]
    weight_in = [refs.pop(0) for _ in range(pieces)]
    cot_in = [refs.pop(0) for _ in range(n)]
    down, up = refs.pop(0), refs.pop(0)
    parts = [refs.pop(0) for _ in range(n)]
    pack = refs.pop(0)
    normed, weight, cot, qkv_t, cot_t, grad_t, sems = refs

    tok = normed_in[0].shape[0]
    seq = n * tok
    cols = weight.shape[1]
    copies = []
    for j in range(n):
        copies.append((normed_in[j], normed.at[pl.ds(j * tok, tok)]))
        copies.append((cot_in[j], cot.at[pl.ds(j * tok, tok)]))
    for i, rows in enumerate(piece_rows):
        base = pl.multiple_of(bases[i], 16)
        copies.append((weight_in[i], weight.at[pl.ds(base, rows)]))
    copies = [pltpu.make_async_copy(a, b, sems.at[i]) for i, (a, b) in enumerate(copies)]
    for c in copies:
        c.start()
    for c in copies:
        c.wait()

    step = math.gcd(512, seq)
    up_all = up[...]
    low_t = []
    for s in range(0, seq, step):
        x = normed[pl.ds(s, step), :]
        low = jnp.dot(x, down[...], preferred_element_type=F32).astype(BF)
        low_t.append(low.T)
        qkv = jnp.dot(x, weight[...], preferred_element_type=F32)
        qkv = qkv + 0.5 * jnp.dot(low, up_all, preferred_element_type=F32)
        qkv_t[:, pl.ds(s, step)] = qkv.astype(BF).T
        cot_t[:, pl.ds(s, step)] = cot[pl.ds(s, step), :].T

    for h in range(heads):
        o = 3 * HEAD * h
        kf = qkv_t[pl.ds(o + HEAD, HEAD), :].astype(F32)
        k_inv = lax.rsqrt(jnp.sum(kf * kf, 0, keepdims=True) + EPS)
        k_unit = kf * k_inv
        k_low = k_unit.astype(BF)
        v = qkv_t[pl.ds(o + 2 * HEAD, HEAD), :]
        sc = scale[h]
        gk = gv = None
        for s in range(0, seq, step):
            qf = qkv_t[pl.ds(o, HEAD), pl.ds(s, step)].astype(F32)
            q_inv = lax.rsqrt(jnp.sum(qf * qf, 0, keepdims=True) + EPS)
            q_unit = qf * q_inv
            q_low = q_unit.astype(BF)
            g = cot_t[pl.ds(HEAD * h, HEAD), pl.ds(s, step)]
            e = jnp.exp2(contract(k_low, q_low, 0, 0) * (sc * LOG2E))
            attention = e * (1.0 / jnp.sum(e, 0, keepdims=True))
            grad_probs = contract(v, g, 0, 0)
            delta = jnp.sum(attention * grad_probs, 0, keepdims=True)
            grad_scores = (attention * (grad_probs - delta)).astype(BF)
            gv_s = contract(g, attention.astype(BF), 1, 1)
            gk_s = sc * contract(q_low, grad_scores, 1, 1)
            gq = sc * jnp.dot(k_low, grad_scores, preferred_element_type=F32)
            gq = q_inv * (gq - q_unit * jnp.sum(q_unit * gq, 0, keepdims=True))
            grad_t[pl.ds(o, HEAD), pl.ds(s, step)] = gq.astype(BF)
            gv = gv_s if gv is None else gv + gv_s
            gk = gk_s if gk is None else gk + gk_s
        gk = k_inv * (gk - k_unit * jnp.sum(k_unit * gk, 0, keepdims=True))
        grad_t[pl.ds(o + HEAD, HEAD), :] = gk.astype(BF)
        grad_t[pl.ds(o + 2 * HEAD, HEAD), :] = gv.astype(BF)

    up_part = None
    for i, s in enumerate(range(0, seq, step)):
        gt = grad_t[:, pl.ds(s, step)]
        term = contract(low_t[i], gt, 1, 1)
        up_part = term if up_part is None else up_part + term
        low_grad_t = 0.5 * jnp.dot(up_all, gt, preferred_element_type=F32)
        pack[pl.ds(up.shape[0], up.shape[0]), pl.ds(s, step)] = low_grad_t
        grad = gt.T
        part = contract(grad, weight[...], 1, 1)
        part = part + contract(low_grad_t.astype(BF).T, down[...], 1, 1)
        for b in range(step // tok):
            j = s // tok + b
            parts[j][...] = part[b * tok : (b + 1) * tok].astype(parts[j].dtype)
    pack[pl.ds(0, up.shape[0]), pl.ds(0, cols)] = 0.5 * up_part


def attention_call(bases, scale, normed, pieces, cot, down, up):
    n = len(normed)
    tok, width = normed[0].shape
    seq = n * tok
    cols = pieces[0].shape[1]
    heads = cols // (3 * HEAD)
    rank = up.shape[0]
    any_ = pl.BlockSpec(memory_space=pl.ANY)
    smem = pl.BlockSpec(memory_space=pltpu.SMEM)
    vmem = pl.BlockSpec(memory_space=pltpu.VMEM)
    total = 2 * n + len(pieces)
    out_shape = [jax.ShapeDtypeStruct((tok, width), BF if j % 2 else F32) for j in range(n)]
    out_shape.append(jax.ShapeDtypeStruct((2 * rank, max(cols, seq)), F32))
    return pl.pallas_call(
        functools.partial(attention_kernel, n, heads, tuple(p.shape[0] for p in pieces)),
        out_shape=out_shape,
        in_specs=[smem, smem] + [any_] * total + [vmem, vmem],
        out_specs=[vmem] * (n + 1),
        scratch_shapes=[
            pltpu.VMEM((seq, width), BF),
            pltpu.VMEM((width, cols), BF),
            pltpu.VMEM((seq, cols // 3), BF),
            pltpu.VMEM((cols, seq), BF),
            pltpu.VMEM((cols // 3, seq), BF),
            pltpu.VMEM((cols, seq), BF),
            pltpu.SemaphoreType.DMA((total,)),
        ],
        compiler_params=pltpu.CompilerParams(vmem_limit_bytes=48 * 1024 * 1024),
        name="attention_grads",
    )(bases, scale, *normed, *pieces, *cot, down, up)


def per_device(
    mesh_shape,
    tokens,
    timestep,
    timestep_gain_map,
    query_key_value_weight,
    adapter_down_weight,
    adapter_up_weight,
    head_score_scale,
    heads_output_grad,
):
    dp, n = mesh_shape
    axes = ("dp", "rows")
    r, d = lax.axis_index("rows"), lax.axis_index("dp")
    odd = d % 2

    def send(x, target):
        perm = []
        for a in range(dp):
            for b in range(n):
                a2, b2 = target(a, b)
                perm.append((a * n + b, a2 * n + b2))
        return lax.ppermute(x, axes, perm)

    def to_row(x, j):
        return send(x, lambda a, b: (a, b ^ j))

    tok = tokens.shape[0]
    weight = query_key_value_weight
    k_rows = weight.shape[0]
    cols = weight.shape[1] // n
    head_cols = heads_output_grad.shape[1] // n
    half = k_rows // 2

    def weight_slice(row, rows, owner):
        return lax.dynamic_slice(weight, (row, owner * cols), (rows, cols))

    def cot_slice(owner):
        return lax.dynamic_slice(heads_output_grad, (0, owner * head_cols), (tok, head_cols))

    pieces, bases = [], []
    fetched = []
    for j in range(2, n, 2):
        for c in range(2):
            piece = weight_slice(c * half, half, r ^ (j + odd))
            piece = send(piece, lambda a, b, j=j: (a, b ^ (j + a % 2)))
            fetched.append((piece, j, c))
    for piece, j, c in fetched:
        pieces.append(piece)
        bases.append((r ^ (j + odd)) * k_rows + c * half)
        pieces.append(send(piece, lambda a, b: (a ^ 1, b)))
        bases.append((r ^ (j + 1 - odd)) * k_rows + c * half)
    pieces.append(weight_slice(0, k_rows, r))
    bases.append(r * k_rows)
    pieces.append(to_row(weight_slice(0, k_rows, r ^ 1), 1))
    bases.append((r ^ 1) * k_rows)

    ada_gain = 1.0 + jnp.dot(time_features(timestep), timestep_gain_map, precision=lax.Precision.HIGHEST)
    tokens_f = tokens.astype(F32)
    inv_rms = lax.rsqrt(jnp.mean(tokens_f * tokens_f, -1, keepdims=True) + EPS)
    normed = [(tokens_f * inv_rms * ada_gain).astype(BF)]
    normed.append(to_row(normed[0], 1))
    for j in range(2, n, 2):
        normed.append(to_row(normed[0], j))
        normed.append(to_row(normed[j], 1))
    cot = [cot_slice(r)] + [to_row(cot_slice(r ^ j), j) for j in range(1, n)]

    up_here = lax.dynamic_slice(adapter_up_weight, (0, r * cols), (adapter_up_weight.shape[0], cols))
    *parts, pack = attention_call(
        jnp.stack(bases).astype(jnp.int32), head_score_scale, normed, pieces, cot, adapter_down_weight, up_here
    )

    rank = adapter_up_weight.shape[0]
    grad = None
    for j in list(range(2, n, 2)) + [0]:
        summed = parts[j] + to_row(parts[j ^ 1], 1).astype(F32)
        if j:
            summed = to_row(summed.astype(BF), j).astype(F32)
        grad = summed if grad is None else grad + summed

    packs = [pack, to_row(pack, 1)]
    for j in range(2, n, 2):
        packs.append(to_row(pack, j))
        packs.append(to_row(packs[j], 1))
    low_grad_t = None
    for j in range(n):
        blocks = [packs[j][rank:, (q ^ j) * tok : (q ^ j) * tok + tok] for q in range(n)]
        term = jnp.concatenate(blocks, axis=1)
        low_grad_t = term if low_grad_t is None else low_grad_t + term
    low_grad_t = low_grad_t.astype(BF)
    down_t = None
    for j in range(n):
        term = jnp.dot(low_grad_t[:, j * tok : (j + 1) * tok], normed[j], preferred_element_type=F32)
        down_t = term if down_t is None else down_t + term
    up_grad = jnp.zeros(adapter_up_weight.shape, F32)
    for j in range(n):
        up_grad = lax.dynamic_update_slice(up_grad, packs[j][:rank, :cols], (0, (r ^ j) * cols))

    scaled = grad * ada_gain
    input_grad = inv_rms * (
        scaled - tokens_f * inv_rms * inv_rms * jnp.mean(scaled * tokens_f, -1, keepdims=True)
    )
    return (input_grad.astype(BF), down_t.T, up_grad)


def solution(mesh):
    in_specs = (
        P(("dp", "rows"), None),
        P("dp"),
        P(),
        P("rows", None),
        P(),
        P(),
        P("rows"),
        P(("dp", "rows"), None),
    )
    out_specs = (P(("dp", "rows"), None), P("dp", None), P("dp", None))
    shape = (mesh.shape["dp"], mesh.shape["rows"])
    return jax.shard_map(
        functools.partial(per_device, shape), mesh=mesh, in_specs=in_specs, out_specs=out_specs, check_vma=False
    )
```

```python
import functools
import math

import jax
import jax.numpy as jnp
from jax import lax
from jax.experimental import pallas as pl
from jax.experimental.pallas import tpu as pltpu
from jax.sharding import PartitionSpec as P

HEAD = 64
EMB = 256
EPS = 1e-06
LOG2E = 1.4426950408889634
BF = jnp.bfloat16
F32 = jnp.float32
VMEM = 32 * 1024 * 1024
SMALL = pl.CostEstimate(flops=1, bytes_accessed=1, transcendentals=0)


def time_features(timestep):
    half_emb = EMB // 2
    frequency = jnp.exp(-math.log(10000.0) * jnp.arange(half_emb, dtype=F32) / half_emb)
    phases = timestep.astype(F32)[0] * frequency
    return jnp.stack([jnp.cos(phases), jnp.sin(phases)])


def contract(a, b, a_dim, b_dim):
    return lax.dot_general(a, b, (((a_dim,), (b_dim,)), ((), ())), preferred_element_type=F32)


def norm_kernel(features, gain_map, tokens, normed, gain, inv_rms):
    half = features.shape[1]
    col = features[...].T
    total = jnp.sum(col[:, :1] * gain_map[:half, :], 0, keepdims=True)
    total = total + jnp.sum(col[:, 1:] * gain_map[half:, :], 0, keepdims=True)
    gain[...] = 1.0 + total
    x = tokens[...].astype(F32)
    inv = lax.rsqrt(jnp.mean(x * x, -1, keepdims=True) + EPS)
    inv_rms[...] = inv
    normed[...] = (x * inv * gain[...]).astype(BF)


def norm_call(features, gain_map, tokens):
    rows, width = tokens.shape
    vmem = pl.BlockSpec(memory_space=pltpu.VMEM)
    return pl.pallas_call(
        norm_kernel,
        out_shape=[
            jax.ShapeDtypeStruct((rows, width), BF),
            jax.ShapeDtypeStruct((1, width), F32),
            jax.ShapeDtypeStruct((rows, 1), F32),
        ],
        in_specs=[vmem] * 3,
        out_specs=[vmem] * 3,
        cost_estimate=SMALL,
        name="norm",
    )(features, gain_map, tokens)


def qkv_kernel(x_from, w_from, *refs):
    bases, refs = refs[0], refs[1:]
    down_t, up = refs[-6:-4]
    x_all, w_all, qkv_t, low_t = refs[-4:]
    at = 0
    for i, row, rows, col in x_from:
        x_all[pl.ds(at, rows), :] = refs[i][pl.ds(row, rows), pl.ds(col, x_all.shape[1])]
        at += rows
    for k, (i, row, rows, col, cols, to) in enumerate(w_from):
        base = pl.multiple_of(bases[k], 16)
        w_all[pl.ds(base, rows), pl.ds(to, cols)] = refs[i][pl.ds(row, rows), pl.ds(col, cols)]
    seq = x_all.shape[0]
    step = math.gcd(512, seq)
    for s in range(0, seq, step):
        x = x_all[pl.ds(s, step), :]
        low = contract(x, down_t[...], 1, 1).astype(BF)
        low_t[:, pl.ds(s, step)] = low.T
        qkv = jnp.dot(x, w_all[...], preferred_element_type=F32)
        qkv = qkv + 0.5 * jnp.dot(low, up[...], preferred_element_type=F32)
        qkv_t[:, pl.ds(s, step)] = qkv.astype(BF).T


def whole_vmem(count):
    return [pl.BlockSpec(memory_space=pltpu.VMEM)] * count


def qkv_call(bases, arrays, x_from, w_from, down_t, up, seq):
    rank, width = down_t.shape
    cols = up.shape[1]
    return pl.pallas_call(
        functools.partial(qkv_kernel, x_from, w_from),
        out_shape=[
            jax.ShapeDtypeStruct((seq, width), BF),
            jax.ShapeDtypeStruct((width, cols), BF),
            jax.ShapeDtypeStruct((cols, seq), BF),
            jax.ShapeDtypeStruct((rank, seq), BF),
        ],
        in_specs=[pl.BlockSpec(memory_space=pltpu.SMEM)] + whole_vmem(len(arrays) + 2),
        out_specs=whole_vmem(4),
        compiler_params=pltpu.CompilerParams(vmem_limit_bytes=VMEM),
        cost_estimate=SMALL,
        name="qkv",
    )(bases, *arrays, down_t, up)


def token_grads(low_grad_t, grad_t, w_all, down_t, at, rows):
    grad = grad_t[:, pl.ds(at, rows)].T
    part = contract(grad, w_all[...], 1, 1)
    return part + contract(low_grad_t[:, pl.ds(at, rows)].astype(BF), down_t[...], 0, 0)


def attention_kernel(heads, tok, c_from, first, outs, *refs):
    refs = list(refs)
    scale, half = refs.pop(0), refs.pop(0)
    cots = [refs.pop(0) for _ in range(1 + max(i for i, *_ in c_from))]
    qkv_t, low_t, w_all, down_t, up = (refs.pop(0) for _ in range(5))
    parts = [refs.pop(0) for _ in range(outs)]
    grad_t, pack, cot_t = refs

    seq = qkv_t.shape[1]
    cols = up.shape[1]
    step = math.gcd(512, seq)
    width = cot_t.shape[0]
    for j, (i, col, choose) in enumerate(c_from):
        if choose and width % 128 == 0:
            block = cots[i][:, pl.ds(pl.multiple_of(half[0] * width, 128), width)]
        elif choose:
            block = jnp.where(half[0] == 0, cots[i][:, pl.ds(0, width)], cots[i][:, pl.ds(width, width)])
        else:
            block = cots[i][:, pl.ds(col, width)]
        cot_t[:, pl.ds(j * tok, tok)] = block.T

    for h in range(heads):
        o = 3 * HEAD * h
        kf = qkv_t[pl.ds(o + HEAD, HEAD), :].astype(F32)
        k_inv = lax.rsqrt(jnp.sum(kf * kf, 0, keepdims=True) + EPS)
        k_unit = kf * k_inv
        k_low = k_unit.astype(BF)
        v = qkv_t[pl.ds(o + 2 * HEAD, HEAD), :]
        sc = scale[h]
        gk = gv = None
        for s in range(0, seq, step):
            qf = qkv_t[pl.ds(o, HEAD), pl.ds(s, step)].astype(F32)
            q_inv = lax.rsqrt(jnp.sum(qf * qf, 0, keepdims=True) + EPS)
            q_unit = qf * q_inv
            q_low = q_unit.astype(BF)
            g = cot_t[pl.ds(HEAD * h, HEAD), pl.ds(s, step)]
            e = jnp.exp2(contract(k_low, q_low, 0, 0) * (sc * LOG2E))
            attention = e * (1.0 / jnp.sum(e, 0, keepdims=True))
            grad_probs = contract(v, g, 0, 0)
            delta = jnp.sum(attention * grad_probs, 0, keepdims=True)
            grad_scores = (attention * (grad_probs - delta)).astype(BF)
            gv_s = contract(g, attention.astype(BF), 1, 1)
            gk_s = sc * contract(q_low, grad_scores, 1, 1)
            gq = sc * jnp.dot(k_low, grad_scores, preferred_element_type=F32)
            gq = q_inv * (gq - q_unit * jnp.sum(q_unit * gq, 0, keepdims=True))
            grad_t[pl.ds(o, HEAD), pl.ds(s, step)] = gq.astype(BF)
            gv = gv_s if gv is None else gv + gv_s
            gk = gk_s if gk is None else gk + gk_s
        gk = k_inv * (gk - k_unit * jnp.sum(k_unit * gk, 0, keepdims=True))
        grad_t[pl.ds(o + HEAD, HEAD), :] = gk.astype(BF)
        grad_t[pl.ds(o + 2 * HEAD, HEAD), :] = gv.astype(BF)

    rank = up.shape[0]
    pack[pl.ds(0, rank), pl.ds(0, cols)] = 0.5 * contract(low_t[...], grad_t[...], 1, 1)
    low_grad_t = pack.at[pl.ds(rank, rank), pl.ds(0, seq)]
    low_grad_t[...] = 0.5 * jnp.dot(up[...], grad_t[...], preferred_element_type=F32)
    for p in range(outs):
        part = token_grads(low_grad_t, grad_t, w_all, down_t, (first + p) * tok, tok)
        parts[p][...] = part.astype(parts[p].dtype)


def attention_call(scale, half, cots, c_from, qkv_t, low_t, w_all, down_t, up, tok, first, dtypes):
    cols, seq = qkv_t.shape
    rank, width = down_t.shape
    smem = pl.BlockSpec(memory_space=pltpu.SMEM)
    outs = len(dtypes)
    return pl.pallas_call(
        functools.partial(attention_kernel, cols // (3 * HEAD), tok, c_from, first, outs),
        out_shape=[jax.ShapeDtypeStruct((tok, width), t) for t in dtypes]
        + [jax.ShapeDtypeStruct((cols, seq), BF), jax.ShapeDtypeStruct((2 * rank, max(cols, seq)), F32)],
        in_specs=[smem, smem] + whole_vmem(len(cots) + 5),
        out_specs=whole_vmem(outs + 2),
        scratch_shapes=[pltpu.VMEM((cols // 3, seq), BF)],
        compiler_params=pltpu.CompilerParams(vmem_limit_bytes=VMEM),
        cost_estimate=SMALL,
        name="attention_grads",
    )(scale, half, *cots, qkv_t, low_t, w_all, down_t, up)


def own_kernel(grad_t, pack, w_all, down_t, *parts):
    tok = parts[0].shape[0]
    rank = down_t.shape[0]
    low_grad_t = pack.at[pl.ds(rank, rank), :]
    for p, out in enumerate(parts):
        out[...] = token_grads(low_grad_t, grad_t, w_all, down_t, p * tok, tok).astype(out.dtype)


def own_call(grad_t, pack, w_all, down_t, tok, dtypes):
    return pl.pallas_call(
        own_kernel,
        out_shape=[jax.ShapeDtypeStruct((tok, down_t.shape[1]), t) for t in dtypes],
        in_specs=whole_vmem(4),
        out_specs=whole_vmem(len(dtypes)),
        compiler_params=pltpu.CompilerParams(vmem_limit_bytes=VMEM),
        cost_estimate=SMALL,
        name="own_grads",
    )(grad_t, pack, w_all, down_t)


def prepare_kernel(layout, features, gain_map, tokens, weight, cot, normed, to_core, own_w, own_cot, chip_cot, gain, inv_rms, sems):
    r = lax.axis_index("rows")
    tok, cols, head_cols, stack, width = layout
    core = r ^ 1
    copies = []
    for i in range(stack):
        src = weight.at[pl.ds(i * tok, tok), pl.ds(pl.multiple_of(core * cols, 128), cols)]
        copies.append((src, to_core.at[:, pl.ds(i * cols, cols)]))
    at = stack * cols + width
    copies.append(
        (cot.at[:, pl.ds(pl.multiple_of(core * head_cols, 128), head_cols)], to_core.at[:, pl.ds(at, head_cols)])
    )
    copies.append((weight.at[:, pl.ds(pl.multiple_of(r * cols, 128), cols)], own_w))
    copies.append((cot.at[:, pl.ds(pl.multiple_of(r * head_cols, 128), head_cols)], own_cot))
    chip = lax.div(r ^ 2, 2) * 2
    copies.append((cot.at[:, pl.ds(pl.multiple_of(chip * head_cols, 128), 2 * head_cols)], chip_cot))
    copies = [pltpu.make_async_copy(a, b, sems.at[i]) for i, (a, b) in enumerate(copies)]
    for c in copies:
        c.start()
    half = features.shape[1]
    col = features[...].T
    total = jnp.sum(col[:, :1] * gain_map[:half, :], 0, keepdims=True)
    total = total + jnp.sum(col[:, 1:] * gain_map[half:, :], 0, keepdims=True)
    gain[...] = 1.0 + total
    x = tokens[...].astype(F32)
    inv = lax.rsqrt(jnp.mean(x * x, -1, keepdims=True) + EPS)
    inv_rms[...] = inv
    y = (x * inv * gain[...]).astype(BF)
    normed[...] = y
    to_core[:, pl.ds(stack * cols, width)] = y
    for c in copies:
        c.wait()


def prepare_call(features, gain_map, tokens, weight, cot, n):
    tok, width = tokens.shape
    cols, head_cols = weight.shape[1] // n, cot.shape[1] // n
    stack = weight.shape[0] // tok
    any_ = pl.BlockSpec(memory_space=pl.ANY)
    shapes = [
        ((tok, width), BF),
        ((tok, stack * cols + width + head_cols), BF),
        ((weight.shape[0], cols), BF),
        ((tok, head_cols), BF),
        ((tok, 2 * head_cols), BF),
        ((1, width), F32),
        ((tok, 1), F32),
    ]
    return pl.pallas_call(
        functools.partial(prepare_kernel, (tok, cols, head_cols, stack, width)),
        out_shape=[jax.ShapeDtypeStruct(*shape) for shape in shapes],
        in_specs=whole_vmem(3) + [any_, any_],
        out_specs=whole_vmem(7),
        scratch_shapes=[pltpu.SemaphoreType.DMA((stack + 4,))],
        cost_estimate=SMALL,
        name="prepare",
    )(features, gain_map, tokens, weight, cot)


def per_device(
    mesh_shape,
    tokens,
    timestep,
    timestep_gain_map,
    query_key_value_weight,
    adapter_down_weight,
    adapter_up_weight,
    head_score_scale,
    heads_output_grad,
):
    dp, n = mesh_shape
    axes = ("dp", "rows")
    r, d = lax.axis_index("rows"), lax.axis_index("dp")

    def send(x, target):
        perm = []
        for a in range(dp):
            for b in range(n):
                a2, b2 = target(a, b)
                perm.append((a * n + b, a2 * n + b2))
        return lax.ppermute(x, axes, perm)

    def to_row(x, j):
        return send(x, lambda a, b: (a, b ^ j))

    tok, width = tokens.shape
    weight, cot_all = query_key_value_weight, heads_output_grad
    k_rows = weight.shape[0]
    cols = weight.shape[1] // n
    head_cols = cot_all.shape[1] // n
    chips = list(range(2, n, 2))

    cuts = 2 if cols % 256 == 0 else 1
    part_cols = cols // cuts
    odd = d % 2
    fetched = []
    for j in chips:
        for c in range(cuts):
            x = lax.dynamic_slice(weight, (0, (r ^ (j + odd)) * cols + c * part_cols), (k_rows, part_cols))
            fetched.append((send(x, lambda a, b, j=j: (a, b ^ (j + a % 2))), j, c))

    features = time_features(timestep)
    if cols % 128 == 0 and head_cols % 128 == 0 and k_rows % tok == 0 and n == 4:
        normed, to_core, own_w, own_cot, chip_cot, gain, inv_rms = prepare_call(
            features, timestep_gain_map, tokens, weight, cot_all, n
        )
        chip_cot = [chip_cot]
        core = to_row(to_core, 1)
        stack = k_rows // tok
        arrays = [own_w, core, normed]
        x_from = [(2, 0, tok, 0), (1, 0, tok, stack * cols)]
        w_from = [(0, 0, k_rows, 0, cols, 0)] + [(1, 0, tok, i * cols, cols, 0) for i in range(stack)]
        bases = [r * k_rows] + [(r ^ 1) * k_rows + i * tok for i in range(stack)]
        cots = [own_cot, core]
        c_from = [(0, 0, False), (1, stack * cols + width, False)]
    else:
        normed, gain, inv_rms = norm_call(features, timestep_gain_map, tokens)

        def columns(x, at, count):
            return lax.dynamic_slice(x, (0, at), (x.shape[0], count))

        chip_cot = [columns(cot_all, (r ^ j) // 2 * (2 * head_cols), 2 * head_cols) for j in chips]
        arrays = [columns(weight, r * cols, cols), to_row(columns(weight, (r ^ 1) * cols, cols), 1)]
        arrays += [normed, to_row(normed, 1)]
        x_from = [(2, 0, tok, 0), (3, 0, tok, 0)]
        w_from = [(i, 0, k_rows, 0, cols, 0) for i in range(2)]
        bases = [(r ^ i) * k_rows for i in range(2)]
        cots = [columns(cot_all, r * head_cols, head_cols), to_row(columns(cot_all, (r ^ 1) * head_cols, head_cols), 1)]
        c_from = [(0, 0, False), (1, 0, False)]

    for x, j, c in fetched:
        for other in range(2):
            w_from.append((len(arrays), 0, k_rows, 0, part_cols, c * part_cols))
            bases.append((r ^ (j + (odd ^ other))) * k_rows)
            arrays.append(send(x, lambda a, b: (a ^ 1, b)) if other else x)

    chip_normed = [to_row(normed, j) for j in chips]
    chip_cot = [to_row(x, j) for j, x in zip(chips, chip_cot)]
    rows = tok // 2 if tok % 32 == 0 else tok
    for x in chip_normed:
        x_from.append((len(arrays), 0, tok, 0))
        arrays.append(x)
        for at in range(0, tok, rows):
            x_from.append((len(arrays), 0, rows, 0))
            arrays.append(to_row(x[at : at + rows], 1))
    for x in chip_cot:
        other = lax.dynamic_slice(x, (0, (r ^ 1) % 2 * head_cols), (tok, head_cols))
        c_from += [(len(cots), 0, True), (len(cots) + 1, 0, False)]
        cots += [x, to_row(other, 1)]

    rank = adapter_up_weight.shape[0]
    down_t = adapter_down_weight.T
    up = lax.dynamic_slice(adapter_up_weight, (0, r * cols), (rank, cols))
    x_all, w_all, qkv_t, low_t = qkv_call(
        jnp.stack(bases).astype(jnp.int32), arrays, tuple(x_from), tuple(w_from), down_t, up, n * tok
    )
    half = (r % 2).astype(jnp.int32)[None]
    *others, grad_t, pack = attention_call(
        head_score_scale, half, cots, tuple(c_from), qkv_t, low_t, w_all, down_t, up, tok, 2, (F32, BF) * len(chips)
    )

    sums = []
    for i, j in enumerate(chips):
        total = others[2 * i] + to_row(others[2 * i + 1], 1).astype(F32)
        sums.append(to_row(total.astype(BF), j))
    mine, core_part = own_call(grad_t, pack, w_all, down_t, tok, (F32, BF))
    grad = mine + to_row(core_part, 1).astype(F32)
    for x in sums:
        grad = grad + x.astype(F32)

    packs = [pack, to_row(pack, 1)]
    for j in chips:
        packs.append(to_row(pack, j))
        packs.append(to_row(packs[j], 1))
    low_grad_t = None
    for j in range(n):
        blocks = [packs[j][rank:, (q ^ j) * tok : (q ^ j) * tok + tok] for q in range(n)]
        term = jnp.concatenate(blocks, axis=1)
        low_grad_t = term if low_grad_t is None else low_grad_t + term
    down_grad_t = jnp.dot(low_grad_t.astype(BF), x_all, preferred_element_type=F32)
    up_grad = jnp.zeros(adapter_up_weight.shape, F32)
    for j in range(n):
        up_grad = lax.dynamic_update_slice(up_grad, packs[j][:rank, :cols], (0, (r ^ j) * cols))

    x = tokens.astype(F32)
    scaled = grad * gain
    input_grad = inv_rms * (scaled - x * inv_rms * inv_rms * jnp.mean(scaled * x, -1, keepdims=True))
    return (input_grad.astype(BF), down_grad_t.T, up_grad)


def solution(mesh):
    in_specs = (
        P(("dp", "rows"), None),
        P("dp"),
        P(),
        P("rows", None),
        P(),
        P(),
        P("rows"),
        P(("dp", "rows"), None),
    )
    out_specs = (P(("dp", "rows"), None), P("dp", None), P("dp", None))
    shape = (mesh.shape["dp"], mesh.shape["rows"])
    return jax.shard_map(
        functools.partial(per_device, shape), mesh=mesh, in_specs=in_specs, out_specs=out_specs, check_vma=False
    )
```

```python
import functools
import math

import jax
import jax.numpy as jnp
from jax import lax
from jax.experimental import pallas as pl
from jax.experimental.pallas import tpu as pltpu
from jax.sharding import PartitionSpec as P

HEAD = 64
EMB = 256
EPS = 1e-06
LOG2E = 1.4426950408889634
BF = jnp.bfloat16
F32 = jnp.float32
VMEM = 16 * 1024 * 1024
SMALL = pl.CostEstimate(flops=1, bytes_accessed=1, transcendentals=0)


def time_features(timestep):
    half_emb = EMB // 2
    frequency = jnp.exp(-math.log(10000.0) * jnp.arange(half_emb, dtype=F32) / half_emb)
    phases = timestep.astype(F32)[0] * frequency
    return jnp.stack([jnp.cos(phases), jnp.sin(phases)])


def contract(a, b, a_dim, b_dim):
    return lax.dot_general(a, b, (((a_dim,), (b_dim,)), ((), ())), preferred_element_type=F32)


def columns(x, size):
    if x.shape[1] == size:
        return x[...]
    return x[:, pl.ds(pl.multiple_of(lax.axis_index("rows") * size, 128), size)]


def qkv_kernel(x_from, w_from, *refs):
    down_t, up_in = refs[-6:-4]
    r, odd = lax.axis_index("rows"), lax.rem(lax.axis_index("dp"), 2)
    up = columns(up_in, refs[-2].shape[0])
    x_all, w_all, qkv_t, low_t = refs[-4:]
    at = 0
    for i, rows in x_from:
        x_all[pl.ds(at, rows), :] = refs[i][...]
        at += rows
    for i, to, j, other in w_from:
        rows, cols = refs[i].shape
        holder = r ^ j if other is None else r ^ (j + (odd ^ other))
        base = pl.multiple_of(holder * rows, 16)
        w_all[pl.ds(base, rows), pl.ds(to, cols)] = refs[i][...]
    seq = x_all.shape[0]
    step = math.gcd(512, seq)
    for s in range(0, seq, step):
        x = x_all[pl.ds(s, step), :]
        low = contract(x, down_t[...], 1, 1).astype(BF)
        low_t[:, pl.ds(s, step)] = low.T
        qkv = jnp.dot(x, w_all[...], preferred_element_type=F32)
        qkv = qkv + 0.5 * jnp.dot(low, up, preferred_element_type=F32)
        qkv_t[:, pl.ds(s, step)] = qkv.astype(BF).T


def gate(xs, rows, *deps):
    wanted = [(i, at) for i, x in enumerate(xs) for at in range(0, x.shape[0], rows[i])]

    def kernel(*refs):
        for (i, at), out in zip(wanted, refs[len(xs) + len(deps) :]):
            out[...] = refs[i][pl.ds(at, rows[i]), :]

    return pl.pallas_call(
        kernel,
        out_shape=[in_vmem((rows[i], xs[i].shape[1]), xs[i].dtype) for i, _ in wanted],
        in_specs=whole_vmem(len(xs) + len(deps)),
        out_specs=whole_vmem(len(wanted)),
        compiler_params=pltpu.CompilerParams(vmem_limit_bytes=VMEM),
        cost_estimate=SMALL,
        name="gate",
    )(*vmem(xs), *vmem(deps))


def in_vmem(shape, dtype):
    return pltpu.VMEM(shape, dtype)


def vmem(xs):
    return [pltpu.with_memory_space_constraint(x, pltpu.VMEM) for x in xs]


def hbm(xs):
    return [pltpu.with_memory_space_constraint(x, pltpu.HBM) for x in xs]


def whole_vmem(count):
    return [pl.BlockSpec(memory_space=pltpu.VMEM)] * count


def qkv_call(arrays, x_from, w_from, down_t, up, seq, cols):
    rank, width = down_t.shape
    return pl.pallas_call(
        functools.partial(qkv_kernel, x_from, w_from),
        out_shape=[
            in_vmem((seq, width), BF),
            in_vmem((width, cols), BF),
            in_vmem((cols, seq), BF),
            in_vmem((rank, seq), BF),
        ],
        in_specs=whole_vmem(len(arrays) + 2),
        out_specs=whole_vmem(4),
        compiler_params=pltpu.CompilerParams(vmem_limit_bytes=VMEM),
        cost_estimate=SMALL,
        name="qkv",
    )(*vmem(arrays), down_t, up)


def token_grads(low_grad_t, grad_t, w_all, down_t, at, rows):
    grad = grad_t[:, pl.ds(at, rows)].T
    part = contract(grad, w_all[...], 1, 1)
    return part + contract(low_grad_t[:, pl.ds(at, rows)].astype(BF), down_t[...], 0, 0)


def attention_kernel(heads, tok, c_from, first, outs, *refs):
    refs = list(refs)
    scale = refs.pop(0)
    cots = [refs.pop(0) for _ in c_from]
    qkv_t, low_t, w_all, down_t, up_in = (refs.pop(0) for _ in range(5))
    parts = [refs.pop(0) for _ in range(outs)]
    grad_t, pack, cot_t = refs

    cols, seq = qkv_t.shape
    up = columns(up_in, cols)
    step = math.gcd(512, seq)
    width = cot_t.shape[0]
    start = lax.rem(lax.axis_index("rows"), 2) * width
    for j, (i, choose) in enumerate(c_from):
        if not choose:
            block = cots[i][...]
        elif width % 128 == 0:
            block = cots[i][:, pl.ds(pl.multiple_of(start, 128), width)]
        else:
            block = jnp.where(start == 0, cots[i][:, pl.ds(0, width)], cots[i][:, pl.ds(width, width)])
        cot_t[:, pl.ds(j * tok, tok)] = block.T

    for h in range(heads):
        o = 3 * HEAD * h
        kf = qkv_t[pl.ds(o + HEAD, HEAD), :].astype(F32)
        k_inv = lax.rsqrt(jnp.sum(kf * kf, 0, keepdims=True) + EPS)
        k_unit = kf * k_inv
        k_low = k_unit.astype(BF)
        v = qkv_t[pl.ds(o + 2 * HEAD, HEAD), :]
        sc = scale[h]
        gk = gv = None
        for s in range(0, seq, step):
            qf = qkv_t[pl.ds(o, HEAD), pl.ds(s, step)].astype(F32)
            q_inv = lax.rsqrt(jnp.sum(qf * qf, 0, keepdims=True) + EPS)
            q_unit = qf * q_inv
            q_low = q_unit.astype(BF)
            g = cot_t[pl.ds(HEAD * h, HEAD), pl.ds(s, step)]
            e = jnp.exp2(contract(k_low, q_low, 0, 0) * (sc * LOG2E))
            attention = e * (1.0 / jnp.sum(e, 0, keepdims=True))
            grad_probs = contract(v, g, 0, 0)
            delta = jnp.sum(attention * grad_probs, 0, keepdims=True)
            grad_scores = (attention * (grad_probs - delta)).astype(BF)
            gv_s = contract(g, attention.astype(BF), 1, 1)
            gk_s = sc * contract(q_low, grad_scores, 1, 1)
            gq = sc * jnp.dot(k_low, grad_scores, preferred_element_type=F32)
            gq = q_inv * (gq - q_unit * jnp.sum(q_unit * gq, 0, keepdims=True))
            grad_t[pl.ds(o, HEAD), pl.ds(s, step)] = gq.astype(BF)
            gv = gv_s if gv is None else gv + gv_s
            gk = gk_s if gk is None else gk + gk_s
        gk = k_inv * (gk - k_unit * jnp.sum(k_unit * gk, 0, keepdims=True))
        grad_t[pl.ds(o + HEAD, HEAD), :] = gk.astype(BF)
        grad_t[pl.ds(o + 2 * HEAD, HEAD), :] = gv.astype(BF)

    rank = up.shape[0]
    pack[pl.ds(0, rank), pl.ds(0, cols)] = 0.5 * contract(low_t[...], grad_t[...], 1, 1)
    low_grad_t = pack.at[pl.ds(rank, rank), pl.ds(0, seq)]
    low_grad_t[...] = 0.5 * jnp.dot(up, grad_t[...], preferred_element_type=F32)
    for p in range(outs):
        part = token_grads(low_grad_t, grad_t, w_all, down_t, (first + p) * tok, tok)
        parts[p][...] = part.astype(parts[p].dtype)


def attention_call(scale, cots, c_from, qkv_t, low_t, w_all, down_t, up, tok, first, dtypes):
    cols, seq = qkv_t.shape
    rank, width = down_t.shape
    smem = pl.BlockSpec(memory_space=pltpu.SMEM)
    outs = len(dtypes)
    return pl.pallas_call(
        functools.partial(attention_kernel, cols // (3 * HEAD), tok, c_from, first, outs),
        out_shape=[in_vmem((tok, width), t) for t in dtypes]
        + [in_vmem((cols, seq), BF), in_vmem((2 * rank, max(cols, seq)), F32)],
        in_specs=[smem] + whole_vmem(len(cots) + 5),
        out_specs=whole_vmem(outs + 2),
        scratch_shapes=[pltpu.VMEM((cols // 3, seq), BF)],
        compiler_params=pltpu.CompilerParams(vmem_limit_bytes=VMEM),
        cost_estimate=SMALL,
        name="attention_grads",
    )(scale, *vmem(cots), qkv_t, low_t, w_all, down_t, up)


def other_half(x):
    rows, cols = x.shape
    half = cols // 2
    if half % 128:
        return lax.dynamic_slice(x, (0, (lax.axis_index("rows") ^ 1) % 2 * half), (rows, half))

    def kernel(x, out):
        core = lax.rem(lax.axis_index("rows") ^ 1, 2)
        out[...] = x[:, pl.ds(pl.multiple_of(core * half, 128), half)]

    return pl.pallas_call(
        kernel,
        out_shape=in_vmem((rows, half), x.dtype),
        in_specs=whole_vmem(1),
        out_specs=whole_vmem(1)[0],
        compiler_params=pltpu.CompilerParams(vmem_limit_bytes=VMEM),
        cost_estimate=SMALL,
        name="other_half",
    )(*vmem([x]))


def add(a, b):
    def kernel(a, b, out):
        out[...] = (a[...] + b[...].astype(F32)).astype(BF)

    return pl.pallas_call(
        kernel,
        out_shape=in_vmem(a.shape, BF),
        in_specs=whole_vmem(2),
        out_specs=whole_vmem(1)[0],
        compiler_params=pltpu.CompilerParams(vmem_limit_bytes=VMEM),
        cost_estimate=SMALL,
        name="add",
    )(*vmem([a, b]))


def own_kernel(deps, grad_t, pack, w_all, down_t, *refs):
    mine, rest = refs[deps], refs[deps + 1 :]
    tok = mine.shape[0]
    rank = down_t.shape[0]
    low_grad_t = pack.at[pl.ds(rank, rank), :]
    mine[...] = token_grads(low_grad_t, grad_t, w_all, down_t, 0, tok)
    part = token_grads(low_grad_t, grad_t, w_all, down_t, tok, tok).astype(BF)
    at = 0
    for out in rest:
        out[...] = part[at : at + out.shape[0]]
        at += out.shape[0]


def own_call(grad_t, pack, w_all, down_t, tok, blocks, deps):
    width = down_t.shape[1]
    return pl.pallas_call(
        functools.partial(own_kernel, len(deps)),
        out_shape=[in_vmem((tok, width), F32)] + [in_vmem((rows, width), BF) for rows in blocks],
        in_specs=whole_vmem(4 + len(deps)),
        out_specs=whole_vmem(1 + len(blocks)),
        compiler_params=pltpu.CompilerParams(vmem_limit_bytes=VMEM),
        cost_estimate=SMALL,
        name="own_grads",
    )(grad_t, pack, w_all, down_t, *vmem(deps))


def adapter_kernel(tok, *refs):
    packs, (x_all, down_grad_t, up_grad) = refs[:-3], refs[-3:]
    rank = down_grad_t.shape[0]
    r = lax.axis_index("rows")
    total = None
    for j, pack in enumerate(packs):
        blocks = [pack[pl.ds(rank, rank), pl.ds((q ^ j) * tok, tok)] for q in range(len(packs))]
        term = jnp.concatenate(blocks, axis=1)
        total = term if total is None else total + term
    down_grad_t[...] = jnp.dot(total.astype(BF), x_all[...], preferred_element_type=F32)
    cols = up_grad.shape[1] // len(packs)
    for j, pack in enumerate(packs):
        if cols % 128 == 0:
            up_grad[:, pl.ds(pl.multiple_of((r ^ j) * cols, 128), cols)] = pack[pl.ds(0, rank), pl.ds(0, cols)]


def adapter_call(packs, x_all, rank, all_cols, tok):
    down_grad_t, up_grad = pl.pallas_call(
        functools.partial(adapter_kernel, tok),
        out_shape=[
            jax.ShapeDtypeStruct((rank, x_all.shape[1]), F32),
            jax.ShapeDtypeStruct((rank, all_cols), F32),
        ],
        in_specs=whole_vmem(len(packs) + 1),
        out_specs=whole_vmem(2),
        compiler_params=pltpu.CompilerParams(vmem_limit_bytes=VMEM),
        cost_estimate=SMALL,
        name="adapter_grads",
    )(*vmem(packs), x_all)
    cols = all_cols // len(packs)
    if cols % 128:
        for j, pack in enumerate(packs):
            up_grad = lax.dynamic_update_slice(up_grad, pack[:rank, :cols], (0, (lax.axis_index("rows") ^ j) * cols))
    return down_grad_t, up_grad


def final_kernel(tokens, gain, inv_rms, mine, *refs):
    refs, out = refs[:-1], refs[-1]
    grad = mine[...]
    part = []
    for x in refs:
        part.append(x[...].astype(F32))
        if sum(p.shape[0] for p in part) == tokens.shape[0]:
            grad = grad + jnp.concatenate(part, axis=0)
            part = []
    x = tokens[...].astype(F32)
    inv = inv_rms[...]
    scaled = grad * gain[...]
    mean = jnp.mean(scaled * x, -1, keepdims=True)
    out[...] = (inv * (scaled - x * (inv * inv * mean))).astype(BF)


def final_call(tokens, gain, inv_rms, mine, terms):
    return pl.pallas_call(
        final_kernel,
        out_shape=jax.ShapeDtypeStruct(tokens.shape, BF),
        in_specs=whole_vmem(4 + len(terms)),
        out_specs=whole_vmem(1)[0],
        compiler_params=pltpu.CompilerParams(vmem_limit_bytes=VMEM),
        cost_estimate=SMALL,
        name="input_grads",
    )(tokens, gain, inv_rms, mine, *vmem(terms))


def prepare_kernel(chips, head_cols, sizes, features, gain_map, tokens, core_tokens, cot, *refs):
    count, outs = len(sizes), len(sizes) + len(chips)
    normed, core_normed, gain, inv_rms = refs[count : count + 4]
    cut = refs[count + 4 : count + 4 + outs]
    map_in, tokens_in, core_in, sems = refs[count + 4 + outs :]
    r = lax.axis_index("rows")
    copies = [(tokens, tokens_in), (core_tokens, core_in), (gain_map, map_in)]
    for x, size, out in zip(refs, sizes, cut):
        copies.append((x.at[:, pl.ds(pl.multiple_of(r * size, 128), size)] if size else x, out))
    for j, out in zip(chips, cut[count:]):
        chip = lax.div(r ^ j, 2) * (2 * head_cols)
        copies.append((cot.at[:, pl.ds(pl.multiple_of(chip, 128), 2 * head_cols)], out))
    copies = [pltpu.make_async_copy(a, b, sems.at[i]) for i, (a, b) in enumerate(copies)]
    for c in copies:
        c.start()
    half = features.shape[1]
    col = features[...].T
    for c in copies[:3]:
        c.wait()
    total = jnp.sum(col[:, :1] * map_in[:half, :], 0, keepdims=True)
    total = total + jnp.sum(col[:, 1:] * map_in[half:, :], 0, keepdims=True)
    gain[...] = 1.0 + total
    for x, out in ((tokens_in, normed), (core_in, core_normed)):
        x = x[...].astype(F32)
        inv = lax.rsqrt(jnp.mean(x * x, -1, keepdims=True) + EPS)
        if out is normed:
            inv_rms[...] = inv
        out[...] = (x * inv * gain[...]).astype(BF)
    for c in copies[3:]:
        c.wait()


def prepare_call(features, gain_map, tokens, core_tokens, cot, chips, head_cols, arrays):
    tok, width = tokens.shape
    shapes = [((tok, width), BF), ((tok, width), BF), ((1, width), F32), ((tok, 1), F32)]
    shapes += [((x.shape[0], size or x.shape[1]), BF) for x, size in arrays]
    shapes += [((tok, 2 * head_cols), BF)] * len(chips)
    copies = 3 + len(arrays) + len(chips)
    return pl.pallas_call(
        functools.partial(prepare_kernel, chips, head_cols, [size for _, size in arrays]),
        out_shape=[in_vmem(*shape) for shape in shapes],
        in_specs=whole_vmem(1) + [pl.BlockSpec(memory_space=pl.ANY)] * (4 + len(arrays)),
        out_specs=whole_vmem(len(shapes)),
        scratch_shapes=[
            pltpu.VMEM(gain_map.shape, F32),
            pltpu.VMEM((tok, width), BF),
            pltpu.VMEM((tok, width), BF),
            pltpu.SemaphoreType.DMA((copies,)),
        ],
        compiler_params=pltpu.CompilerParams(vmem_limit_bytes=VMEM),
        cost_estimate=SMALL,
        name="prepare",
    )(features, gain_map, tokens, core_tokens, cot, *[x for x, _ in arrays])


def per_device(
    mesh_shape,
    tokens,
    timestep,
    timestep_gain_map,
    query_key_value_weight,
    adapter_down_weight,
    adapter_up_weight,
    head_score_scale,
    heads_output_grad,
):
    dp, n = mesh_shape
    axes = ("dp", "rows")
    r, d = lax.axis_index("rows"), lax.axis_index("dp")

    def send(x, target):
        perm = []
        for a in range(dp):
            for b in range(n):
                a2, b2 = target(a, b)
                perm.append((a * n + b, a2 * n + b2))
        return lax.ppermute(x, axes, perm)

    def to_row(x, j):
        return send(x, lambda a, b: (a, b ^ j))

    tok, width = tokens.shape
    weight, cot_all = query_key_value_weight, heads_output_grad
    k_rows = weight.shape[0]
    cols = weight.shape[1] // n
    head_cols = cot_all.shape[1] // n
    chips = list(range(2, n, 2))

    cuts = 2 if cols % 256 == 0 else 1
    part_cols = cols // cuts
    odd = d % 2
    fetched = []
    for j in chips:
        for c in range(cuts):
            x = lax.dynamic_slice(weight, (0, (r ^ (j + odd)) * cols + c * part_cols), (k_rows, part_cols))
            fetched.append((send(x, lambda a, b, j=j: (a, b ^ (j + a % 2))), j, c))

    core_weight, core_tokens, core_cot = (to_row(x, 1) for x in (weight, tokens, cot_all))

    def mine(x, size):
        return (x, size) if size % 128 == 0 else (lax.dynamic_slice(x, (0, r * size), (x.shape[0], size)), 0)

    own_map, own_tokens, own_cot = hbm([timestep_gain_map, tokens, cot_all])
    normed, core_normed, gain, inv_rms, own_w, core_w, own_cot, core_cot, *chip_cot = prepare_call(
        time_features(timestep), own_map, own_tokens, core_tokens, own_cot, chips, head_cols,
        [mine(weight, cols), mine(core_weight, cols), mine(cot_all, head_cols), mine(core_cot, head_cols)],
    )
    arrays = [own_w, core_w, normed, core_normed]
    w_from, x_from = [(0, 0, 0, None), (1, 0, 1, None)], [(2, tok), (3, tok)]
    rows = tok // 2 if tok % 32 == 0 else tok
    count = tok // rows
    first = [i for i, (_, _, c) in enumerate(fetched) if c == 0]
    later = gate(
        [normed] + chip_cot + [fetched[i][0] for i in first], [rows] + [tok] * len(chips) + [k_rows] * len(first)
    )
    later_normed, chip_cot = later[:count], later[count : count + len(chips)]
    for i, x in zip(first, later[count + len(chips) :]):
        fetched[i] = (x, *fetched[i][1:])
    sharers = []
    for x, j, c in fetched:
        for other in range(2):
            w_from.append((len(arrays), c * part_cols, j, other))
            arrays.append(send(x, lambda a, b: (a ^ 1, b)) if other else x)
            if other and c == 0:
                sharers.append(arrays[-1])

    halves = [to_row(x, j) for j in chips for x in later_normed]
    later = list(gate(halves, [rows] * len(halves), *sharers))
    for i in range(0, len(halves), count):
        for x in halves[i : i + count] + [to_row(x, 1) for x in later[i : i + count]]:
            x_from.append((len(arrays), rows))
            arrays.append(x)

    cots, c_from = [own_cot, core_cot], [(0, False), (1, False)]
    for j, x in zip(chips, chip_cot):
        x = to_row(x, j)
        c_from += [(len(cots), True), (len(cots) + 1, False)]
        cots += [x, to_row(other_half(x), 1)]

    rank = adapter_up_weight.shape[0]
    down_t = adapter_down_weight.T
    up = adapter_up_weight
    if cols % 128:
        up = lax.dynamic_slice(up, (0, r * cols), (rank, cols))
    x_all, w_all, qkv_t, low_t = qkv_call(
        arrays, tuple(x_from), tuple(w_from), down_t, up, n * tok, cols
    )
    *others, grad_t, pack = attention_call(
        head_score_scale, cots, tuple(c_from), qkv_t, low_t, w_all, down_t, up, tok, 2, (F32, BF) * len(chips)
    )

    totals = [add(others[2 * i], to_row(others[2 * i + 1], 1)) for i in range(len(chips))]
    sums = [to_row(x, j) for x, j in zip(totals, chips)]
    packs = {0: pack, 1: to_row(pack, 1)}
    for j in chips:
        packs[j] = to_row(pack, j)
    blocks = (tok * 3 // 4, tok // 4) if tok % 64 == 0 else (tok,)
    mine, *core_part = own_call(grad_t, pack, w_all, down_t, tok, blocks, totals + [packs[j] for j in chips])
    core_part = [to_row(x, 1) for x in core_part]

    for j in chips:
        packs[j ^ 1] = to_row(packs[j], 1)
    down_grad_t, up_grad = adapter_call([packs[j] for j in range(n)], x_all, rank, n * cols, tok)

    input_grad = final_call(tokens, gain, inv_rms, mine, core_part + sums)
    return (input_grad, down_grad_t.T, up_grad)


def solution(mesh):
    in_specs = (
        P(("dp", "rows"), None),
        P("dp"),
        P(),
        P("rows", None),
        P(),
        P(),
        P("rows"),
        P(("dp", "rows"), None),
    )
    out_specs = (P(("dp", "rows"), None), P("dp", None), P("dp", None))
    shape = (mesh.shape["dp"], mesh.shape["rows"])
    return jax.shard_map(
        functools.partial(per_device, shape), mesh=mesh, in_specs=in_specs, out_specs=out_specs, check_vma=False
    )
```

```python
import functools
import math

import jax
import jax.numpy as jnp
from jax import lax
from jax.experimental import pallas as pl
from jax.experimental.pallas import tpu as pltpu
from jax.sharding import PartitionSpec as P

HEAD = 64
EMB = 256
EPS = 1e-06
LOG2E = 1.4426950408889634
BF = jnp.bfloat16
F32 = jnp.float32
VMEM = 16 * 1024 * 1024
SMALL = pl.CostEstimate(flops=1, bytes_accessed=1, transcendentals=0)


def time_features(timestep):
    half_emb = EMB // 2
    frequency = jnp.exp(-math.log(10000.0) * jnp.arange(half_emb, dtype=F32) / half_emb)
    phases = timestep.astype(F32)[0] * frequency
    return jnp.stack([jnp.cos(phases), jnp.sin(phases)])


def contract(a, b, a_dim, b_dim):
    return lax.dot_general(a, b, (((a_dim,), (b_dim,)), ((), ())), preferred_element_type=F32)


def columns(x, size):
    if x.shape[1] == size:
        return x[...]
    return x[:, pl.ds(pl.multiple_of(lax.axis_index("rows") * size, 128), size)]


def qkv_kernel(x_from, w_from, *refs):
    down_t, up_in = refs[-6:-4]
    r, odd = lax.axis_index("rows"), lax.rem(lax.axis_index("dp"), 2)
    up = columns(up_in, refs[-2].shape[0])
    x_all, w_all, qkv_t, low_t = refs[-4:]
    at = 0
    for i, rows in x_from:
        x_all[pl.ds(at, rows), :] = refs[i][...]
        at += rows
    for i, to, j, other in w_from:
        rows, cols = refs[i].shape
        holder = r ^ j if other is None else r ^ (j + (odd ^ other))
        base = pl.multiple_of(holder * rows, 16)
        w_all[pl.ds(base, rows), pl.ds(to, cols)] = refs[i][...]
    seq = x_all.shape[0]
    step = math.gcd(512, seq)
    for s in range(0, seq, step):
        x = x_all[pl.ds(s, step), :]
        low = contract(x, down_t[...], 1, 1).astype(BF)
        low_t[:, pl.ds(s, step)] = low.T
        qkv = jnp.dot(x, w_all[...], preferred_element_type=F32)
        qkv = qkv + 0.5 * jnp.dot(low, up, preferred_element_type=F32)
        qkv_t[:, pl.ds(s, step)] = qkv.astype(BF).T


def gate(xs, rows, *deps):
    wanted = [(i, at) for i, x in enumerate(xs) for at in range(0, x.shape[0], rows[i])]

    def kernel(*refs):
        for (i, at), out in zip(wanted, refs[len(xs) + len(deps) :]):
            out[...] = refs[i][pl.ds(at, rows[i]), :]

    return pl.pallas_call(
        kernel,
        out_shape=[in_vmem((rows[i], xs[i].shape[1]), xs[i].dtype) for i, _ in wanted],
        in_specs=whole_vmem(len(xs) + len(deps)),
        out_specs=whole_vmem(len(wanted)),
        compiler_params=pltpu.CompilerParams(vmem_limit_bytes=VMEM),
        cost_estimate=SMALL,
        name="gate",
    )(*vmem(xs), *vmem(deps))


def in_vmem(shape, dtype):
    return pltpu.VMEM(shape, dtype)


def vmem(xs):
    return [pltpu.with_memory_space_constraint(x, pltpu.VMEM) for x in xs]


def hbm(xs):
    return [pltpu.with_memory_space_constraint(x, pltpu.HBM) for x in xs]


def whole_vmem(count):
    return [pl.BlockSpec(memory_space=pltpu.VMEM)] * count


def qkv_call(arrays, x_from, w_from, down_t, up, seq, cols):
    rank, width = down_t.shape
    return pl.pallas_call(
        functools.partial(qkv_kernel, x_from, w_from),
        out_shape=[
            in_vmem((seq, width), BF),
            in_vmem((width, cols), BF),
            in_vmem((cols, seq), BF),
            in_vmem((rank, seq), BF),
        ],
        in_specs=whole_vmem(len(arrays) + 2),
        out_specs=whole_vmem(4),
        compiler_params=pltpu.CompilerParams(vmem_limit_bytes=VMEM),
        cost_estimate=SMALL,
        name="qkv",
    )(*vmem(arrays), down_t, up)


def token_grads(low_grad_t, grad_t, w_all, down_t, at, rows):
    grad = grad_t[:, pl.ds(at, rows)].T
    part = contract(grad, w_all[...], 1, 1)
    return part + contract(low_grad_t[:, pl.ds(at, rows)], down_t[...], 0, 0)


def attention_kernel(heads, tok, c_from, first, outs, *refs):
    refs = list(refs)
    scale = refs.pop(0)
    cots = [refs.pop(0) for _ in c_from]
    qkv_t, low_t, w_all, down_t, up_in = (refs.pop(0) for _ in range(5))
    parts = [refs.pop(0) for _ in range(outs)]
    grad_t, pack, cot_t = refs

    cols, seq = qkv_t.shape
    up = columns(up_in, cols)
    step = math.gcd(512, seq)
    width = cot_t.shape[0]
    start = lax.rem(lax.axis_index("rows"), 2) * width
    for j, (i, choose) in enumerate(c_from):
        if not choose:
            block = cots[i][...]
        elif width % 128 == 0:
            block = cots[i][:, pl.ds(pl.multiple_of(start, 128), width)]
        else:
            block = jnp.where(start == 0, cots[i][:, pl.ds(0, width)], cots[i][:, pl.ds(width, width)])
        cot_t[:, pl.ds(j * tok, tok)] = block.T

    for h in range(heads):
        o = 3 * HEAD * h
        kf = qkv_t[pl.ds(o + HEAD, HEAD), :].astype(F32)
        k_inv = lax.rsqrt(jnp.sum(kf * kf, 0, keepdims=True) + EPS)
        k_unit = kf * k_inv
        k_low = k_unit.astype(BF)
        v = qkv_t[pl.ds(o + 2 * HEAD, HEAD), :]
        sc = scale[h]
        gk = gv = None
        for s in range(0, seq, step):
            qf = qkv_t[pl.ds(o, HEAD), pl.ds(s, step)].astype(F32)
            q_inv = lax.rsqrt(jnp.sum(qf * qf, 0, keepdims=True) + EPS)
            q_unit = qf * q_inv
            q_low = q_unit.astype(BF)
            g = cot_t[pl.ds(HEAD * h, HEAD), pl.ds(s, step)]
            e = jnp.exp2(contract(k_low, q_low, 0, 0) * (sc * LOG2E))
            share = 1.0 / jnp.sum(e, 0, keepdims=True)
            grad_probs = contract(v, g, 0, 0)
            delta = jnp.sum(e * grad_probs, 0, keepdims=True) * share
            attention = e * share
            grad_scores = (attention * (grad_probs - delta)).astype(BF)
            gv_s = jnp.dot(attention.astype(BF), g.T, preferred_element_type=F32)
            gk_s = jnp.dot(grad_scores, q_low.T, preferred_element_type=F32)
            gq = sc * jnp.dot(k_low, grad_scores, preferred_element_type=F32)
            gq = q_inv * (gq - q_unit * jnp.sum(q_unit * gq, 0, keepdims=True))
            grad_t[pl.ds(o, HEAD), pl.ds(s, step)] = gq.astype(BF)
            gv = gv_s if gv is None else gv + gv_s
            gk = gk_s if gk is None else gk + gk_s
        gk = sc * gk.T
        gk = k_inv * (gk - k_unit * jnp.sum(k_unit * gk, 0, keepdims=True))
        grad_t[pl.ds(o + HEAD, HEAD), :] = gk.astype(BF)
        grad_t[pl.ds(o + 2 * HEAD, HEAD), :] = gv.astype(BF).T

    rank = up.shape[0]
    pack[pl.ds(0, rank), pl.ds(0, cols)] = (0.5 * contract(low_t[...], grad_t[...], 1, 1)).astype(BF)
    low_grad_t = pack.at[pl.ds(rank, rank), pl.ds(0, seq)]
    low_grad_t[...] = (0.5 * jnp.dot(up, grad_t[...], preferred_element_type=F32)).astype(BF)
    for p in range(outs):
        part = token_grads(low_grad_t, grad_t, w_all, down_t, (first + p) * tok, tok)
        parts[p][...] = part.astype(parts[p].dtype)


def attention_call(scale, cots, c_from, qkv_t, low_t, w_all, down_t, up, tok, first, dtypes):
    cols, seq = qkv_t.shape
    rank, width = down_t.shape
    smem = pl.BlockSpec(memory_space=pltpu.SMEM)
    outs = len(dtypes)
    return pl.pallas_call(
        functools.partial(attention_kernel, cols // (3 * HEAD), tok, c_from, first, outs),
        out_shape=[in_vmem((tok, width), t) for t in dtypes]
        + [in_vmem((cols, seq), BF), in_vmem((2 * rank, max(cols, seq)), BF)],
        in_specs=[smem] + whole_vmem(len(cots) + 5),
        out_specs=whole_vmem(outs + 2),
        scratch_shapes=[pltpu.VMEM((cols // 3, seq), BF)],
        compiler_params=pltpu.CompilerParams(vmem_limit_bytes=VMEM),
        cost_estimate=SMALL,
        name="attention_grads",
    )(scale, *vmem(cots), qkv_t, low_t, w_all, down_t, up)


def other_half(x):
    rows, cols = x.shape
    half = cols // 2
    if half % 128:
        return lax.dynamic_slice(x, (0, (lax.axis_index("rows") ^ 1) % 2 * half), (rows, half))

    def kernel(x, out):
        core = lax.rem(lax.axis_index("rows") ^ 1, 2)
        out[...] = x[:, pl.ds(pl.multiple_of(core * half, 128), half)]

    return pl.pallas_call(
        kernel,
        out_shape=in_vmem((rows, half), x.dtype),
        in_specs=whole_vmem(1),
        out_specs=whole_vmem(1)[0],
        compiler_params=pltpu.CompilerParams(vmem_limit_bytes=VMEM),
        cost_estimate=SMALL,
        name="other_half",
    )(*vmem([x]))


def add(a, b):
    def kernel(a, b, out):
        out[...] = (a[...] + b[...].astype(F32)).astype(BF)

    return pl.pallas_call(
        kernel,
        out_shape=in_vmem(a.shape, BF),
        in_specs=whole_vmem(2),
        out_specs=whole_vmem(1)[0],
        compiler_params=pltpu.CompilerParams(vmem_limit_bytes=VMEM),
        cost_estimate=SMALL,
        name="add",
    )(*vmem([a, b]))


def own_kernel(deps, grad_t, pack, w_all, down_t, *refs):
    mine, rest = refs[deps], refs[deps + 1 :]
    tok = mine.shape[0]
    rank = down_t.shape[0]
    low_grad_t = pack.at[pl.ds(rank, rank), :]
    mine[...] = token_grads(low_grad_t, grad_t, w_all, down_t, 0, tok)
    part = token_grads(low_grad_t, grad_t, w_all, down_t, tok, tok).astype(BF)
    at = 0
    for out in rest:
        out[...] = part[at : at + out.shape[0]]
        at += out.shape[0]


def own_call(grad_t, pack, w_all, down_t, tok, blocks, deps):
    width = down_t.shape[1]
    return pl.pallas_call(
        functools.partial(own_kernel, len(deps)),
        out_shape=[in_vmem((tok, width), F32)] + [in_vmem((rows, width), BF) for rows in blocks],
        in_specs=whole_vmem(4 + len(deps)),
        out_specs=whole_vmem(1 + len(blocks)),
        compiler_params=pltpu.CompilerParams(vmem_limit_bytes=VMEM),
        cost_estimate=SMALL,
        name="own_grads",
    )(grad_t, pack, w_all, down_t, *vmem(deps))


def adapter_kernel(tok, *refs):
    packs, (x_all, down_grad_t, up_grad) = refs[:-3], refs[-3:]
    rank = down_grad_t.shape[0]
    r = lax.axis_index("rows")
    total = None
    for j, pack in enumerate(packs):
        blocks = [pack[pl.ds(rank, rank), pl.ds((q ^ j) * tok, tok)] for q in range(len(packs))]
        term = jnp.concatenate(blocks, axis=1).astype(F32)
        total = term if total is None else total + term
    down_grad_t[...] = jnp.dot(total.astype(BF), x_all[...], preferred_element_type=F32)
    cols = up_grad.shape[1] // len(packs)
    for j, pack in enumerate(packs):
        if cols % 128 == 0:
            up_grad[:, pl.ds(pl.multiple_of((r ^ j) * cols, 128), cols)] = pack[pl.ds(0, rank), pl.ds(0, cols)].astype(F32)


def adapter_call(packs, x_all, rank, all_cols, tok):
    down_grad_t, up_grad = pl.pallas_call(
        functools.partial(adapter_kernel, tok),
        out_shape=[
            jax.ShapeDtypeStruct((rank, x_all.shape[1]), F32),
            jax.ShapeDtypeStruct((rank, all_cols), F32),
        ],
        in_specs=whole_vmem(len(packs) + 1),
        out_specs=whole_vmem(2),
        compiler_params=pltpu.CompilerParams(vmem_limit_bytes=VMEM),
        cost_estimate=SMALL,
        name="adapter_grads",
    )(*vmem(packs), x_all)
    cols = all_cols // len(packs)
    if cols % 128:
        for j, pack in enumerate(packs):
            up_grad = lax.dynamic_update_slice(up_grad, pack[:rank, :cols].astype(F32), (0, (lax.axis_index("rows") ^ j) * cols))
    return down_grad_t, up_grad


def final_kernel(tokens, gain, inv_rms, mine, *refs):
    refs, out = refs[:-1], refs[-1]
    grad = mine[...]
    part = []
    for x in refs:
        part.append(x[...].astype(F32))
        if sum(p.shape[0] for p in part) == tokens.shape[0]:
            grad = grad + jnp.concatenate(part, axis=0)
            part = []
    x = tokens[...].astype(F32)
    inv = inv_rms[...]
    scaled = grad * gain[...]
    mean = jnp.mean(scaled * x, -1, keepdims=True)
    out[...] = (inv * (scaled - x * (inv * inv * mean))).astype(BF)


def final_call(tokens, gain, inv_rms, mine, terms):
    return pl.pallas_call(
        final_kernel,
        out_shape=jax.ShapeDtypeStruct(tokens.shape, BF),
        in_specs=whole_vmem(4 + len(terms)),
        out_specs=whole_vmem(1)[0],
        compiler_params=pltpu.CompilerParams(vmem_limit_bytes=VMEM),
        cost_estimate=SMALL,
        name="input_grads",
    )(tokens, gain, inv_rms, mine, *vmem(terms))


def prepare_kernel(chips, head_cols, sizes, features, gain_map, tokens, core_tokens, cot, *refs):
    count, outs = len(sizes), len(sizes) + len(chips)
    normed, core_normed, gain, inv_rms = refs[count : count + 4]
    cut = refs[count + 4 : count + 4 + outs]
    map_in, tokens_in, core_in, sems = refs[count + 4 + outs :]
    r = lax.axis_index("rows")
    copies = [(tokens, tokens_in), (core_tokens, core_in), (gain_map, map_in)]
    for x, size, out in zip(refs, sizes, cut):
        copies.append((x.at[:, pl.ds(pl.multiple_of(r * size, 128), size)] if size else x, out))
    for j, out in zip(chips, cut[count:]):
        chip = lax.div(r ^ j, 2) * (2 * head_cols)
        copies.append((cot.at[:, pl.ds(pl.multiple_of(chip, 128), 2 * head_cols)], out))
    copies = [pltpu.make_async_copy(a, b, sems.at[i]) for i, (a, b) in enumerate(copies)]
    for c in copies:
        c.start()
    half = features.shape[1]
    col = features[...].T
    for c in copies[:3]:
        c.wait()
    total = jnp.sum(col[:, :1] * map_in[:half, :], 0, keepdims=True)
    total = total + jnp.sum(col[:, 1:] * map_in[half:, :], 0, keepdims=True)
    gain[...] = 1.0 + total
    for x, out in ((tokens_in, normed), (core_in, core_normed)):
        x = x[...].astype(F32)
        inv = lax.rsqrt(jnp.mean(x * x, -1, keepdims=True) + EPS)
        if out is normed:
            inv_rms[...] = inv
        out[...] = (x * inv * gain[...]).astype(BF)
    for c in copies[3:]:
        c.wait()


def prepare_call(features, gain_map, tokens, core_tokens, cot, chips, head_cols, arrays):
    tok, width = tokens.shape
    shapes = [((tok, width), BF), ((tok, width), BF), ((1, width), F32), ((tok, 1), F32)]
    shapes += [((x.shape[0], size or x.shape[1]), BF) for x, size in arrays]
    shapes += [((tok, 2 * head_cols), BF)] * len(chips)
    copies = 3 + len(arrays) + len(chips)
    return pl.pallas_call(
        functools.partial(prepare_kernel, chips, head_cols, [size for _, size in arrays]),
        out_shape=[in_vmem(*shape) for shape in shapes],
        in_specs=whole_vmem(1) + [pl.BlockSpec(memory_space=pl.ANY)] * (4 + len(arrays)),
        out_specs=whole_vmem(len(shapes)),
        scratch_shapes=[
            pltpu.VMEM(gain_map.shape, F32),
            pltpu.VMEM((tok, width), BF),
            pltpu.VMEM((tok, width), BF),
            pltpu.SemaphoreType.DMA((copies,)),
        ],
        compiler_params=pltpu.CompilerParams(vmem_limit_bytes=VMEM),
        cost_estimate=SMALL,
        name="prepare",
    )(features, gain_map, tokens, core_tokens, cot, *[x for x, _ in arrays])


def per_device(
    mesh_shape,
    tokens,
    timestep,
    timestep_gain_map,
    query_key_value_weight,
    adapter_down_weight,
    adapter_up_weight,
    head_score_scale,
    heads_output_grad,
):
    dp, n = mesh_shape
    axes = ("dp", "rows")
    r, d = lax.axis_index("rows"), lax.axis_index("dp")

    def send(x, target):
        perm = []
        for a in range(dp):
            for b in range(n):
                a2, b2 = target(a, b)
                perm.append((a * n + b, a2 * n + b2))
        return lax.ppermute(x, axes, perm)

    def to_row(x, j):
        return send(x, lambda a, b: (a, b ^ j))

    tok, width = tokens.shape
    weight, cot_all = query_key_value_weight, heads_output_grad
    k_rows = weight.shape[0]
    cols = weight.shape[1] // n
    head_cols = cot_all.shape[1] // n
    chips = list(range(2, n, 2))

    cuts = 2 if cols % 256 == 0 else 1
    part_cols = cols // cuts
    odd = d % 2
    fetched = []
    for j in chips:
        for c in range(cuts):
            x = lax.dynamic_slice(weight, (0, (r ^ (j + odd)) * cols + c * part_cols), (k_rows, part_cols))
            fetched.append((send(x, lambda a, b, j=j: (a, b ^ (j + a % 2))), j, c))

    core_weight, core_tokens, core_cot = (to_row(x, 1) for x in (weight, tokens, cot_all))

    def mine(x, size):
        return (x, size) if size % 128 == 0 else (lax.dynamic_slice(x, (0, r * size), (x.shape[0], size)), 0)

    own_map, own_tokens, own_cot = hbm([timestep_gain_map, tokens, cot_all])
    normed, core_normed, gain, inv_rms, own_w, core_w, own_cot, core_cot, *chip_cot = prepare_call(
        time_features(timestep), own_map, own_tokens, core_tokens, own_cot, chips, head_cols,
        [mine(weight, cols), mine(core_weight, cols), mine(cot_all, head_cols), mine(core_cot, head_cols)],
    )
    arrays = [own_w, core_w, normed, core_normed]
    w_from, x_from = [(0, 0, 0, None), (1, 0, 1, None)], [(2, tok), (3, tok)]
    rows = tok // 2 if tok % 32 == 0 else tok
    count = tok // rows
    first = [i for i, (_, _, c) in enumerate(fetched) if c == 0]
    later = gate(
        [normed] + chip_cot + [fetched[i][0] for i in first], [rows] + [tok] * len(chips) + [k_rows] * len(first)
    )
    later_normed, chip_cot = later[:count], later[count : count + len(chips)]
    for i, x in zip(first, later[count + len(chips) :]):
        fetched[i] = (x, *fetched[i][1:])
    sharers = []
    for x, j, c in fetched:
        for other in range(2):
            w_from.append((len(arrays), c * part_cols, j, other))
            arrays.append(send(x, lambda a, b: (a ^ 1, b)) if other else x)
            if other and c == 0:
                sharers.append(arrays[-1])

    halves = [to_row(x, j) for j in chips for x in later_normed]
    later = list(gate(halves, [rows] * len(halves), *sharers))
    for i in range(0, len(halves), count):
        for x in halves[i : i + count] + [to_row(x, 1) for x in later[i : i + count]]:
            x_from.append((len(arrays), rows))
            arrays.append(x)

    cots, c_from = [own_cot, core_cot], [(0, False), (1, False)]
    for j, x in zip(chips, chip_cot):
        x = to_row(x, j)
        c_from += [(len(cots), True), (len(cots) + 1, False)]
        cots += [x, to_row(other_half(x), 1)]

    rank = adapter_up_weight.shape[0]
    down_t = adapter_down_weight.T
    up = adapter_up_weight
    if cols % 128:
        up = lax.dynamic_slice(up, (0, r * cols), (rank, cols))
    x_all, w_all, qkv_t, low_t = qkv_call(
        arrays, tuple(x_from), tuple(w_from), down_t, up, n * tok, cols
    )
    *others, grad_t, pack = attention_call(
        head_score_scale, cots, tuple(c_from), qkv_t, low_t, w_all, down_t, up, tok, 2, (F32, BF) * len(chips)
    )

    totals = [add(others[2 * i], to_row(others[2 * i + 1], 1)) for i in range(len(chips))]
    sums = [to_row(x, j) for x, j in zip(totals, chips)]
    packs = {0: pack, 1: to_row(pack, 1)}
    for j in chips:
        packs[j] = to_row(pack, j)
    blocks = (tok * 7 // 8, tok // 8) if tok % 128 == 0 else (tok,)
    mine, *core_part = own_call(grad_t, pack, w_all, down_t, tok, blocks, totals + [packs[j] for j in chips])
    core_part = [to_row(x, 1) for x in core_part]

    for j in chips:
        packs[j ^ 1] = to_row(packs[j], 1)
    down_grad_t, up_grad = adapter_call([packs[j] for j in range(n)], x_all, rank, n * cols, tok)

    input_grad = final_call(tokens, gain, inv_rms, mine, core_part + sums)
    return (input_grad, down_grad_t.T, up_grad)


def solution(mesh):
    in_specs = (
        P(("dp", "rows"), None),
        P("dp"),
        P(),
        P("rows", None),
        P(),
        P(),
        P("rows"),
        P(("dp", "rows"), None),
    )
    out_specs = (P(("dp", "rows"), None), P("dp", None), P("dp", None))
    shape = (mesh.shape["dp"], mesh.shape["rows"])
    return jax.shard_map(
        functools.partial(per_device, shape), mesh=mesh, in_specs=in_specs, out_specs=out_specs, check_vma=False
    )
```

```python
import functools
import math

import jax
import jax.numpy as jnp
from jax import lax
from jax.experimental import pallas as pl
from jax.experimental.pallas import tpu as pltpu
from jax.sharding import PartitionSpec as P

HEAD = 64
EMB = 256
EPS = 1e-06
LOG2E = 1.4426950408889634
BF = jnp.bfloat16
F32 = jnp.float32
VMEM = 16 * 1024 * 1024
SMALL = pl.CostEstimate(flops=1, bytes_accessed=1, transcendentals=0)


def time_features(timestep):
    half_emb = EMB // 2
    frequency = jnp.exp(-math.log(10000.0) * jnp.arange(half_emb, dtype=F32) / half_emb)
    phases = timestep.astype(F32)[0] * frequency
    return jnp.stack([jnp.cos(phases), jnp.sin(phases)])


def contract(a, b, a_dim, b_dim):
    return lax.dot_general(a, b, (((a_dim,), (b_dim,)), ((), ())), preferred_element_type=F32)


def columns(x, size):
    if x.shape[1] == size:
        return x[...]
    return x[:, pl.ds(pl.multiple_of(lax.axis_index("rows") * size, 128), size)]


def multiply(x_all, w_all, down_t, up, put):
    seq = x_all.shape[0]
    step = math.gcd(512, seq) if seq > 512 else seq
    for s in range(0, seq, step):
        x = x_all[pl.ds(s, step), :]
        low = contract(x, down_t[...], 1, 1).astype(BF)
        qkv = jnp.dot(x, w_all[...], preferred_element_type=F32)
        qkv = qkv + 0.5 * jnp.dot(low, up, preferred_element_type=F32)
        put(s, step, qkv.astype(BF).T, low.T)


def qkv_kernel(x_from, w_from, *refs):
    down_t, up_in = refs[-6:-4]
    r, odd = lax.axis_index("rows"), lax.rem(lax.axis_index("dp"), 2)
    up = columns(up_in, refs[-2].shape[0])
    x_all, w_all, qkv_t, low_t = refs[-4:]
    at = 0
    for i, rows in x_from:
        x_all[pl.ds(at, rows), :] = refs[i][...]
        at += rows
    for i, to, j, other in w_from:
        rows, cols = refs[i].shape
        holder = r ^ j if other is None else r ^ (j + (odd ^ other))
        base = pl.multiple_of(holder * rows, 16)
        w_all[pl.ds(base, rows), pl.ds(to, cols)] = refs[i][...]

    def put(start, rows, qkv, low):
        qkv_t[:, pl.ds(start, rows)] = qkv
        low_t[:, pl.ds(start, rows)] = low

    multiply(x_all, w_all, down_t, up, put)


def qkv_call(arrays, x_from, w_from, down_t, up, seq, cols):
    rank, width = down_t.shape
    return pl.pallas_call(
        functools.partial(qkv_kernel, x_from, w_from),
        out_shape=[
            in_vmem((seq, width), BF),
            in_vmem((width, cols), BF),
            in_vmem((cols, seq), BF),
            in_vmem((rank, seq), BF),
        ],
        in_specs=whole_vmem(len(arrays) + 2),
        out_specs=whole_vmem(4),
        compiler_params=pltpu.CompilerParams(vmem_limit_bytes=VMEM),
        cost_estimate=SMALL,
        name="qkv",
    )(*vmem(arrays), down_t, up)


def last_qkv_kernel(tok, places, last_places, *refs):
    w_all, first_qkv, first_low, down_t, up_in, x_all, qkv_t, low_t = refs[-8:]
    at = 0
    for x in refs[:-8]:
        rows = x.shape[0]
        x_all[pl.ds(at, rows), :] = x[...]
        at += rows
    for i, place in enumerate(places):
        qkv_t[:, pl.ds(place * tok, tok)] = first_qkv[:, pl.ds(i * tok, tok)]
        low_t[:, pl.ds(place * tok, tok)] = first_low[:, pl.ds(i * tok, tok)]

    def put(start, rows, qkv, low):
        for at in range(start, start + rows, tok):
            place = last_places[at // tok] * tok
            qkv_t[:, pl.ds(place, tok)] = qkv[:, at - start : at - start + tok]
            low_t[:, pl.ds(place, tok)] = low[:, at - start : at - start + tok]

    multiply(x_all, w_all, down_t, columns(up_in, qkv_t.shape[0]), put)


def last_qkv_call(tok, places, last_places, xs, w_all, first_qkv, first_low, down_t, up):
    rank, width = down_t.shape
    cols = w_all.shape[1]
    seq = (len(places) + len(last_places)) * tok
    return pl.pallas_call(
        functools.partial(last_qkv_kernel, tok, places, last_places),
        out_shape=[
            in_vmem((len(last_places) * tok, width), BF),
            in_vmem((cols, seq), BF),
            in_vmem((rank, seq), BF),
        ],
        in_specs=whole_vmem(len(xs) + 5),
        out_specs=whole_vmem(3),
        compiler_params=pltpu.CompilerParams(vmem_limit_bytes=VMEM),
        cost_estimate=SMALL,
        name="last_qkv",
    )(*vmem(xs), *vmem([w_all, first_qkv, first_low]), down_t, up)


def gate(xs, blocks, *deps):
    wanted = [(i, sum(sizes[:k]), rows) for i, sizes in enumerate(blocks) for k, rows in enumerate(sizes)]

    def kernel(*refs):
        for (i, at, rows), out in zip(wanted, refs[len(xs) + len(deps) :]):
            out[...] = refs[i][pl.ds(at, rows), :]

    return pl.pallas_call(
        kernel,
        out_shape=[in_vmem((rows, xs[i].shape[1]), xs[i].dtype) for i, _, rows in wanted],
        in_specs=whole_vmem(len(xs) + len(deps)),
        out_specs=whole_vmem(len(wanted)),
        compiler_params=pltpu.CompilerParams(vmem_limit_bytes=VMEM),
        cost_estimate=SMALL,
        name="gate",
    )(*vmem(xs), *vmem(deps))


def in_vmem(shape, dtype):
    return pltpu.VMEM(shape, dtype)


def vmem(xs):
    return [pltpu.with_memory_space_constraint(x, pltpu.VMEM) for x in xs]


def hbm(xs):
    return [pltpu.with_memory_space_constraint(x, pltpu.HBM) for x in xs]


def whole_vmem(count):
    return [pl.BlockSpec(memory_space=pltpu.VMEM)] * count


def qkv_call(arrays, x_from, w_from, down_t, up, seq, cols):
    rank, width = down_t.shape
    return pl.pallas_call(
        functools.partial(qkv_kernel, x_from, w_from),
        out_shape=[
            in_vmem((seq, width), BF),
            in_vmem((width, cols), BF),
            in_vmem((cols, seq), BF),
            in_vmem((rank, seq), BF),
        ],
        in_specs=whole_vmem(len(arrays) + 2),
        out_specs=whole_vmem(4),
        compiler_params=pltpu.CompilerParams(vmem_limit_bytes=VMEM),
        cost_estimate=SMALL,
        name="qkv",
    )(*vmem(arrays), down_t, up)


def token_grads(low_grad_t, grad_t, w_all, down_t, at, rows):
    grad = grad_t[:, pl.ds(at, rows)].T
    part = contract(grad, w_all[...], 1, 1)
    return part + contract(low_grad_t[:, pl.ds(at, rows)], down_t[...], 0, 0)


def attention_kernel(heads, tok, c_from, first, outs, *refs):
    refs = list(refs)
    scale = refs.pop(0)
    cots = [refs.pop(0) for _ in c_from]
    qkv_t, low_t, w_all, down_t, up_in = (refs.pop(0) for _ in range(5))
    parts = [refs.pop(0) for _ in range(outs)]
    grad_t, pack, cot_t = refs

    cols, seq = qkv_t.shape
    up = columns(up_in, cols)
    step = math.gcd(512, seq)
    width = cot_t.shape[0]
    start = lax.rem(lax.axis_index("rows"), 2) * width
    for j, (i, choose) in enumerate(c_from):
        if not choose:
            block = cots[i][...]
        elif width % 128 == 0:
            block = cots[i][:, pl.ds(pl.multiple_of(start, 128), width)]
        else:
            block = jnp.where(start == 0, cots[i][:, pl.ds(0, width)], cots[i][:, pl.ds(width, width)])
        cot_t[:, pl.ds(j * tok, tok)] = block.T

    for h in range(heads):
        o = 3 * HEAD * h
        kf = qkv_t[pl.ds(o + HEAD, HEAD), :].astype(F32)
        k_inv = lax.rsqrt(jnp.sum(kf * kf, 0, keepdims=True) + EPS)
        k_unit = kf * k_inv
        k_low = k_unit.astype(BF)
        v = qkv_t[pl.ds(o + 2 * HEAD, HEAD), :]
        sc = scale[h]
        gk = gv = None
        for s in range(0, seq, step):
            qf = qkv_t[pl.ds(o, HEAD), pl.ds(s, step)].astype(F32)
            q_inv = lax.rsqrt(jnp.sum(qf * qf, 0, keepdims=True) + EPS)
            q_unit = qf * q_inv
            q_low = q_unit.astype(BF)
            g = cot_t[pl.ds(HEAD * h, HEAD), pl.ds(s, step)]
            e = jnp.exp2(contract(k_low, q_low, 0, 0) * (sc * LOG2E))
            share = 1.0 / jnp.sum(e, 0, keepdims=True)
            grad_probs = contract(v, g, 0, 0)
            delta = jnp.sum(e * grad_probs, 0, keepdims=True) * share
            attention = e * share
            grad_scores = (attention * (grad_probs - delta)).astype(BF)
            gv_s = jnp.dot(attention.astype(BF), g.T, preferred_element_type=F32)
            gk_s = jnp.dot(grad_scores, q_low.T, preferred_element_type=F32)
            gq = sc * jnp.dot(k_low, grad_scores, preferred_element_type=F32)
            gq = q_inv * (gq - q_unit * jnp.sum(q_unit * gq, 0, keepdims=True))
            grad_t[pl.ds(o, HEAD), pl.ds(s, step)] = gq.astype(BF)
            gv = gv_s if gv is None else gv + gv_s
            gk = gk_s if gk is None else gk + gk_s
        gk = sc * gk.T
        gk = k_inv * (gk - k_unit * jnp.sum(k_unit * gk, 0, keepdims=True))
        grad_t[pl.ds(o + HEAD, HEAD), :] = gk.astype(BF)
        grad_t[pl.ds(o + 2 * HEAD, HEAD), :] = gv.astype(BF).T

    rank = up.shape[0]
    pack[pl.ds(0, rank), pl.ds(0, cols)] = (0.5 * contract(low_t[...], grad_t[...], 1, 1)).astype(BF)
    low_grad_t = pack.at[pl.ds(rank, rank), pl.ds(0, seq)]
    low_grad_t[...] = (0.5 * jnp.dot(up, grad_t[...], preferred_element_type=F32)).astype(BF)
    for p in range(0, outs, 4):
        count = min(4, outs - p)
        part = token_grads(low_grad_t, grad_t, w_all, down_t, (first + p) * tok, count * tok)
        for i in range(count):
            out = parts[p + i]
            out[...] = part[i * tok : (i + 1) * tok].astype(out.dtype)


def attention_call(scale, cots, c_from, qkv_t, low_t, w_all, down_t, up, tok, first, dtypes):
    cols, seq = qkv_t.shape
    rank, width = down_t.shape
    smem = pl.BlockSpec(memory_space=pltpu.SMEM)
    outs = len(dtypes)
    return pl.pallas_call(
        functools.partial(attention_kernel, cols // (3 * HEAD), tok, c_from, first, outs),
        out_shape=[in_vmem((tok, width), t) for t in dtypes]
        + [in_vmem((cols, seq), BF), in_vmem((2 * rank, max(cols, seq)), BF)],
        in_specs=[smem] + whole_vmem(len(cots) + 5),
        out_specs=whole_vmem(outs + 2),
        scratch_shapes=[pltpu.VMEM((cols // 3, seq), BF)],
        compiler_params=pltpu.CompilerParams(vmem_limit_bytes=VMEM),
        cost_estimate=SMALL,
        name="attention_grads",
    )(scale, *vmem(cots), qkv_t, low_t, w_all, down_t, up)


def other_half(x, dep):
    rows, cols = x.shape
    half = cols // 2
    if half % 128:
        return lax.dynamic_slice(x, (0, (lax.axis_index("rows") ^ 1) % 2 * half), (rows, half))

    def kernel(x, dep, out):
        core = lax.rem(lax.axis_index("rows") ^ 1, 2)
        out[...] = x[:, pl.ds(pl.multiple_of(core * half, 128), half)]

    return pl.pallas_call(
        kernel,
        out_shape=in_vmem((rows, half), x.dtype),
        in_specs=whole_vmem(2),
        out_specs=whole_vmem(1)[0],
        compiler_params=pltpu.CompilerParams(vmem_limit_bytes=VMEM),
        cost_estimate=SMALL,
        name="other_half",
    )(*vmem([x, dep]))


def add(a, b):
    def kernel(a, b, out):
        out[...] = (a[...] + b[...].astype(F32)).astype(BF)

    return pl.pallas_call(
        kernel,
        out_shape=in_vmem(a.shape, BF),
        in_specs=whole_vmem(2),
        out_specs=whole_vmem(1)[0],
        compiler_params=pltpu.CompilerParams(vmem_limit_bytes=VMEM),
        cost_estimate=SMALL,
        name="add",
    )(*vmem([a, b]))


def own_kernel(deps, grad_t, pack, w_all, down_t, *refs):
    mine, rest = refs[deps], refs[deps + 1 :]
    tok = mine.shape[0]
    rank = down_t.shape[0]
    low_grad_t = pack.at[pl.ds(rank, rank), :]
    part = token_grads(low_grad_t, grad_t, w_all, down_t, 0, 2 * tok)
    mine[...] = part[:tok]
    part = part[tok:].astype(BF)
    at = 0
    for out in rest:
        out[...] = part[at : at + out.shape[0]]
        at += out.shape[0]


def own_call(grad_t, pack, w_all, down_t, tok, blocks, deps):
    width = down_t.shape[1]
    return pl.pallas_call(
        functools.partial(own_kernel, len(deps)),
        out_shape=[in_vmem((tok, width), F32)] + [in_vmem((rows, width), BF) for rows in blocks],
        in_specs=whole_vmem(4 + len(deps)),
        out_specs=whole_vmem(1 + len(blocks)),
        compiler_params=pltpu.CompilerParams(vmem_limit_bytes=VMEM),
        cost_estimate=SMALL,
        name="own_grads",
    )(grad_t, pack, w_all, down_t, *vmem(deps))


def adapter_kernel(tok, places, *refs):
    packs, (first_x, last_x, down_grad_t, up_grad) = refs[:-4], refs[-4:]
    rank = down_grad_t.shape[0]
    r = lax.axis_index("rows")
    total = None
    for j, pack in enumerate(packs):
        blocks = [pack[pl.ds(rank, rank), pl.ds((q ^ j) * tok, tok)] for q in range(len(packs))]
        term = jnp.concatenate(blocks, axis=1).astype(F32)
        total = term if total is None else total + term
    total = total.astype(BF)
    grad = None
    for x, held in zip((first_x, last_x), places):
        part = jnp.concatenate([total[:, p * tok : (p + 1) * tok] for p in held], axis=1)
        term = jnp.dot(part, x[...], preferred_element_type=F32)
        grad = term if grad is None else grad + term
    down_grad_t[...] = grad
    cols = up_grad.shape[1] // len(packs)
    for j, pack in enumerate(packs):
        if cols % 128 == 0:
            up_grad[:, pl.ds(pl.multiple_of((r ^ j) * cols, 128), cols)] = pack[pl.ds(0, rank), pl.ds(0, cols)].astype(F32)


def adapter_call(packs, first_x, last_x, places, rank, all_cols, tok):
    down_grad_t, up_grad = pl.pallas_call(
        functools.partial(adapter_kernel, tok, places),
        out_shape=[
            jax.ShapeDtypeStruct((rank, first_x.shape[1]), F32),
            jax.ShapeDtypeStruct((rank, all_cols), F32),
        ],
        in_specs=whole_vmem(len(packs) + 2),
        out_specs=whole_vmem(2),
        compiler_params=pltpu.CompilerParams(vmem_limit_bytes=VMEM),
        cost_estimate=SMALL,
        name="adapter_grads",
    )(*vmem(packs), *vmem([first_x, last_x]))
    cols = all_cols // len(packs)
    if cols % 128:
        for j, pack in enumerate(packs):
            up_grad = lax.dynamic_update_slice(up_grad, pack[:rank, :cols].astype(F32), (0, (lax.axis_index("rows") ^ j) * cols))
    return down_grad_t, up_grad


def final_kernel(tokens, gain, inv_rms, mine, *refs):
    refs, out = refs[:-1], refs[-1]
    grad = mine[...]
    part = []
    for x in refs:
        part.append(x[...].astype(F32))
        if sum(p.shape[0] for p in part) == tokens.shape[0]:
            grad = grad + jnp.concatenate(part, axis=0)
            part = []
    x = tokens[...].astype(F32)
    inv = inv_rms[...]
    scaled = grad * gain[...]
    mean = jnp.mean(scaled * x, -1, keepdims=True)
    out[...] = (inv * (scaled - x * (inv * inv * mean))).astype(BF)


def final_call(tokens, gain, inv_rms, mine, terms):
    return pl.pallas_call(
        final_kernel,
        out_shape=jax.ShapeDtypeStruct(tokens.shape, BF),
        in_specs=whole_vmem(4 + len(terms)),
        out_specs=whole_vmem(1)[0],
        compiler_params=pltpu.CompilerParams(vmem_limit_bytes=VMEM),
        cost_estimate=SMALL,
        name="input_grads",
    )(tokens, gain, inv_rms, mine, *vmem(terms))


def prepare_kernel(chips, head_cols, sizes, features, gain_map, tokens, core_tokens, cot, *refs):
    count, outs = len(sizes), len(sizes) + len(chips)
    normed, core_normed, gain, inv_rms = refs[count : count + 4]
    cut = refs[count + 4 : count + 4 + outs]
    map_in, tokens_in, core_in, sems = refs[count + 4 + outs :]
    r = lax.axis_index("rows")
    copies = [(tokens, tokens_in), (core_tokens, core_in), (gain_map, map_in)]
    for x, size, out in zip(refs, sizes, cut):
        copies.append((x.at[:, pl.ds(pl.multiple_of(r * size, 128), size)] if size else x, out))
    for j, out in zip(chips, cut[count:]):
        chip = lax.div(r ^ j, 2) * (2 * head_cols)
        copies.append((cot.at[:, pl.ds(pl.multiple_of(chip, 128), 2 * head_cols)], out))
    copies = [pltpu.make_async_copy(a, b, sems.at[i]) for i, (a, b) in enumerate(copies)]
    for c in copies:
        c.start()
    half = features.shape[1]
    col = features[...].T
    for c in copies[:3]:
        c.wait()
    total = jnp.sum(col[:, :1] * map_in[:half, :], 0, keepdims=True)
    total = total + jnp.sum(col[:, 1:] * map_in[half:, :], 0, keepdims=True)
    gain[...] = 1.0 + total
    for x, out in ((tokens_in, normed), (core_in, core_normed)):
        x = x[...].astype(F32)
        inv = lax.rsqrt(jnp.mean(x * x, -1, keepdims=True) + EPS)
        if out is normed:
            inv_rms[...] = inv
        out[...] = (x * inv * gain[...]).astype(BF)
    for c in copies[3:]:
        c.wait()


def prepare_call(features, gain_map, tokens, core_tokens, cot, chips, head_cols, arrays):
    tok, width = tokens.shape
    shapes = [((tok, width), BF), ((tok, width), BF), ((1, width), F32), ((tok, 1), F32)]
    shapes += [((x.shape[0], size or x.shape[1]), BF) for x, size in arrays]
    shapes += [((tok, 2 * head_cols), BF)] * len(chips)
    copies = 3 + len(arrays) + len(chips)
    return pl.pallas_call(
        functools.partial(prepare_kernel, chips, head_cols, [size for _, size in arrays]),
        out_shape=[in_vmem(*shape) for shape in shapes],
        in_specs=whole_vmem(1) + [pl.BlockSpec(memory_space=pl.ANY)] * (4 + len(arrays)),
        out_specs=whole_vmem(len(shapes)),
        scratch_shapes=[
            pltpu.VMEM(gain_map.shape, F32),
            pltpu.VMEM((tok, width), BF),
            pltpu.VMEM((tok, width), BF),
            pltpu.SemaphoreType.DMA((copies,)),
        ],
        compiler_params=pltpu.CompilerParams(vmem_limit_bytes=VMEM),
        cost_estimate=SMALL,
        name="prepare",
    )(features, gain_map, tokens, core_tokens, cot, *[x for x, _ in arrays])


def per_device(
    mesh_shape,
    tokens,
    timestep,
    timestep_gain_map,
    query_key_value_weight,
    adapter_down_weight,
    adapter_up_weight,
    head_score_scale,
    heads_output_grad,
):
    dp, n = mesh_shape
    axes = ("dp", "rows")
    r, d = lax.axis_index("rows"), lax.axis_index("dp")

    def send(x, target):
        perm = []
        for a in range(dp):
            for b in range(n):
                a2, b2 = target(a, b)
                perm.append((a * n + b, a2 * n + b2))
        return lax.ppermute(x, axes, perm)

    def to_row(x, j):
        return send(x, lambda a, b: (a, b ^ j))

    tok, width = tokens.shape
    weight, cot_all = query_key_value_weight, heads_output_grad
    k_rows = weight.shape[0]
    cols = weight.shape[1] // n
    head_cols = cot_all.shape[1] // n
    chips = list(range(2, n, 2))

    cuts = 2 if cols % 256 == 0 else 1
    part_cols = cols // cuts
    odd = d % 2
    fetched = []
    for j in chips:
        for c in range(cuts):
            x = lax.dynamic_slice(weight, (0, (r ^ (j + odd)) * cols + c * part_cols), (k_rows, part_cols))
            fetched.append((send(x, lambda a, b, j=j: (a, b ^ (j + a % 2))), j, c))

    core_weight, core_tokens, core_cot = (to_row(x, 1) for x in (weight, tokens, cot_all))

    def mine(x, size):
        if size % 128 == 0 and x is weight:
            return hbm([x])[0], size
        return (x, size) if size % 128 == 0 else (lax.dynamic_slice(x, (0, r * size), (x.shape[0], size)), 0)

    own_map, own_tokens, own_cot = hbm([timestep_gain_map, tokens, cot_all])
    normed, core_normed, gain, inv_rms, own_w, core_w, own_cot, core_cot, *chip_cot = prepare_call(
        time_features(timestep), own_map, own_tokens, core_tokens, own_cot, chips, head_cols,
        [mine(weight, cols), mine(core_weight, cols), mine(cot_all, head_cols), mine(core_cot, head_cols)],
    )
    arrays = [own_w, core_w, normed, core_normed]
    w_from, x_from = [(0, 0, 0, None), (1, 0, 1, None)], [(2, tok), (3, tok)]
    rows = (tok * 5 // 8, tok * 3 // 8) if tok % 128 == 0 else (tok,)
    first = [i for i, (_, _, c) in enumerate(fetched) if c == 0]
    later = gate(
        [normed] + chip_cot + [fetched[i][0] for i in first], [rows] + [(tok,)] * len(chips) + [(k_rows,)] * len(first)
    )
    later_normed, chip_cot = later[: len(rows)], later[len(rows) : len(rows) + len(chips)]
    for i, x in zip(first, later[len(rows) + len(chips) :]):
        fetched[i] = (x, *fetched[i][1:])
    sharers = []
    for x, j, c in fetched:
        for other in range(2):
            w_from.append((len(arrays), c * part_cols, j, other))
            arrays.append(send(x, lambda a, b: (a ^ 1, b)) if other else x)
            if other and c == 0:
                sharers.append(arrays[-1])

    chip_normed = [to_row(x, j) for j in chips for x in later_normed]
    later = list(gate(chip_normed, [(x.shape[0],) for x in chip_normed], *sharers))
    for x in chip_normed:
        x_from.append((len(arrays), x.shape[0]))
        arrays.append(x)

    rank = adapter_up_weight.shape[0]
    down_t = adapter_down_weight.T
    up = adapter_up_weight
    if cols % 128:
        up = lax.dynamic_slice(up, (0, r * cols), (rank, cols))
    places, last_places = (0, 1, *chips), tuple(j + 1 for j in chips)
    first_x, w_all, first_qkv, first_low = qkv_call(
        arrays, tuple(x_from), tuple(w_from), down_t, up, len(places) * tok, cols
    )
    last_x, qkv_t, low_t = last_qkv_call(
        tok, places, last_places, [to_row(x, 1) for x in later], w_all, first_qkv, first_low, down_t, up
    )

    cots, c_from = [own_cot, core_cot], [(0, False), (1, False)]
    for j, x in zip(chips, chip_cot):
        x = to_row(x, j)
        c_from += [(len(cots), True), (len(cots) + 1, False)]
        cots += [x, to_row(other_half(x, first_low), 1)]

    *others, grad_t, pack = attention_call(
        head_score_scale, cots, tuple(c_from), qkv_t, low_t, w_all, down_t, up, tok, 2, (F32, BF) * len(chips)
    )

    totals = [add(others[2 * i], to_row(others[2 * i + 1], 1)) for i in range(len(chips))]
    sums = [to_row(x, j) for x, j in zip(totals, chips)]
    packs = {0: pack, 1: to_row(pack, 1)}
    for j in chips:
        packs[j] = to_row(pack, j)
    blocks = (tok * 7 // 8, tok // 8) if tok % 128 == 0 else (tok,)
    mine, *core_part = own_call(grad_t, pack, w_all, down_t, tok, blocks, totals + [packs[j] for j in chips])
    core_part = [to_row(x, 1) for x in core_part]

    for j in chips:
        packs[j ^ 1] = to_row(packs[j], 1)
    down_grad_t, up_grad = adapter_call(
        [packs[j] for j in range(n)], first_x, last_x, (places, last_places), rank, n * cols, tok
    )

    input_grad = final_call(tokens, gain, inv_rms, mine, core_part + sums)
    return (input_grad, down_grad_t.T, up_grad)


def solution(mesh):
    in_specs = (
        P(("dp", "rows"), None),
        P("dp"),
        P(),
        P("rows", None),
        P(),
        P(),
        P("rows"),
        P(("dp", "rows"), None),
    )
    out_specs = (P(("dp", "rows"), None), P("dp", None), P("dp", None))
    shape = (mesh.shape["dp"], mesh.shape["rows"])
    return jax.shard_map(
        functools.partial(per_device, shape), mesh=mesh, in_specs=in_specs, out_specs=out_specs, check_vma=False
    )
```

```python
import functools
import math

import jax
import jax.numpy as jnp
from jax import lax
from jax.experimental import pallas as pl
from jax.experimental.pallas import tpu as pltpu
from jax.sharding import PartitionSpec as P

HEAD = 64
EMB = 256
EPS = 1e-06
LOG2E = 1.4426950408889634
BF = jnp.bfloat16
F32 = jnp.float32
VMEM = 16 * 1024 * 1024
SMALL = pl.CostEstimate(flops=1, bytes_accessed=1, transcendentals=0)


def time_features(timestep):
    half_emb = EMB // 2
    frequency = jnp.exp(-math.log(10000.0) * jnp.arange(half_emb, dtype=F32) / half_emb)
    phases = timestep.astype(F32)[0] * frequency
    return jnp.stack([jnp.cos(phases), jnp.sin(phases)])


def contract(a, b, a_dim, b_dim):
    return lax.dot_general(a, b, (((a_dim,), (b_dim,)), ((), ())), preferred_element_type=F32)


def columns(x, size):
    if x.shape[1] == size:
        return x[...]
    return x[:, pl.ds(pl.multiple_of(lax.axis_index("rows") * size, 128), size)]


def multiply(x_all, w_all, down_t, up, put):
    seq = x_all.shape[0]
    step = math.gcd(512, seq) if seq > 512 else seq
    for s in range(0, seq, step):
        x = x_all[pl.ds(s, step), :]
        low = contract(x, down_t[...], 1, 1).astype(BF)
        qkv = jnp.dot(x, w_all[...], preferred_element_type=F32)
        qkv = qkv + 0.5 * jnp.dot(low, up, preferred_element_type=F32)
        put(s, step, qkv.astype(BF).T, low.T)


def qkv_kernel(x_from, w_from, *refs):
    down_t, up_in = refs[-6:-4]
    r, odd = lax.axis_index("rows"), lax.rem(lax.axis_index("dp"), 2)
    up = columns(up_in, refs[-2].shape[0])
    x_all, w_all, qkv_t, low_t = refs[-4:]
    at = 0
    for i, rows in x_from:
        x_all[pl.ds(at, rows), :] = refs[i][...]
        at += rows
    for i, to, j, other in w_from:
        rows, cols = refs[i].shape
        holder = r ^ j if other is None else r ^ (j + (odd ^ other))
        base = pl.multiple_of(holder * rows, 16)
        w_all[pl.ds(base, rows), pl.ds(to, cols)] = refs[i][...]

    def put(start, rows, qkv, low):
        qkv_t[:, pl.ds(start, rows)] = qkv
        low_t[:, pl.ds(start, rows)] = low

    multiply(x_all, w_all, down_t, up, put)


def qkv_call(arrays, x_from, w_from, down_t, up, seq, cols):
    rank, width = down_t.shape
    return pl.pallas_call(
        functools.partial(qkv_kernel, x_from, w_from),
        out_shape=[
            in_vmem((seq, width), BF),
            in_vmem((width, cols), BF),
            in_vmem((cols, seq), BF),
            in_vmem((rank, seq), BF),
        ],
        in_specs=whole_vmem(len(arrays) + 2),
        out_specs=whole_vmem(4),
        compiler_params=pltpu.CompilerParams(vmem_limit_bytes=VMEM),
        cost_estimate=SMALL,
        name="qkv",
    )(*vmem(arrays), down_t, up)


def last_qkv_kernel(tok, places, last_places, *refs):
    w_all, first_qkv, first_low, down_t, up_in, x_all, qkv_t, low_t = refs[-8:]
    at = 0
    for x in refs[:-8]:
        rows = x.shape[0]
        x_all[pl.ds(at, rows), :] = x[...]
        at += rows
    for i, place in enumerate(places):
        qkv_t[:, pl.ds(place * tok, tok)] = first_qkv[:, pl.ds(i * tok, tok)]
        low_t[:, pl.ds(place * tok, tok)] = first_low[:, pl.ds(i * tok, tok)]

    def put(start, rows, qkv, low):
        for at in range(start, start + rows, tok):
            place = last_places[at // tok] * tok
            qkv_t[:, pl.ds(place, tok)] = qkv[:, at - start : at - start + tok]
            low_t[:, pl.ds(place, tok)] = low[:, at - start : at - start + tok]

    multiply(x_all, w_all, down_t, columns(up_in, qkv_t.shape[0]), put)


def last_qkv_call(tok, places, last_places, xs, w_all, first_qkv, first_low, down_t, up):
    rank, width = down_t.shape
    cols = w_all.shape[1]
    seq = (len(places) + len(last_places)) * tok
    return pl.pallas_call(
        functools.partial(last_qkv_kernel, tok, places, last_places),
        out_shape=[
            in_vmem((len(last_places) * tok, width), BF),
            in_vmem((cols, seq), BF),
            in_vmem((rank, seq), BF),
        ],
        in_specs=whole_vmem(len(xs) + 5),
        out_specs=whole_vmem(3),
        compiler_params=pltpu.CompilerParams(vmem_limit_bytes=VMEM),
        cost_estimate=SMALL,
        name="last_qkv",
    )(*vmem(xs), *vmem([w_all, first_qkv, first_low]), down_t, up)


def gate(xs, blocks, *deps):
    xs = [x if isinstance(x, list) else [x] for x in xs]
    flat = [(i, x) for i, parts in enumerate(xs) for x in parts]
    wanted = [(i, sum(sizes[:k]), rows) for i, sizes in enumerate(blocks) for k, rows in enumerate(sizes)]

    def kernel(*refs):
        outs = refs[len(flat) + len(deps) :]
        for (i, at, rows), out in zip(wanted, outs):
            start = 0
            for (owner, _), x in zip(flat, refs):
                if owner == i:
                    low, high = max(at, start), min(at + rows, start + x.shape[0])
                    if low < high:
                        out[pl.ds(low - at, high - low), :] = x[pl.ds(low - start, high - low), :]
                    start += x.shape[0]

    return pl.pallas_call(
        kernel,
        out_shape=[in_vmem((rows, xs[i][0].shape[1]), xs[i][0].dtype) for i, _, rows in wanted],
        in_specs=whole_vmem(len(flat) + len(deps)),
        out_specs=whole_vmem(len(wanted)),
        compiler_params=pltpu.CompilerParams(vmem_limit_bytes=VMEM),
        cost_estimate=SMALL,
        name="gate",
    )(*vmem([x for _, x in flat]), *vmem(deps))


def in_vmem(shape, dtype):
    return pltpu.VMEM(shape, dtype)


def vmem(xs):
    return [pltpu.with_memory_space_constraint(x, pltpu.VMEM) for x in xs]


def hbm(xs):
    return [pltpu.with_memory_space_constraint(x, pltpu.HBM) for x in xs]


def whole_vmem(count):
    return [pl.BlockSpec(memory_space=pltpu.VMEM)] * count


def qkv_call(arrays, x_from, w_from, down_t, up, seq, cols):
    rank, width = down_t.shape
    return pl.pallas_call(
        functools.partial(qkv_kernel, x_from, w_from),
        out_shape=[
            in_vmem((seq, width), BF),
            in_vmem((width, cols), BF),
            in_vmem((cols, seq), BF),
            in_vmem((rank, seq), BF),
        ],
        in_specs=whole_vmem(len(arrays) + 2),
        out_specs=whole_vmem(4),
        compiler_params=pltpu.CompilerParams(vmem_limit_bytes=VMEM),
        cost_estimate=SMALL,
        name="qkv",
    )(*vmem(arrays), down_t, up)


def token_grads(low_grad_t, grad_t, w_all, down_t, at, rows):
    grad = grad_t[:, pl.ds(at, rows)].T
    part = contract(grad, w_all[...], 1, 1)
    return part + contract(low_grad_t[:, pl.ds(at, rows)], down_t[...], 0, 0)


def attention_kernel(heads, tok, c_from, first, outs, *refs):
    refs = list(refs)
    scale = refs.pop(0)
    cots = [refs.pop(0) for _ in c_from]
    qkv_t, low_t, w_all, down_t, up_in = (refs.pop(0) for _ in range(5))
    parts = [refs.pop(0) for _ in range(outs)]
    grad_t, pack, cot_t = refs

    cols, seq = qkv_t.shape
    up = columns(up_in, cols)
    step = math.gcd(512, seq)
    width = cot_t.shape[0]
    start = lax.rem(lax.axis_index("rows"), 2) * width
    for j, (i, choose) in enumerate(c_from):
        if not choose:
            block = cots[i][...]
        elif width % 128 == 0:
            block = cots[i][:, pl.ds(pl.multiple_of(start, 128), width)]
        else:
            block = jnp.where(start == 0, cots[i][:, pl.ds(0, width)], cots[i][:, pl.ds(width, width)])
        cot_t[:, pl.ds(j * tok, tok)] = block.T

    for h in range(heads):
        o = 3 * HEAD * h
        kf = qkv_t[pl.ds(o + HEAD, HEAD), :].astype(F32)
        k_inv = lax.rsqrt(jnp.sum(kf * kf, 0, keepdims=True) + EPS)
        k_unit = kf * k_inv
        k_low = k_unit.astype(BF)
        v = qkv_t[pl.ds(o + 2 * HEAD, HEAD), :]
        sc = scale[h]
        gk = gv = None
        for s in range(0, seq, step):
            qf = qkv_t[pl.ds(o, HEAD), pl.ds(s, step)].astype(F32)
            q_inv = lax.rsqrt(jnp.sum(qf * qf, 0, keepdims=True) + EPS)
            q_unit = qf * q_inv
            q_low = q_unit.astype(BF)
            g = cot_t[pl.ds(HEAD * h, HEAD), pl.ds(s, step)]
            e = jnp.exp2(contract(k_low, q_low, 0, 0) * (sc * LOG2E))
            share = 1.0 / jnp.sum(e, 0, keepdims=True)
            grad_probs = contract(v, g, 0, 0)
            delta = jnp.sum(e * grad_probs, 0, keepdims=True) * share
            attention = e * share
            grad_scores = (attention * (grad_probs - delta)).astype(BF)
            gv_s = jnp.dot(attention.astype(BF), g.T, preferred_element_type=F32)
            gk_s = jnp.dot(grad_scores, q_low.T, preferred_element_type=F32)
            gq = sc * jnp.dot(k_low, grad_scores, preferred_element_type=F32)
            gq = q_inv * (gq - q_unit * jnp.sum(q_unit * gq, 0, keepdims=True))
            grad_t[pl.ds(o, HEAD), pl.ds(s, step)] = gq.astype(BF)
            gv = gv_s if gv is None else gv + gv_s
            gk = gk_s if gk is None else gk + gk_s
        gk = sc * gk.T
        gk = k_inv * (gk - k_unit * jnp.sum(k_unit * gk, 0, keepdims=True))
        grad_t[pl.ds(o + HEAD, HEAD), :] = gk.astype(BF)
        grad_t[pl.ds(o + 2 * HEAD, HEAD), :] = gv.astype(BF).T

    rank = up.shape[0]
    pack[:, pl.ds(seq, cols)] = (0.5 * contract(low_t[...], grad_t[...], 1, 1)).astype(BF)
    low_grad_t = pack.at[:, pl.ds(0, seq)]
    low_grad_t[...] = (0.5 * jnp.dot(up, grad_t[...], preferred_element_type=F32)).astype(BF)
    for p in range(0, outs, 4):
        count = min(4, outs - p)
        part = token_grads(low_grad_t, grad_t, w_all, down_t, (first + p) * tok, count * tok)
        for i in range(count):
            out = parts[p + i]
            out[...] = part[i * tok : (i + 1) * tok].astype(out.dtype)


def attention_call(scale, cots, c_from, qkv_t, low_t, w_all, down_t, up, tok, first, dtypes):
    cols, seq = qkv_t.shape
    rank, width = down_t.shape
    smem = pl.BlockSpec(memory_space=pltpu.SMEM)
    outs = len(dtypes)
    return pl.pallas_call(
        functools.partial(attention_kernel, cols // (3 * HEAD), tok, c_from, first, outs),
        out_shape=[in_vmem((tok, width), t) for t in dtypes]
        + [in_vmem((cols, seq), BF), in_vmem((rank, seq + cols), BF)],
        in_specs=[smem] + whole_vmem(len(cots) + 5),
        out_specs=whole_vmem(outs + 2),
        scratch_shapes=[pltpu.VMEM((cols // 3, seq), BF)],
        compiler_params=pltpu.CompilerParams(vmem_limit_bytes=VMEM),
        cost_estimate=SMALL,
        name="attention_grads",
    )(scale, *vmem(cots), qkv_t, low_t, w_all, down_t, up)


def other_half(x, dep):
    rows, cols = x.shape
    half = cols // 2
    if half % 128:
        return lax.dynamic_slice(x, (0, (lax.axis_index("rows") ^ 1) % 2 * half), (rows, half))

    def kernel(x, dep, out):
        core = lax.rem(lax.axis_index("rows") ^ 1, 2)
        out[...] = x[:, pl.ds(pl.multiple_of(core * half, 128), half)]

    return pl.pallas_call(
        kernel,
        out_shape=in_vmem((rows, half), x.dtype),
        in_specs=whole_vmem(2),
        out_specs=whole_vmem(1)[0],
        compiler_params=pltpu.CompilerParams(vmem_limit_bytes=VMEM),
        cost_estimate=SMALL,
        name="other_half",
    )(*vmem([x, dep]))


def add(a, b):
    def kernel(a, b, out):
        out[...] = (a[...] + b[...].astype(F32)).astype(BF)

    return pl.pallas_call(
        kernel,
        out_shape=in_vmem(a.shape, BF),
        in_specs=whole_vmem(2),
        out_specs=whole_vmem(1)[0],
        compiler_params=pltpu.CompilerParams(vmem_limit_bytes=VMEM),
        cost_estimate=SMALL,
        name="add",
    )(*vmem([a, b]))


def own_kernel(deps, grad_t, pack, w_all, down_t, *refs):
    mine, rest = refs[deps], refs[deps + 1 :]
    tok = mine.shape[0]
    part = token_grads(pack, grad_t, w_all, down_t, 0, 2 * tok)
    mine[...] = part[:tok]
    part = part[tok:].astype(BF)
    at = 0
    for out in rest:
        out[...] = part[at : at + out.shape[0]]
        at += out.shape[0]


def own_call(grad_t, pack, w_all, down_t, tok, blocks, deps):
    width = down_t.shape[1]
    return pl.pallas_call(
        functools.partial(own_kernel, len(deps)),
        out_shape=[in_vmem((tok, width), F32)] + [in_vmem((rows, width), BF) for rows in blocks],
        in_specs=whole_vmem(4 + len(deps)),
        out_specs=whole_vmem(1 + len(blocks)),
        compiler_params=pltpu.CompilerParams(vmem_limit_bytes=VMEM),
        cost_estimate=SMALL,
        name="own_grads",
    )(grad_t, pack, w_all, down_t, *vmem(deps))


def adapter_kernel(tok, places, *refs):
    packs, (first_x, last_x, down_grad_t, up_grad) = refs[:-4], refs[-4:]
    r = lax.axis_index("rows")
    total = None
    for j, pack in enumerate(packs):
        blocks = [pack[:, pl.ds((q ^ j) * tok, tok)] for q in range(len(packs))]
        term = jnp.concatenate(blocks, axis=1).astype(F32)
        total = term if total is None else total + term
    total = total.astype(BF)
    grad = None
    for x, held in zip((first_x, last_x), places):
        part = jnp.concatenate([total[:, p * tok : (p + 1) * tok] for p in held], axis=1)
        term = jnp.dot(part, x[...], preferred_element_type=F32)
        grad = term if grad is None else grad + term
    down_grad_t[...] = grad
    cols = up_grad.shape[1] // len(packs)
    for j, pack in enumerate(packs):
        if cols % 128 == 0:
            up_grad[:, pl.ds(pl.multiple_of((r ^ j) * cols, 128), cols)] = pack[:, pl.ds(len(packs) * tok, cols)].astype(F32)


def adapter_call(packs, first_x, last_x, places, rank, all_cols, tok):
    down_grad_t, up_grad = pl.pallas_call(
        functools.partial(adapter_kernel, tok, places),
        out_shape=[
            jax.ShapeDtypeStruct((rank, first_x.shape[1]), F32),
            jax.ShapeDtypeStruct((rank, all_cols), F32),
        ],
        in_specs=whole_vmem(len(packs) + 2),
        out_specs=whole_vmem(2),
        compiler_params=pltpu.CompilerParams(vmem_limit_bytes=VMEM),
        cost_estimate=SMALL,
        name="adapter_grads",
    )(*vmem(packs), *vmem([first_x, last_x]))
    cols = all_cols // len(packs)
    if cols % 128:
        for j, pack in enumerate(packs):
            up_grad = lax.dynamic_update_slice(up_grad, pack[:, len(packs) * tok :].astype(F32), (0, (lax.axis_index("rows") ^ j) * cols))
    return down_grad_t, up_grad


def scale_kernel(tokens, gain, inv_rms, mine, *refs):
    blocks, (total, token_gain, scale, slope) = refs[:-4], refs[-4:]
    at = 0
    for block in blocks:
        rows = pl.ds(at, block.shape[0])
        total[rows, :] = mine[rows, :] + block[...].astype(F32)
        at += block.shape[0]
    x = tokens[...].astype(F32)
    inv = inv_rms[...]
    token_gain[...] = x * gain[...]
    scale[...] = inv * gain[...]
    slope[...] = x * (inv * inv * inv * (1.0 / x.shape[1]))


def scale_call(tokens, gain, inv_rms, mine, blocks):
    return pl.pallas_call(
        scale_kernel,
        out_shape=[in_vmem(tokens.shape, F32)] * 4,
        in_specs=whole_vmem(4 + len(blocks)),
        out_specs=whole_vmem(4),
        compiler_params=pltpu.CompilerParams(vmem_limit_bytes=VMEM),
        cost_estimate=SMALL,
        name="scale",
    )(tokens, gain, inv_rms, mine, *vmem(blocks))


def final_kernel(total, token_gain, scale, slope, *refs):
    terms, (out, made, sems) = refs[:-3], refs[-3:]
    count = sems.shape[0]
    rows = made.shape[0] // count
    copies = []
    for i in range(count):
        block = pl.ds(i * rows, rows)
        grad = total[block, :]
        for x in terms:
            grad = grad + x[block, :].astype(F32)
        moment = jnp.sum(grad * token_gain[block, :], -1, keepdims=True)
        made[block, :] = (grad * scale[block, :] - slope[block, :] * moment).astype(BF)
        copies.append(pltpu.make_async_copy(made.at[block], out.at[block], sems.at[i]))
        copies[-1].start()
    for c in copies:
        c.wait()


def final_call(held, terms):
    shape = held[0].shape
    count = 4 if shape[0] % 64 == 0 else 1
    return pl.pallas_call(
        final_kernel,
        out_shape=jax.ShapeDtypeStruct(shape, BF),
        in_specs=whole_vmem(4 + len(terms)),
        out_specs=pl.BlockSpec(memory_space=pltpu.HBM),
        scratch_shapes=[pltpu.VMEM(shape, BF), pltpu.SemaphoreType.DMA((count,))],
        compiler_params=pltpu.CompilerParams(vmem_limit_bytes=VMEM),
        cost_estimate=SMALL,
        name="input_grads",
    )(*vmem(held), *vmem(terms))


def prepare_kernel(chips, head_cols, sizes, features, gain_map, tokens, core_tokens, cot, *refs):
    count, outs = len(sizes), len(sizes) + len(chips)
    normed, core_normed, gain, inv_rms = refs[count : count + 4]
    cut = refs[count + 4 : count + 4 + outs]
    map_in, tokens_in, core_in, sems = refs[count + 4 + outs :]
    r = lax.axis_index("rows")
    copies = [(tokens, tokens_in), (core_tokens, core_in), (gain_map, map_in)]
    for x, size, out in zip(refs, sizes, cut):
        copies.append((x.at[:, pl.ds(pl.multiple_of(r * size, 128), size)] if size else x, out))
    for j, out in zip(chips, cut[count:]):
        chip = lax.div(r ^ j, 2) * (2 * head_cols)
        copies.append((cot.at[:, pl.ds(pl.multiple_of(chip, 128), 2 * head_cols)], out))
    copies = [pltpu.make_async_copy(a, b, sems.at[i]) for i, (a, b) in enumerate(copies)]
    for c in copies:
        c.start()
    half = features.shape[1]
    col = features[...].T
    for c in copies[:3]:
        c.wait()
    total = jnp.sum(col[:, :1] * map_in[:half, :], 0, keepdims=True)
    total = total + jnp.sum(col[:, 1:] * map_in[half:, :], 0, keepdims=True)
    gain[...] = 1.0 + total
    for x, out in ((tokens_in, normed), (core_in, core_normed)):
        x = x[...].astype(F32)
        inv = lax.rsqrt(jnp.mean(x * x, -1, keepdims=True) + EPS)
        if out is normed:
            inv_rms[...] = inv
        out[...] = (x * inv * gain[...]).astype(BF)
    for c in copies[3:]:
        c.wait()


def prepare_call(features, gain_map, tokens, core_tokens, cot, chips, head_cols, arrays):
    tok, width = tokens.shape
    shapes = [((tok, width), BF), ((tok, width), BF), ((1, width), F32), ((tok, 1), F32)]
    shapes += [((x.shape[0], size or x.shape[1]), BF) for x, size in arrays]
    shapes += [((tok, 2 * head_cols), BF)] * len(chips)
    copies = 3 + len(arrays) + len(chips)
    return pl.pallas_call(
        functools.partial(prepare_kernel, chips, head_cols, [size for _, size in arrays]),
        out_shape=[in_vmem(*shape) for shape in shapes],
        in_specs=whole_vmem(1) + [pl.BlockSpec(memory_space=pl.ANY)] * (4 + len(arrays)),
        out_specs=whole_vmem(len(shapes)),
        scratch_shapes=[
            pltpu.VMEM(gain_map.shape, F32),
            pltpu.VMEM((tok, width), BF),
            pltpu.VMEM((tok, width), BF),
            pltpu.SemaphoreType.DMA((copies,)),
        ],
        compiler_params=pltpu.CompilerParams(vmem_limit_bytes=VMEM),
        cost_estimate=SMALL,
        name="prepare",
    )(features, gain_map, tokens, core_tokens, cot, *[x for x, _ in arrays])


def per_device(
    mesh_shape,
    tokens,
    timestep,
    timestep_gain_map,
    query_key_value_weight,
    adapter_down_weight,
    adapter_up_weight,
    head_score_scale,
    heads_output_grad,
):
    dp, n = mesh_shape
    axes = ("dp", "rows")
    r, d = lax.axis_index("rows"), lax.axis_index("dp")

    def send(x, target):
        perm = []
        for a in range(dp):
            for b in range(n):
                a2, b2 = target(a, b)
                perm.append((a * n + b, a2 * n + b2))
        return lax.ppermute(x, axes, perm)

    def to_row(x, j):
        return send(x, lambda a, b: (a, b ^ j))

    tok, width = tokens.shape
    weight, cot_all = query_key_value_weight, heads_output_grad
    k_rows = weight.shape[0]
    cols = weight.shape[1] // n
    head_cols = cot_all.shape[1] // n
    chips = list(range(2, n, 2))

    cuts = 2 if cols % 256 == 0 else 1
    part_cols = cols // cuts
    odd = d % 2
    fetched = []
    for j in chips:
        for c in range(cuts):
            x = lax.dynamic_slice(weight, (0, (r ^ (j + odd)) * cols + c * part_cols), (k_rows, part_cols))
            fetched.append((send(x, lambda a, b, j=j: (a, b ^ (j + a % 2))), j, c))

    core_weight, core_tokens, core_cot = (to_row(x, 1) for x in (weight, tokens, cot_all))

    def mine(x, size):
        if size % 128 == 0 and x is weight:
            return hbm([x])[0], size
        return (x, size) if size % 128 == 0 else (lax.dynamic_slice(x, (0, r * size), (x.shape[0], size)), 0)

    own_map, own_tokens, own_cot = hbm([timestep_gain_map, tokens, cot_all])
    normed, core_normed, gain, inv_rms, own_w, core_w, own_cot, core_cot, *chip_cot = prepare_call(
        time_features(timestep), own_map, own_tokens, core_tokens, own_cot, chips, head_cols,
        [mine(weight, cols), mine(core_weight, cols), mine(cot_all, head_cols), mine(core_cot, head_cols)],
    )
    arrays = [own_w, core_w, normed, core_normed]
    w_from, x_from = [(0, 0, 0, None), (1, 0, 1, None)], [(2, tok), (3, tok)]
    rows = (tok // 2, tok // 2) if tok % 128 == 0 else (tok,)
    relay_rows = (tok * 5 // 8, tok * 3 // 8) if tok % 128 == 0 else (tok,)
    first = [i for i, (_, _, c) in enumerate(fetched) if c == 0]
    later = gate(
        [normed] + chip_cot + [fetched[i][0] for i in first], [rows] + [(tok,)] * len(chips) + [(k_rows,)] * len(first)
    )
    later_normed, chip_cot = later[: len(rows)], later[len(rows) : len(rows) + len(chips)]
    for i, x in zip(first, later[len(rows) + len(chips) :]):
        fetched[i] = (x, *fetched[i][1:])
    sharers = []
    for x, j, c in fetched:
        for other in range(2):
            w_from.append((len(arrays), c * part_cols, j, other))
            arrays.append(send(x, lambda a, b: (a ^ 1, b)) if other else x)
            if other and c == 0:
                sharers.append(arrays[-1])

    chip_normed = [[to_row(x, j) for x in later_normed] for j in chips]
    later = list(gate(chip_normed, [relay_rows] * len(chips), *sharers))
    for x in sum(chip_normed, []):
        x_from.append((len(arrays), x.shape[0]))
        arrays.append(x)

    rank = adapter_up_weight.shape[0]
    down_t = adapter_down_weight.T
    up = adapter_up_weight
    if cols % 128:
        up = lax.dynamic_slice(up, (0, r * cols), (rank, cols))
    places, last_places = (0, 1, *chips), tuple(j + 1 for j in chips)
    first_x, w_all, first_qkv, first_low = qkv_call(
        arrays, tuple(x_from), tuple(w_from), down_t, up, len(places) * tok, cols
    )
    last_x, qkv_t, low_t = last_qkv_call(
        tok, places, last_places, [to_row(x, 1) for x in later], w_all, first_qkv, first_low, down_t, up
    )

    cots, c_from = [own_cot, core_cot], [(0, False), (1, False)]
    for j, x in zip(chips, chip_cot):
        x = to_row(x, j)
        c_from += [(len(cots), True), (len(cots) + 1, False)]
        cots += [x, to_row(other_half(x, first_low), 1)]

    *others, grad_t, pack = attention_call(
        head_score_scale, cots, tuple(c_from), qkv_t, low_t, w_all, down_t, up, tok, 2, (F32, BF) * len(chips)
    )

    totals = [add(others[2 * i], to_row(others[2 * i + 1], 1)) for i in range(len(chips))]
    sums = [to_row(x, j) for x, j in zip(totals, chips)]
    packs = {0: pack, 1: to_row(pack, 1)}
    for j in chips:
        packs[j] = to_row(pack, j)
    blocks = (tok * 7 // 8, tok // 8) if tok % 128 == 0 else (tok,)
    mine, *core_part = own_call(grad_t, pack, w_all, down_t, tok, blocks, totals + [packs[j] for j in chips])
    core_part = [to_row(x, 1) for x in core_part]

    for j in chips:
        packs[j ^ 1] = to_row(packs[j], 1)
    down_grad_t, up_grad = adapter_call(
        [packs[j] for j in range(n)], first_x, last_x, (places, last_places), rank, n * cols, tok
    )

    input_grad = final_call(scale_call(tokens, gain, inv_rms, mine, core_part), sums)
    return (input_grad, down_grad_t.T, up_grad)


def solution(mesh):
    in_specs = (
        P(("dp", "rows"), None),
        P("dp"),
        P(),
        P("rows", None),
        P(),
        P(),
        P("rows"),
        P(("dp", "rows"), None),
    )
    out_specs = (P(("dp", "rows"), None), P("dp", None), P("dp", None))
    shape = (mesh.shape["dp"], mesh.shape["rows"])
    return jax.shard_map(
        functools.partial(per_device, shape), mesh=mesh, in_specs=in_specs, out_specs=out_specs, check_vma=False
    )
```

```python
import functools
import math

import jax
import jax.numpy as jnp
from jax import lax
from jax.experimental import pallas as pl
from jax.experimental.pallas import tpu as pltpu
from jax.sharding import PartitionSpec as P

HEAD = 64
EMB = 256
EPS = 1e-06
LOG2E = 1.4426950408889634
BF = jnp.bfloat16
F32 = jnp.float32
VMEM = 16 * 1024 * 1024
SMALL = pl.CostEstimate(flops=1, bytes_accessed=1, transcendentals=0)


def time_features(timestep):
    half_emb = EMB // 2
    frequency = jnp.exp(-math.log(10000.0) * jnp.arange(half_emb, dtype=F32) / half_emb)
    phases = timestep.astype(F32)[0] * frequency
    return jnp.stack([jnp.cos(phases), jnp.sin(phases)])


def contract(a, b, a_dim, b_dim):
    return lax.dot_general(a, b, (((a_dim,), (b_dim,)), ((), ())), preferred_element_type=F32)


def columns(x, size):
    if x.shape[1] == size:
        return x[...]
    return x[:, pl.ds(pl.multiple_of(lax.axis_index("rows") * size, 128), size)]


def multiply(x_all, w_all, down_t, up, put):
    seq = x_all.shape[0]
    step = math.gcd(512, seq) if seq > 512 else seq
    for s in range(0, seq, step):
        x = x_all[pl.ds(s, step), :]
        low = contract(x, down_t[...], 1, 1).astype(BF)
        qkv = jnp.dot(x, w_all[...], preferred_element_type=F32)
        qkv = qkv + 0.5 * jnp.dot(low, up, preferred_element_type=F32)
        put(s, step, qkv.astype(BF).T, low.T)


def qkv_kernel(n, x_from, w_from, *refs):
    down_t, up_in = refs[-6:-4]
    r, d = lax.axis_index("rows"), lax.axis_index("dp")
    up = columns(up_in, refs[-2].shape[0])
    x_all, w_all, qkv_t, low_t = refs[-4:]
    at = 0
    for i, rows in x_from:
        x_all[pl.ds(at, rows), :] = refs[i][...]
        at += rows
    for i, to, j, group, other, row in w_from:
        rows, cols = refs[i].shape
        holder, part = r ^ j, 0
        if group == 2:
            holder = r ^ (j + (lax.rem(lax.div(d, 2), 2) ^ other))
        elif group == 4:
            share = lax.rem(d, 4) ^ other
            holder, part = r ^ (j + lax.rem(share, 2)), lax.div(share, 2)
        held_rows = w_all.shape[0] // n
        base = pl.multiple_of(holder * held_rows + part * (held_rows // 2) + row, 16)
        w_all[pl.ds(base, rows), pl.ds(to, cols)] = refs[i][...]

    def put(start, rows, qkv, low):
        qkv_t[:, pl.ds(start, rows)] = qkv
        low_t[:, pl.ds(start, rows)] = low

    multiply(x_all, w_all, down_t, up, put)


def qkv_call(n, arrays, x_from, w_from, down_t, up, seq, cols):
    rank, width = down_t.shape
    return pl.pallas_call(
        functools.partial(qkv_kernel, n, x_from, w_from),
        out_shape=[
            in_vmem((seq, width), BF),
            in_vmem((width, cols), BF),
            in_vmem((cols, seq), BF),
            in_vmem((rank, seq), BF),
        ],
        in_specs=whole_vmem(len(arrays) + 2),
        out_specs=whole_vmem(4),
        compiler_params=pltpu.CompilerParams(vmem_limit_bytes=VMEM),
        cost_estimate=SMALL,
        name="qkv",
    )(*vmem(arrays), down_t, up)


def last_qkv_kernel(tok, places, last_places, *refs):
    w_all, first_qkv, first_low, down_t, up_in, x_all, qkv_t, low_t = refs[-8:]
    at = 0
    for x in refs[:-8]:
        rows = x.shape[0]
        x_all[pl.ds(at, rows), :] = x[...]
        at += rows
    for i, place in enumerate(places):
        qkv_t[:, pl.ds(place * tok, tok)] = first_qkv[:, pl.ds(i * tok, tok)]
        low_t[:, pl.ds(place * tok, tok)] = first_low[:, pl.ds(i * tok, tok)]

    def put(start, rows, qkv, low):
        for at in range(start, start + rows, tok):
            place = last_places[at // tok] * tok
            qkv_t[:, pl.ds(place, tok)] = qkv[:, at - start : at - start + tok]
            low_t[:, pl.ds(place, tok)] = low[:, at - start : at - start + tok]

    multiply(x_all, w_all, down_t, columns(up_in, qkv_t.shape[0]), put)


def last_qkv_call(tok, places, last_places, xs, w_all, first_qkv, first_low, down_t, up):
    rank, width = down_t.shape
    cols = w_all.shape[1]
    seq = (len(places) + len(last_places)) * tok
    return pl.pallas_call(
        functools.partial(last_qkv_kernel, tok, places, last_places),
        out_shape=[
            in_vmem((len(last_places) * tok, width), BF),
            in_vmem((cols, seq), BF),
            in_vmem((rank, seq), BF),
        ],
        in_specs=whole_vmem(len(xs) + 5),
        out_specs=whole_vmem(3),
        compiler_params=pltpu.CompilerParams(vmem_limit_bytes=VMEM),
        cost_estimate=SMALL,
        name="last_qkv",
    )(*vmem(xs), *vmem([w_all, first_qkv, first_low]), down_t, up)


def gate(xs, blocks, *deps):
    xs = [x if isinstance(x, list) else [x] for x in xs]
    flat = [(i, x) for i, parts in enumerate(xs) for x in parts]
    wanted = [(i, sum(sizes[:k]), rows) for i, sizes in enumerate(blocks) for k, rows in enumerate(sizes)]

    def kernel(*refs):
        outs = refs[len(flat) + len(deps) :]
        for (i, at, rows), out in zip(wanted, outs):
            start = 0
            for (owner, _), x in zip(flat, refs):
                if owner == i:
                    low, high = max(at, start), min(at + rows, start + x.shape[0])
                    if low < high:
                        out[pl.ds(low - at, high - low), :] = x[pl.ds(low - start, high - low), :]
                    start += x.shape[0]

    return pl.pallas_call(
        kernel,
        out_shape=[in_vmem((rows, xs[i][0].shape[1]), xs[i][0].dtype) for i, _, rows in wanted],
        in_specs=whole_vmem(len(flat) + len(deps)),
        out_specs=whole_vmem(len(wanted)),
        compiler_params=pltpu.CompilerParams(vmem_limit_bytes=VMEM),
        cost_estimate=SMALL,
        name="gate",
    )(*vmem([x for _, x in flat]), *vmem(deps))


def in_vmem(shape, dtype):
    return pltpu.VMEM(shape, dtype)


def vmem(xs):
    return [pltpu.with_memory_space_constraint(x, pltpu.VMEM) for x in xs]


def hbm(xs):
    return [pltpu.with_memory_space_constraint(x, pltpu.HBM) for x in xs]


def whole_vmem(count):
    return [pl.BlockSpec(memory_space=pltpu.VMEM)] * count


def qkv_call(n, arrays, x_from, w_from, down_t, up, seq, cols):
    rank, width = down_t.shape
    return pl.pallas_call(
        functools.partial(qkv_kernel, n, x_from, w_from),
        out_shape=[
            in_vmem((seq, width), BF),
            in_vmem((width, cols), BF),
            in_vmem((cols, seq), BF),
            in_vmem((rank, seq), BF),
        ],
        in_specs=whole_vmem(len(arrays) + 2),
        out_specs=whole_vmem(4),
        compiler_params=pltpu.CompilerParams(vmem_limit_bytes=VMEM),
        cost_estimate=SMALL,
        name="qkv",
    )(*vmem(arrays), down_t, up)


def token_grads(low_grad_t, grad_t, w_all, down_t, at, rows):
    grad = grad_t[:, pl.ds(at, rows)].T
    part = contract(grad, w_all[...], 1, 1)
    return part + contract(low_grad_t[:, pl.ds(at, rows)], down_t[...], 0, 0)


def attention_kernel(heads, tok, c_from, first, outs, *refs):
    refs = list(refs)
    scale = refs.pop(0)
    cots = [[refs.pop(0) for _ in range(count)] for count, _ in c_from]
    qkv_t, low_t, w_all, down_t, up_in = (refs.pop(0) for _ in range(5))
    parts = [refs.pop(0) for _ in range(outs)]
    grad_t, pack, cot_t = refs

    cols, seq = qkv_t.shape
    up = columns(up_in, cols)
    step = math.gcd(512, seq)
    width = cot_t.shape[0]
    start = lax.rem(lax.axis_index("rows"), 2) * width
    for j, (blocks, (_, choose)) in enumerate(zip(cots, c_from)):
        if not choose:
            block = jnp.concatenate([x[...] for x in blocks], axis=0)
        elif width % 128 == 0:
            block = blocks[0][:, pl.ds(pl.multiple_of(start, 128), width)]
        else:
            block = jnp.where(start == 0, blocks[0][:, pl.ds(0, width)], blocks[0][:, pl.ds(width, width)])
        cot_t[:, pl.ds(j * tok, tok)] = block.T

    for h in range(heads):
        o = 3 * HEAD * h
        kf = qkv_t[pl.ds(o + HEAD, HEAD), :].astype(F32)
        k_inv = lax.rsqrt(jnp.sum(kf * kf, 0, keepdims=True) + EPS)
        k_unit = kf * k_inv
        k_low = k_unit.astype(BF)
        v = qkv_t[pl.ds(o + 2 * HEAD, HEAD), :]
        sc = scale[h]
        gk = gv = None
        for s in range(0, seq, step):
            qf = qkv_t[pl.ds(o, HEAD), pl.ds(s, step)].astype(F32)
            q_inv = lax.rsqrt(jnp.sum(qf * qf, 0, keepdims=True) + EPS)
            q_unit = qf * q_inv
            q_low = q_unit.astype(BF)
            g = cot_t[pl.ds(HEAD * h, HEAD), pl.ds(s, step)]
            e = jnp.exp2(contract(k_low, q_low, 0, 0) * (sc * LOG2E))
            share = 1.0 / jnp.sum(e, 0, keepdims=True)
            grad_probs = contract(v, g, 0, 0)
            delta = jnp.sum(e * grad_probs, 0, keepdims=True) * share
            attention = e * share
            grad_scores = (attention * (grad_probs - delta)).astype(BF)
            gv_s = jnp.dot(attention.astype(BF), g.T, preferred_element_type=F32)
            gk_s = jnp.dot(grad_scores, q_low.T, preferred_element_type=F32)
            gq = sc * jnp.dot(k_low, grad_scores, preferred_element_type=F32)
            gq = q_inv * (gq - q_unit * jnp.sum(q_unit * gq, 0, keepdims=True))
            grad_t[pl.ds(o, HEAD), pl.ds(s, step)] = gq.astype(BF)
            gv = gv_s if gv is None else gv + gv_s
            gk = gk_s if gk is None else gk + gk_s
        gk = sc * gk.T
        gk = k_inv * (gk - k_unit * jnp.sum(k_unit * gk, 0, keepdims=True))
        grad_t[pl.ds(o + HEAD, HEAD), :] = gk.astype(BF)
        grad_t[pl.ds(o + 2 * HEAD, HEAD), :] = gv.astype(BF).T

    rank = up.shape[0]
    pack[:, pl.ds(seq, cols)] = (0.5 * contract(low_t[...], grad_t[...], 1, 1)).astype(BF)
    low_grad_t = pack.at[:, pl.ds(0, seq)]
    low_grad_t[...] = (0.5 * jnp.dot(up, grad_t[...], preferred_element_type=F32)).astype(BF)
    for p in range(0, outs, 4):
        count = min(4, outs - p)
        part = token_grads(low_grad_t, grad_t, w_all, down_t, (first + p) * tok, count * tok)
        for i in range(count):
            out = parts[p + i]
            out[...] = part[i * tok : (i + 1) * tok].astype(out.dtype)


def attention_call(scale, cots, c_from, qkv_t, low_t, w_all, down_t, up, tok, first, dtypes):
    cols, seq = qkv_t.shape
    rank, width = down_t.shape
    smem = pl.BlockSpec(memory_space=pltpu.SMEM)
    outs = len(dtypes)
    return pl.pallas_call(
        functools.partial(attention_kernel, cols // (3 * HEAD), tok, c_from, first, outs),
        out_shape=[in_vmem((tok, width), t) for t in dtypes]
        + [in_vmem((cols, seq), BF), in_vmem((rank, seq + cols), BF)],
        in_specs=[smem] + whole_vmem(len(cots) + 5),
        out_specs=whole_vmem(outs + 2),
        scratch_shapes=[pltpu.VMEM((cols // 3, seq), BF)],
        compiler_params=pltpu.CompilerParams(vmem_limit_bytes=VMEM),
        cost_estimate=SMALL,
        name="attention_grads",
    )(scale, *vmem(cots), qkv_t, low_t, w_all, down_t, up)


def other_half(x, blocks, dep):
    half = x.shape[1] // 2
    starts = [sum(blocks[:i]) for i in range(len(blocks))]
    if half % 128:
        col = (lax.axis_index("rows") ^ 1) % 2 * half
        return [lax.dynamic_slice(x, (at, col), (rows, half)) for at, rows in zip(starts, blocks)]

    def kernel(x, dep, *outs):
        core = lax.rem(lax.axis_index("rows") ^ 1, 2)
        for at, rows, out in zip(starts, blocks, outs):
            out[...] = x[pl.ds(at, rows), pl.ds(pl.multiple_of(core * half, 128), half)]

    return pl.pallas_call(
        kernel,
        out_shape=[in_vmem((rows, half), x.dtype) for rows in blocks],
        in_specs=whole_vmem(2),
        out_specs=whole_vmem(len(blocks)),
        compiler_params=pltpu.CompilerParams(vmem_limit_bytes=VMEM),
        cost_estimate=SMALL,
        name="other_half",
    )(*vmem([x, dep]))


def add(a, b):
    def kernel(a, b, out):
        out[...] = (a[...] + b[...].astype(F32)).astype(BF)

    return pl.pallas_call(
        kernel,
        out_shape=in_vmem(a.shape, BF),
        in_specs=whole_vmem(2),
        out_specs=whole_vmem(1)[0],
        compiler_params=pltpu.CompilerParams(vmem_limit_bytes=VMEM),
        cost_estimate=SMALL,
        name="add",
    )(*vmem([a, b]))


def own_kernel(deps, grad_t, pack, w_all, down_t, *refs):
    mine, rest = refs[deps], refs[deps + 1 :]
    tok = mine.shape[0]
    part = token_grads(pack, grad_t, w_all, down_t, 0, 2 * tok)
    mine[...] = part[:tok]
    part = part[tok:].astype(BF)
    at = 0
    for out in rest:
        out[...] = part[at : at + out.shape[0]]
        at += out.shape[0]


def own_call(grad_t, pack, w_all, down_t, tok, blocks, deps):
    width = down_t.shape[1]
    return pl.pallas_call(
        functools.partial(own_kernel, len(deps)),
        out_shape=[in_vmem((tok, width), F32)] + [in_vmem((rows, width), BF) for rows in blocks],
        in_specs=whole_vmem(4 + len(deps)),
        out_specs=whole_vmem(1 + len(blocks)),
        compiler_params=pltpu.CompilerParams(vmem_limit_bytes=VMEM),
        cost_estimate=SMALL,
        name="own_grads",
    )(grad_t, pack, w_all, down_t, *vmem(deps))


def adapter_kernel(tok, places, *refs):
    packs, (first_x, last_x, down_grad_t, up_grad) = refs[:-4], refs[-4:]
    r = lax.axis_index("rows")
    total = None
    for j, pack in enumerate(packs):
        blocks = [pack[:, pl.ds((q ^ j) * tok, tok)] for q in range(len(packs))]
        term = jnp.concatenate(blocks, axis=1).astype(F32)
        total = term if total is None else total + term
    total = total.astype(BF)
    grad = None
    for x, held in zip((first_x, last_x), places):
        part = jnp.concatenate([total[:, p * tok : (p + 1) * tok] for p in held], axis=1)
        term = jnp.dot(part, x[...], preferred_element_type=F32)
        grad = term if grad is None else grad + term
    down_grad_t[...] = grad
    cols = up_grad.shape[1] // len(packs)
    for j, pack in enumerate(packs):
        if cols % 128 == 0:
            up_grad[:, pl.ds(pl.multiple_of((r ^ j) * cols, 128), cols)] = pack[:, pl.ds(len(packs) * tok, cols)].astype(F32)


def adapter_call(packs, first_x, last_x, places, rank, all_cols, tok):
    down_grad_t, up_grad = pl.pallas_call(
        functools.partial(adapter_kernel, tok, places),
        out_shape=[
            jax.ShapeDtypeStruct((rank, first_x.shape[1]), F32),
            jax.ShapeDtypeStruct((rank, all_cols), F32),
        ],
        in_specs=whole_vmem(len(packs) + 2),
        out_specs=whole_vmem(2),
        compiler_params=pltpu.CompilerParams(vmem_limit_bytes=VMEM),
        cost_estimate=SMALL,
        name="adapter_grads",
    )(*vmem(packs), *vmem([first_x, last_x]))
    cols = all_cols // len(packs)
    if cols % 128:
        for j, pack in enumerate(packs):
            up_grad = lax.dynamic_update_slice(up_grad, pack[:, len(packs) * tok :].astype(F32), (0, (lax.axis_index("rows") ^ j) * cols))
    return down_grad_t, up_grad


def scale_kernel(tokens, gain, inv_rms, mine, *refs):
    blocks, (total, token_gain, scale, slope) = refs[:-4], refs[-4:]
    at = 0
    for block in blocks:
        rows = pl.ds(at, block.shape[0])
        total[rows, :] = mine[rows, :] + block[...].astype(F32)
        at += block.shape[0]
    x = tokens[...].astype(F32)
    inv = inv_rms[...]
    token_gain[...] = x * gain[...]
    scale[...] = inv * gain[...]
    slope[...] = x * (inv * inv * inv * (1.0 / x.shape[1]))


def scale_call(tokens, gain, inv_rms, mine, blocks):
    return pl.pallas_call(
        scale_kernel,
        out_shape=[in_vmem(tokens.shape, F32)] * 4,
        in_specs=whole_vmem(4 + len(blocks)),
        out_specs=whole_vmem(4),
        compiler_params=pltpu.CompilerParams(vmem_limit_bytes=VMEM),
        cost_estimate=SMALL,
        name="scale",
    )(tokens, gain, inv_rms, mine, *vmem(blocks))


def final_kernel(total, token_gain, scale, slope, *refs):
    terms, (out, made, sems) = refs[:-3], refs[-3:]
    count = sems.shape[0]
    rows = made.shape[0] // count
    copies = []
    for i in range(count):
        block = pl.ds(i * rows, rows)
        grad = total[block, :]
        for x in terms:
            grad = grad + x[block, :].astype(F32)
        moment = jnp.sum(grad * token_gain[block, :], -1, keepdims=True)
        made[block, :] = (grad * scale[block, :] - slope[block, :] * moment).astype(BF)
        copies.append(pltpu.make_async_copy(made.at[block], out.at[block], sems.at[i]))
        copies[-1].start()
    for c in copies:
        c.wait()


def final_call(held, terms):
    shape = held[0].shape
    count = 4 if shape[0] % 64 == 0 else 1
    return pl.pallas_call(
        final_kernel,
        out_shape=jax.ShapeDtypeStruct(shape, BF),
        in_specs=whole_vmem(4 + len(terms)),
        out_specs=pl.BlockSpec(memory_space=pltpu.HBM),
        scratch_shapes=[pltpu.VMEM(shape, BF), pltpu.SemaphoreType.DMA((count,))],
        compiler_params=pltpu.CompilerParams(vmem_limit_bytes=VMEM),
        cost_estimate=SMALL,
        name="input_grads",
    )(*vmem(held), *vmem(terms))


def prepare_kernel(chips, head_cols, sizes, features, gain_map, tokens, core_tokens, cot, *refs):
    count, outs = len(sizes), len(sizes) + len(chips)
    normed, core_normed, gain, inv_rms = refs[count : count + 4]
    cut = refs[count + 4 : count + 4 + outs]
    map_in, tokens_in, core_in, sems = refs[count + 4 + outs :]
    r = lax.axis_index("rows")
    copies = [(tokens, tokens_in), (core_tokens, core_in), (gain_map, map_in)]
    for x, size, out in zip(refs, sizes, cut):
        copies.append((x.at[:, pl.ds(pl.multiple_of(r * size, 128), size)] if size else x, out))
    for j, out in zip(chips, cut[count:]):
        chip = lax.div(r ^ j, 2) * (2 * head_cols)
        copies.append((cot.at[:, pl.ds(pl.multiple_of(chip, 128), 2 * head_cols)], out))
    copies = [pltpu.make_async_copy(a, b, sems.at[i]) for i, (a, b) in enumerate(copies)]
    for c in copies:
        c.start()
    half = features.shape[1]
    col = features[...].T
    for c in copies[:3]:
        c.wait()
    total = jnp.sum(col[:, :1] * map_in[:half, :], 0, keepdims=True)
    total = total + jnp.sum(col[:, 1:] * map_in[half:, :], 0, keepdims=True)
    gain[...] = 1.0 + total
    for x, out in ((tokens_in, normed), (core_in, core_normed)):
        x = x[...].astype(F32)
        inv = lax.rsqrt(jnp.mean(x * x, -1, keepdims=True) + EPS)
        if out is normed:
            inv_rms[...] = inv
        out[...] = (x * inv * gain[...]).astype(BF)
    for c in copies[3:]:
        c.wait()


def prepare_call(features, gain_map, tokens, core_tokens, cot, chips, head_cols, arrays):
    tok, width = tokens.shape
    shapes = [((tok, width), BF), ((tok, width), BF), ((1, width), F32), ((tok, 1), F32)]
    shapes += [((x.shape[0], size or x.shape[1]), BF) for x, size in arrays]
    shapes += [((tok, 2 * head_cols), BF)] * len(chips)
    copies = 3 + len(arrays) + len(chips)
    return pl.pallas_call(
        functools.partial(prepare_kernel, chips, head_cols, [size for _, size in arrays]),
        out_shape=[in_vmem(*shape) for shape in shapes],
        in_specs=whole_vmem(1) + [pl.BlockSpec(memory_space=pl.ANY)] * (4 + len(arrays)),
        out_specs=whole_vmem(len(shapes)),
        scratch_shapes=[
            pltpu.VMEM(gain_map.shape, F32),
            pltpu.VMEM((tok, width), BF),
            pltpu.VMEM((tok, width), BF),
            pltpu.SemaphoreType.DMA((copies,)),
        ],
        compiler_params=pltpu.CompilerParams(vmem_limit_bytes=VMEM),
        cost_estimate=SMALL,
        name="prepare",
    )(features, gain_map, tokens, core_tokens, cot, *[x for x, _ in arrays])


def per_device(
    mesh_shape,
    tokens,
    timestep,
    timestep_gain_map,
    query_key_value_weight,
    adapter_down_weight,
    adapter_up_weight,
    head_score_scale,
    heads_output_grad,
):
    dp, n = mesh_shape
    axes = ("dp", "rows")
    r, d = lax.axis_index("rows"), lax.axis_index("dp")

    def send(x, target):
        perm = []
        for a in range(dp):
            for b in range(n):
                a2, b2 = target(a, b)
                perm.append((a * n + b, a2 * n + b2))
        return lax.ppermute(x, axes, perm)

    def to_row(x, j):
        return send(x, lambda a, b: (a, b ^ j))

    tok, width = tokens.shape
    weight, cot_all = query_key_value_weight, heads_output_grad
    k_rows = weight.shape[0]
    cols = weight.shape[1] // n
    head_cols = cot_all.shape[1] // n
    chips = list(range(2, n, 2))

    pair_cols = cols // 2 if cols % 256 == 0 else cols
    half = k_rows // 2
    pair, quad = [], []
    for j in chips:
        if pair_cols < cols:
            start = (d % 4 // 2 * half, (r ^ (j + d % 2)) * cols + pair_cols)
            x = lax.dynamic_slice(weight, start, (half, cols - pair_cols))
            quad.append(send(x, lambda a, b, j=j: (a, b ^ (j + a % 2))))
        x = lax.dynamic_slice(weight, (0, (r ^ (j + d // 2 % 2)) * cols), (k_rows, pair_cols))
        pair.append(send(x, lambda a, b, j=j: (a, b ^ (j + a // 2 % 2))))

    core_weight, core_tokens, core_cot = (to_row(x, 1) for x in (weight, tokens, cot_all))

    def mine(x, size):
        if size % 128 == 0 and x is weight:
            return hbm([x])[0], size
        return (x, size) if size % 128 == 0 else (lax.dynamic_slice(x, (0, r * size), (x.shape[0], size)), 0)

    own_map, own_tokens, own_cot = hbm([timestep_gain_map, tokens, cot_all])
    normed, core_normed, gain, inv_rms, own_w, core_w, own_cot, core_cot, *chip_cot = prepare_call(
        time_features(timestep), own_map, own_tokens, core_tokens, own_cot, chips, head_cols,
        [mine(weight, cols), mine(core_weight, cols), mine(cot_all, head_cols), mine(core_cot, head_cols)],
    )
    arrays = [own_w, core_w, normed, core_normed]
    w_from, x_from = [(0, 0, 0, 1, 0, 0), (1, 0, 1, 1, 0, 0)], [(2, tok), (3, tok)]
    def exchange(x, other):
        return send(x, lambda a, b: (a ^ other, b))

    early = []
    for j, x in zip(chips, quad):
        held = [x, exchange(x, 1), exchange(x, 2)]
        for other, x in enumerate(held):
            w_from.append((len(arrays), pair_cols, j, 4, other, 0))
            arrays.append(x)
        early.append(held[1])
        cut = (half * 7 // 8, half // 8)
        for at, x in zip((0, cut[0]), gate([held[2]], [cut])):
            early.append(exchange(x, 1))
            w_from.append((len(arrays), pair_cols, j, 4, 3, at))
            arrays.append(early[-1])
    for j, x in zip(chips, pair):
        w_from += [(len(arrays), 0, j, 2, 0, 0), (len(arrays) + 1, 0, j, 2, 1, 0)]
        arrays += [x, exchange(x, 2)]

    relay_rows = (tok * 5 // 8, tok * 3 // 8) if tok % 128 == 0 else (tok,)
    chip_normed = [to_row(normed, j) for j in chips]
    later = list(gate(chip_normed, [relay_rows] * len(chips), *early))
    for x in chip_normed:
        x_from.append((len(arrays), x.shape[0]))
        arrays.append(x)

    rank = adapter_up_weight.shape[0]
    down_t = adapter_down_weight.T
    up = adapter_up_weight
    if cols % 128:
        up = lax.dynamic_slice(up, (0, r * cols), (rank, cols))
    places, last_places = (0, 1, *chips), tuple(j + 1 for j in chips)
    first_x, w_all, first_qkv, first_low = qkv_call(
        n, arrays, tuple(x_from), tuple(w_from), down_t, up, len(places) * tok, cols
    )
    last_x, qkv_t, low_t = last_qkv_call(
        tok, places, last_places, [to_row(x, 1) for x in later], w_all, first_qkv, first_low, down_t, up
    )

    cots, c_from = [own_cot, core_cot], [(1, False), (1, False)]
    blocks = (tok * 7 // 8, tok // 8) if tok % 128 == 0 else (tok,)
    for j, x in zip(chips, chip_cot):
        x = to_row(x, j)
        c_from += [(1, True), (len(blocks), False)]
        cots += [x] + [to_row(y, 1) for y in other_half(x, blocks, first_low)]

    *others, grad_t, pack = attention_call(
        head_score_scale, cots, tuple(c_from), qkv_t, low_t, w_all, down_t, up, tok, 2, (F32, BF) * len(chips)
    )

    totals = [add(others[2 * i], to_row(others[2 * i + 1], 1)) for i in range(len(chips))]
    sums = [to_row(x, j) for x, j in zip(totals, chips)]
    packs = {0: pack, 1: to_row(pack, 1)}
    for j in chips:
        packs[j] = to_row(pack, j)
    blocks = (tok * 7 // 8, tok // 8) if tok % 128 == 0 else (tok,)
    mine, *core_part = own_call(grad_t, pack, w_all, down_t, tok, blocks, totals + [packs[j] for j in chips])
    core_part = [to_row(x, 1) for x in core_part]

    for j in chips:
        packs[j ^ 1] = to_row(packs[j], 1)
    down_grad_t, up_grad = adapter_call(
        [packs[j] for j in range(n)], first_x, last_x, (places, last_places), rank, n * cols, tok
    )

    input_grad = final_call(scale_call(tokens, gain, inv_rms, mine, core_part), sums)
    return (input_grad, down_grad_t.T, up_grad)


def solution(mesh):
    in_specs = (
        P(("dp", "rows"), None),
        P("dp"),
        P(),
        P("rows", None),
        P(),
        P(),
        P("rows"),
        P(("dp", "rows"), None),
    )
    out_specs = (P(("dp", "rows"), None), P("dp", None), P("dp", None))
    shape = (mesh.shape["dp"], mesh.shape["rows"])
    return jax.shard_map(
        functools.partial(per_device, shape), mesh=mesh, in_specs=in_specs, out_specs=out_specs, check_vma=False
    )
```

```python
import functools
import math

import jax
import jax.numpy as jnp
from jax import lax
from jax.experimental import pallas as pl
from jax.experimental.pallas import tpu as pltpu
from jax.sharding import PartitionSpec as P

HEAD = 64
EMB = 256
EPS = 1e-06
LOG2E = 1.4426950408889634
BF = jnp.bfloat16
F32 = jnp.float32
VMEM = 16 * 1024 * 1024
SMALL = pl.CostEstimate(flops=1, bytes_accessed=1, transcendentals=0)


def time_features(timestep):
    half_emb = EMB // 2
    frequency = jnp.exp(-math.log(10000.0) * jnp.arange(half_emb, dtype=F32) / half_emb)
    phases = timestep.astype(F32)[0] * frequency
    return jnp.stack([jnp.cos(phases), jnp.sin(phases)])


def contract(a, b, a_dim, b_dim):
    return lax.dot_general(a, b, (((a_dim,), (b_dim,)), ((), ())), preferred_element_type=F32)


def columns(x, size):
    if x.shape[1] == size:
        return x[...]
    return x[:, pl.ds(pl.multiple_of(lax.axis_index("rows") * size, 128), size)]


def multiply(x_all, w_all, down_t, up, put):
    seq = x_all.shape[0]
    step = math.gcd(512, seq) if seq > 512 else seq
    for s in range(0, seq, step):
        x = x_all[pl.ds(s, step), :]
        low = contract(x, down_t[...], 1, 1).astype(BF)
        qkv = jnp.dot(x, w_all[...], preferred_element_type=F32)
        qkv = qkv + 0.5 * jnp.dot(low, up, preferred_element_type=F32)
        put(s, step, qkv.astype(BF).T, low.T)


def qkv_kernel(n, x_from, w_from, *refs):
    down_t, up_in = refs[-6:-4]
    r, d = lax.axis_index("rows"), lax.axis_index("dp")
    up = columns(up_in, refs[-2].shape[0])
    x_all, w_all, qkv_t, low_t = refs[-4:]
    at = 0
    for i, rows in x_from:
        x_all[pl.ds(at, rows), :] = refs[i][...]
        at += rows
    for i, to, j, group, other, row in w_from:
        rows, cols = refs[i].shape
        holder, part = r ^ j, 0
        if group == 2:
            holder = r ^ (j + (lax.rem(lax.div(d, 2), 2) ^ other))
        elif group == 4:
            share = lax.rem(d, 4) ^ other
            holder, part = r ^ (j + lax.rem(share, 2)), lax.div(share, 2)
        held_rows = w_all.shape[0] // n
        base = pl.multiple_of(holder * held_rows + part * (held_rows // 2) + row, 16)
        w_all[pl.ds(base, rows), pl.ds(to, cols)] = refs[i][...]

    def put(start, rows, qkv, low):
        qkv_t[:, pl.ds(start, rows)] = qkv
        low_t[:, pl.ds(start, rows)] = low

    multiply(x_all, w_all, down_t, up, put)


def qkv_call(n, arrays, x_from, w_from, down_t, up, seq, cols):
    rank, width = down_t.shape
    return pl.pallas_call(
        functools.partial(qkv_kernel, n, x_from, w_from),
        out_shape=[
            in_vmem((seq, width), BF),
            in_vmem((width, cols), BF),
            in_vmem((cols, seq), BF),
            in_vmem((rank, seq), BF),
        ],
        in_specs=whole_vmem(len(arrays) + 2),
        out_specs=whole_vmem(4),
        compiler_params=pltpu.CompilerParams(vmem_limit_bytes=VMEM),
        cost_estimate=SMALL,
        name="qkv",
    )(*vmem(arrays), down_t, up)


def last_qkv_kernel(tok, places, last_places, *refs):
    w_all, first_qkv, first_low, down_t, up_in, x_all, qkv_t, low_t = refs[-8:]
    at = 0
    for x in refs[:-8]:
        rows = x.shape[0]
        x_all[pl.ds(at, rows), :] = x[...]
        at += rows
    for i, place in enumerate(places):
        qkv_t[:, pl.ds(place * tok, tok)] = first_qkv[:, pl.ds(i * tok, tok)]
        low_t[:, pl.ds(place * tok, tok)] = first_low[:, pl.ds(i * tok, tok)]

    def put(start, rows, qkv, low):
        for at in range(start, start + rows, tok):
            place = last_places[at // tok] * tok
            qkv_t[:, pl.ds(place, tok)] = qkv[:, at - start : at - start + tok]
            low_t[:, pl.ds(place, tok)] = low[:, at - start : at - start + tok]

    multiply(x_all, w_all, down_t, columns(up_in, qkv_t.shape[0]), put)


def last_qkv_call(tok, places, last_places, xs, w_all, first_qkv, first_low, down_t, up):
    rank, width = down_t.shape
    cols = w_all.shape[1]
    seq = (len(places) + len(last_places)) * tok
    return pl.pallas_call(
        functools.partial(last_qkv_kernel, tok, places, last_places),
        out_shape=[
            in_vmem((len(last_places) * tok, width), BF),
            in_vmem((cols, seq), BF),
            in_vmem((rank, seq), BF),
        ],
        in_specs=whole_vmem(len(xs) + 5),
        out_specs=whole_vmem(3),
        compiler_params=pltpu.CompilerParams(vmem_limit_bytes=VMEM),
        cost_estimate=SMALL,
        name="last_qkv",
    )(*vmem(xs), *vmem([w_all, first_qkv, first_low]), down_t, up)


def gate(xs, blocks, *deps):
    xs = [x if isinstance(x, list) else [x] for x in xs]
    flat = [(i, x) for i, parts in enumerate(xs) for x in parts]
    wanted = [(i, sum(sizes[:k]), rows) for i, sizes in enumerate(blocks) for k, rows in enumerate(sizes)]

    def kernel(*refs):
        outs = refs[len(flat) + len(deps) :]
        for (i, at, rows), out in zip(wanted, outs):
            start = 0
            for (owner, _), x in zip(flat, refs):
                if owner == i:
                    low, high = max(at, start), min(at + rows, start + x.shape[0])
                    if low < high:
                        out[pl.ds(low - at, high - low), :] = x[pl.ds(low - start, high - low), :]
                    start += x.shape[0]

    return pl.pallas_call(
        kernel,
        out_shape=[in_vmem((rows, xs[i][0].shape[1]), xs[i][0].dtype) for i, _, rows in wanted],
        in_specs=whole_vmem(len(flat) + len(deps)),
        out_specs=whole_vmem(len(wanted)),
        compiler_params=pltpu.CompilerParams(vmem_limit_bytes=VMEM),
        cost_estimate=SMALL,
        name="gate",
    )(*vmem([x for _, x in flat]), *vmem(deps))


def in_vmem(shape, dtype):
    return pltpu.VMEM(shape, dtype)


def vmem(xs):
    return [pltpu.with_memory_space_constraint(x, pltpu.VMEM) for x in xs]


def hbm(xs):
    return [pltpu.with_memory_space_constraint(x, pltpu.HBM) for x in xs]


def whole_vmem(count):
    return [pl.BlockSpec(memory_space=pltpu.VMEM)] * count


def qkv_call(n, arrays, x_from, w_from, down_t, up, seq, cols):
    rank, width = down_t.shape
    return pl.pallas_call(
        functools.partial(qkv_kernel, n, x_from, w_from),
        out_shape=[
            in_vmem((seq, width), BF),
            in_vmem((width, cols), BF),
            in_vmem((cols, seq), BF),
            in_vmem((rank, seq), BF),
        ],
        in_specs=whole_vmem(len(arrays) + 2),
        out_specs=whole_vmem(4),
        compiler_params=pltpu.CompilerParams(vmem_limit_bytes=VMEM),
        cost_estimate=SMALL,
        name="qkv",
    )(*vmem(arrays), down_t, up)


def token_grads(low_grad_t, grad_t, w_all, down_t, at, rows):
    grad = grad_t[:, pl.ds(at, rows)].T
    part = contract(grad, w_all[...], 1, 1)
    return part + contract(low_grad_t[:, pl.ds(at, rows)], down_t[...], 0, 0)


def attention_kernel(heads, tok, c_from, first, outs, *refs):
    refs = list(refs)
    scale = refs.pop(0)
    cots = [[refs.pop(0) for _ in range(count)] for count, _ in c_from]
    qkv_t, low_t, w_all, down_t, up_in = (refs.pop(0) for _ in range(5))
    parts = [refs.pop(0) for _ in range(outs)]
    grad_t, pack, cot_t = refs

    cols, seq = qkv_t.shape
    up = columns(up_in, cols)
    step = math.gcd(512, seq)
    width = cot_t.shape[0]
    start = lax.rem(lax.axis_index("rows"), 2) * width
    for j, (blocks, (_, choose)) in enumerate(zip(cots, c_from)):
        if not choose:
            block = jnp.concatenate([x[...] for x in blocks], axis=0)
        elif width % 128 == 0:
            block = blocks[0][:, pl.ds(pl.multiple_of(start, 128), width)]
        else:
            block = jnp.where(start == 0, blocks[0][:, pl.ds(0, width)], blocks[0][:, pl.ds(width, width)])
        cot_t[:, pl.ds(j * tok, tok)] = block.T

    for h in range(heads):
        o = 3 * HEAD * h
        kf = qkv_t[pl.ds(o + HEAD, HEAD), :].astype(F32)
        k_inv = lax.rsqrt(jnp.sum(kf * kf, 0, keepdims=True) + EPS)
        k_unit = kf * k_inv
        k_low = k_unit.astype(BF)
        v = qkv_t[pl.ds(o + 2 * HEAD, HEAD), :]
        sc = scale[h]
        gk = gv = None
        for s in range(0, seq, step):
            qf = qkv_t[pl.ds(o, HEAD), pl.ds(s, step)].astype(F32)
            q_inv = lax.rsqrt(jnp.sum(qf * qf, 0, keepdims=True) + EPS)
            q_unit = qf * q_inv
            q_low = q_unit.astype(BF)
            g = cot_t[pl.ds(HEAD * h, HEAD), pl.ds(s, step)]
            e = jnp.exp2(contract(k_low, q_low, 0, 0) * (sc * LOG2E))
            share = 1.0 / jnp.sum(e, 0, keepdims=True)
            grad_probs = contract(v, g, 0, 0)
            delta = jnp.sum(e * grad_probs, 0, keepdims=True) * share
            attention = e * share
            grad_scores = (attention * (grad_probs - delta)).astype(BF)
            gv_s = jnp.dot(attention.astype(BF), g.T, preferred_element_type=F32)
            gk_s = jnp.dot(grad_scores, q_low.T, preferred_element_type=F32)
            gq = sc * jnp.dot(k_low, grad_scores, preferred_element_type=F32)
            gq = q_inv * (gq - q_unit * jnp.sum(q_unit * gq, 0, keepdims=True))
            grad_t[pl.ds(o, HEAD), pl.ds(s, step)] = gq.astype(BF)
            gv = gv_s if gv is None else gv + gv_s
            gk = gk_s if gk is None else gk + gk_s
        gk = sc * gk.T
        gk = k_inv * (gk - k_unit * jnp.sum(k_unit * gk, 0, keepdims=True))
        grad_t[pl.ds(o + HEAD, HEAD), :] = gk.astype(BF)
        grad_t[pl.ds(o + 2 * HEAD, HEAD), :] = gv.astype(BF).T

    rank = up.shape[0]
    pack[:, pl.ds(seq, cols)] = (0.5 * contract(low_t[...], grad_t[...], 1, 1)).astype(BF)
    low_grad_t = pack.at[:, pl.ds(0, seq)]
    low_grad_t[...] = (0.5 * jnp.dot(up, grad_t[...], preferred_element_type=F32)).astype(BF)
    for p in range(0, outs, 4):
        count = min(4, outs - p)
        part = token_grads(low_grad_t, grad_t, w_all, down_t, (first + p) * tok, count * tok)
        for i in range(count):
            out = parts[p + i]
            out[...] = part[i * tok : (i + 1) * tok].astype(out.dtype)


def attention_call(scale, cots, c_from, qkv_t, low_t, w_all, down_t, up, tok, first, dtypes):
    cols, seq = qkv_t.shape
    rank, width = down_t.shape
    smem = pl.BlockSpec(memory_space=pltpu.SMEM)
    outs = len(dtypes)
    return pl.pallas_call(
        functools.partial(attention_kernel, cols // (3 * HEAD), tok, c_from, first, outs),
        out_shape=[in_vmem((tok, width), t) for t in dtypes]
        + [in_vmem((cols, seq), BF), in_vmem((rank, seq + cols), BF)],
        in_specs=[smem] + whole_vmem(len(cots) + 5),
        out_specs=whole_vmem(outs + 2),
        scratch_shapes=[pltpu.VMEM((cols // 3, seq), BF)],
        compiler_params=pltpu.CompilerParams(vmem_limit_bytes=VMEM),
        cost_estimate=SMALL,
        name="attention_grads",
    )(scale, *vmem(cots), qkv_t, low_t, w_all, down_t, up)


def other_half(x, blocks, dep):
    half = x.shape[1] // 2
    starts = [sum(blocks[:i]) for i in range(len(blocks))]
    if half % 128:
        col = (lax.axis_index("rows") ^ 1) % 2 * half
        return [lax.dynamic_slice(x, (at, col), (rows, half)) for at, rows in zip(starts, blocks)]

    def kernel(x, dep, *outs):
        core = lax.rem(lax.axis_index("rows") ^ 1, 2)
        for at, rows, out in zip(starts, blocks, outs):
            out[...] = x[pl.ds(at, rows), pl.ds(pl.multiple_of(core * half, 128), half)]

    return pl.pallas_call(
        kernel,
        out_shape=[in_vmem((rows, half), x.dtype) for rows in blocks],
        in_specs=whole_vmem(2),
        out_specs=whole_vmem(len(blocks)),
        compiler_params=pltpu.CompilerParams(vmem_limit_bytes=VMEM),
        cost_estimate=SMALL,
        name="other_half",
    )(*vmem([x, dep]))


def add(a, b):
    def kernel(a, b, out):
        out[...] = (a[...] + b[...].astype(F32)).astype(BF)

    return pl.pallas_call(
        kernel,
        out_shape=in_vmem(a.shape, BF),
        in_specs=whole_vmem(2),
        out_specs=whole_vmem(1)[0],
        compiler_params=pltpu.CompilerParams(vmem_limit_bytes=VMEM),
        cost_estimate=SMALL,
        name="add",
    )(*vmem([a, b]))


def own_kernel(deps, grad_t, pack, w_all, down_t, *refs):
    mine, rest = refs[deps], refs[deps + 1 :]
    tok = mine.shape[0]
    part = token_grads(pack, grad_t, w_all, down_t, 0, 2 * tok)
    mine[...] = part[:tok]
    part = part[tok:].astype(BF)
    at = 0
    for out in rest:
        out[...] = part[at : at + out.shape[0]]
        at += out.shape[0]


def own_call(grad_t, pack, w_all, down_t, tok, blocks, deps):
    width = down_t.shape[1]
    return pl.pallas_call(
        functools.partial(own_kernel, len(deps)),
        out_shape=[in_vmem((tok, width), F32)] + [in_vmem((rows, width), BF) for rows in blocks],
        in_specs=whole_vmem(4 + len(deps)),
        out_specs=whole_vmem(1 + len(blocks)),
        compiler_params=pltpu.CompilerParams(vmem_limit_bytes=VMEM),
        cost_estimate=SMALL,
        name="own_grads",
    )(grad_t, pack, w_all, down_t, *vmem(deps))


def adapter_kernel(tok, places, *refs):
    packs, (first_x, last_x, down_grad_t, up_grad) = refs[:-4], refs[-4:]
    r = lax.axis_index("rows")
    total = None
    for j, pack in enumerate(packs):
        blocks = [pack[:, pl.ds((q ^ j) * tok, tok)] for q in range(len(packs))]
        term = jnp.concatenate(blocks, axis=1).astype(F32)
        total = term if total is None else total + term
    total = total.astype(BF)
    grad = None
    for x, held in zip((first_x, last_x), places):
        part = jnp.concatenate([total[:, p * tok : (p + 1) * tok] for p in held], axis=1)
        term = jnp.dot(part, x[...], preferred_element_type=F32)
        grad = term if grad is None else grad + term
    down_grad_t[...] = grad
    cols = up_grad.shape[1] // len(packs)
    for j, pack in enumerate(packs):
        if cols % 128 == 0:
            up_grad[:, pl.ds(pl.multiple_of((r ^ j) * cols, 128), cols)] = pack[:, pl.ds(len(packs) * tok, cols)].astype(F32)


def adapter_call(packs, first_x, last_x, places, rank, all_cols, tok):
    down_grad_t, up_grad = pl.pallas_call(
        functools.partial(adapter_kernel, tok, places),
        out_shape=[
            jax.ShapeDtypeStruct((rank, first_x.shape[1]), F32),
            jax.ShapeDtypeStruct((rank, all_cols), F32),
        ],
        in_specs=whole_vmem(len(packs) + 2),
        out_specs=whole_vmem(2),
        compiler_params=pltpu.CompilerParams(vmem_limit_bytes=VMEM),
        cost_estimate=SMALL,
        name="adapter_grads",
    )(*vmem(packs), *vmem([first_x, last_x]))
    cols = all_cols // len(packs)
    if cols % 128:
        for j, pack in enumerate(packs):
            up_grad = lax.dynamic_update_slice(up_grad, pack[:, len(packs) * tok :].astype(F32), (0, (lax.axis_index("rows") ^ j) * cols))
    return down_grad_t, up_grad


def scale_kernel(tokens, gain, inv_rms, mine, *refs):
    blocks, (total, token_gain, scale, slope) = refs[:-4], refs[-4:]
    at = 0
    for block in blocks:
        rows = pl.ds(at, block.shape[0])
        total[rows, :] = mine[rows, :] + block[...].astype(F32)
        at += block.shape[0]
    x = tokens[...].astype(F32)
    inv = inv_rms[...]
    token_gain[...] = x * gain[...]
    scale[...] = inv * gain[...]
    slope[...] = x * (inv * inv * inv * (1.0 / x.shape[1]))


def scale_call(tokens, gain, inv_rms, mine, blocks):
    return pl.pallas_call(
        scale_kernel,
        out_shape=[in_vmem(tokens.shape, F32)] * 4,
        in_specs=whole_vmem(4 + len(blocks)),
        out_specs=whole_vmem(4),
        compiler_params=pltpu.CompilerParams(vmem_limit_bytes=VMEM),
        cost_estimate=SMALL,
        name="scale",
    )(tokens, gain, inv_rms, mine, *vmem(blocks))


def final_kernel(total, token_gain, scale, slope, *refs):
    terms, (out, made, sems) = refs[:-3], refs[-3:]
    count = sems.shape[0]
    rows = made.shape[0] // count
    copies = []
    for i in range(count):
        block = pl.ds(i * rows, rows)
        grad = total[block, :]
        for x in terms:
            grad = grad + x[block, :].astype(F32)
        moment = jnp.sum(grad * token_gain[block, :], -1, keepdims=True)
        made[block, :] = (grad * scale[block, :] - slope[block, :] * moment).astype(BF)
        copies.append(pltpu.make_async_copy(made.at[block], out.at[block], sems.at[i]))
        copies[-1].start()
    for c in copies:
        c.wait()


def final_call(held, terms):
    shape = held[0].shape
    count = 4 if shape[0] % 64 == 0 else 1
    return pl.pallas_call(
        final_kernel,
        out_shape=jax.ShapeDtypeStruct(shape, BF),
        in_specs=whole_vmem(4 + len(terms)),
        out_specs=pl.BlockSpec(memory_space=pltpu.HBM),
        scratch_shapes=[pltpu.VMEM(shape, BF), pltpu.SemaphoreType.DMA((count,))],
        compiler_params=pltpu.CompilerParams(vmem_limit_bytes=VMEM),
        cost_estimate=SMALL,
        name="input_grads",
    )(*vmem(held), *vmem(terms))


def prepare_kernel(chips, head_cols, sizes, features, gain_map, tokens, core_tokens, cot, *refs):
    count, outs = len(sizes), len(sizes) + len(chips)
    normed, core_normed, gain, inv_rms = refs[count : count + 4]
    cut = refs[count + 4 : count + 4 + outs]
    map_in, tokens_in, core_in, sems = refs[count + 4 + outs :]
    r = lax.axis_index("rows")
    copies = [(tokens, tokens_in), (core_tokens, core_in), (gain_map, map_in)]
    for x, size, out in zip(refs, sizes, cut):
        copies.append((x.at[:, pl.ds(pl.multiple_of(r * size, 128), size)] if size else x, out))
    for j, out in zip(chips, cut[count:]):
        chip = lax.div(r ^ j, 2) * (2 * head_cols)
        copies.append((cot.at[:, pl.ds(pl.multiple_of(chip, 128), 2 * head_cols)], out))
    copies = [pltpu.make_async_copy(a, b, sems.at[i]) for i, (a, b) in enumerate(copies)]
    for c in copies:
        c.start()
    half = features.shape[1]
    col = features[...].T
    for c in copies[:3]:
        c.wait()
    total = jnp.sum(col[:, :1] * map_in[:half, :], 0, keepdims=True)
    total = total + jnp.sum(col[:, 1:] * map_in[half:, :], 0, keepdims=True)
    gain[...] = 1.0 + total
    for x, out in ((tokens_in, normed), (core_in, core_normed)):
        x = x[...].astype(F32)
        inv = lax.rsqrt(jnp.mean(x * x, -1, keepdims=True) + EPS)
        if out is normed:
            inv_rms[...] = inv
        out[...] = (x * inv * gain[...]).astype(BF)
    for c in copies[3:]:
        c.wait()


def prepare_call(features, gain_map, tokens, core_tokens, cot, chips, head_cols, arrays):
    tok, width = tokens.shape
    shapes = [((tok, width), BF), ((tok, width), BF), ((1, width), F32), ((tok, 1), F32)]
    shapes += [((x.shape[0], size or x.shape[1]), BF) for x, size in arrays]
    shapes += [((tok, 2 * head_cols), BF)] * len(chips)
    copies = 3 + len(arrays) + len(chips)
    return pl.pallas_call(
        functools.partial(prepare_kernel, chips, head_cols, [size for _, size in arrays]),
        out_shape=[in_vmem(*shape) for shape in shapes],
        in_specs=whole_vmem(1) + [pl.BlockSpec(memory_space=pl.ANY)] * (4 + len(arrays)),
        out_specs=whole_vmem(len(shapes)),
        scratch_shapes=[
            pltpu.VMEM(gain_map.shape, F32),
            pltpu.VMEM((tok, width), BF),
            pltpu.VMEM((tok, width), BF),
            pltpu.SemaphoreType.DMA((copies,)),
        ],
        compiler_params=pltpu.CompilerParams(vmem_limit_bytes=VMEM),
        cost_estimate=SMALL,
        name="prepare",
    )(features, gain_map, tokens, core_tokens, cot, *[x for x, _ in arrays])


def per_device(
    mesh_shape,
    tokens,
    timestep,
    timestep_gain_map,
    query_key_value_weight,
    adapter_down_weight,
    adapter_up_weight,
    head_score_scale,
    heads_output_grad,
):
    dp, n = mesh_shape
    axes = ("dp", "rows")
    r, d = lax.axis_index("rows"), lax.axis_index("dp")

    def send(x, target):
        perm = []
        for a in range(dp):
            for b in range(n):
                a2, b2 = target(a, b)
                perm.append((a * n + b, a2 * n + b2))
        return lax.ppermute(x, axes, perm)

    def to_row(x, j):
        return send(x, lambda a, b: (a, b ^ j))

    tok, width = tokens.shape
    weight, cot_all = query_key_value_weight, heads_output_grad
    k_rows = weight.shape[0]
    cols = weight.shape[1] // n
    head_cols = cot_all.shape[1] // n
    chips = list(range(2, n, 2))

    pair_cols = cols // 2 if cols % 256 == 0 else cols
    half = k_rows // 2
    pair, quad = [], []
    for j in chips:
        if pair_cols < cols:
            start = (d % 4 // 2 * half, (r ^ (j + d % 2)) * cols + pair_cols)
            x = lax.dynamic_slice(weight, start, (half, cols - pair_cols))
            quad.append(send(x, lambda a, b, j=j: (a, b ^ (j + a % 2))))
        x = lax.dynamic_slice(weight, (0, (r ^ (j + d // 2 % 2)) * cols), (k_rows, pair_cols))
        pair.append(send(x, lambda a, b, j=j: (a, b ^ (j + a // 2 % 2))))

    core_weight, core_tokens, core_cot = (to_row(x, 1) for x in (weight, tokens, cot_all))

    def mine(x, size):
        if size % 128 == 0 and x is weight:
            return hbm([x])[0], size
        return (x, size) if size % 128 == 0 else (lax.dynamic_slice(x, (0, r * size), (x.shape[0], size)), 0)

    own_map, own_tokens, own_cot = hbm([timestep_gain_map, tokens, cot_all])
    normed, core_normed, gain, inv_rms, own_w, core_w, own_cot, core_cot, *chip_cot = prepare_call(
        time_features(timestep), own_map, own_tokens, core_tokens, own_cot, chips, head_cols,
        [mine(weight, cols), mine(core_weight, cols), mine(cot_all, head_cols), mine(core_cot, head_cols)],
    )
    arrays = [own_w, core_w, normed, core_normed]
    w_from, x_from = [(0, 0, 0, 1, 0, 0), (1, 0, 1, 1, 0, 0)], [(2, tok), (3, tok)]
    def exchange(x, other):
        return send(x, lambda a, b: (a ^ other, b))

    early = []
    for j, x in zip(chips, quad):
        held = [x, exchange(x, 1), exchange(x, 2)]
        for other, x in enumerate(held):
            w_from.append((len(arrays), pair_cols, j, 4, other, 0))
            arrays.append(x)
        early.append(held[1])
        cut = (half * 3 // 4, half // 4)
        for at, x in zip((0, cut[0]), gate([held[2]], [cut])):
            early.append(exchange(x, 1))
            w_from.append((len(arrays), pair_cols, j, 4, 3, at))
            arrays.append(early[-1])
    for j, x in zip(chips, pair):
        w_from += [(len(arrays), 0, j, 2, 0, 0), (len(arrays) + 1, 0, j, 2, 1, 0)]
        arrays += [x, exchange(x, 2)]

    relay_rows = (tok * 5 // 8, tok * 3 // 8) if tok % 128 == 0 else (tok,)
    chip_normed = [to_row(normed, j) for j in chips]
    later = list(gate(chip_normed, [relay_rows] * len(chips), *early))
    for x in chip_normed:
        x_from.append((len(arrays), x.shape[0]))
        arrays.append(x)

    rank = adapter_up_weight.shape[0]
    down_t = adapter_down_weight.T
    up = adapter_up_weight
    if cols % 128:
        up = lax.dynamic_slice(up, (0, r * cols), (rank, cols))
    places, last_places = (0, 1, *chips), tuple(j + 1 for j in chips)
    first_x, w_all, first_qkv, first_low = qkv_call(
        n, arrays, tuple(x_from), tuple(w_from), down_t, up, len(places) * tok, cols
    )
    last_x, qkv_t, low_t = last_qkv_call(
        tok, places, last_places, [to_row(x, 1) for x in later], w_all, first_qkv, first_low, down_t, up
    )

    cots, c_from = [own_cot, core_cot], [(1, False), (1, False)]
    blocks = (tok * 3 // 4, tok // 4) if tok % 64 == 0 else (tok,)
    for j, x in zip(chips, chip_cot):
        x = to_row(x, j)
        c_from += [(1, True), (len(blocks), False)]
        cots += [x] + [to_row(y, 1) for y in other_half(x, blocks, first_low)]

    *others, grad_t, pack = attention_call(
        head_score_scale, cots, tuple(c_from), qkv_t, low_t, w_all, down_t, up, tok, 2, (F32, BF) * len(chips)
    )

    totals = [add(others[2 * i], to_row(others[2 * i + 1], 1)) for i in range(len(chips))]
    sums = [to_row(x, j) for x, j in zip(totals, chips)]
    packs = {0: pack, 1: to_row(pack, 1)}
    for j in chips:
        packs[j] = to_row(pack, j)
    blocks = (tok * 7 // 8, tok // 8) if tok % 128 == 0 else (tok,)
    mine, *core_part = own_call(grad_t, pack, w_all, down_t, tok, blocks, totals + [packs[j] for j in chips])
    core_part = [to_row(x, 1) for x in core_part]

    for j in chips:
        packs[j ^ 1] = to_row(packs[j], 1)
    down_grad_t, up_grad = adapter_call(
        [packs[j] for j in range(n)], first_x, last_x, (places, last_places), rank, n * cols, tok
    )

    input_grad = final_call(scale_call(tokens, gain, inv_rms, mine, core_part), sums)
    return (input_grad, down_grad_t.T, up_grad)


def solution(mesh):
    in_specs = (
        P(("dp", "rows"), None),
        P("dp"),
        P(),
        P("rows", None),
        P(),
        P(),
        P("rows"),
        P(("dp", "rows"), None),
    )
    out_specs = (P(("dp", "rows"), None), P("dp", None), P("dp", None))
    shape = (mesh.shape["dp"], mesh.shape["rows"])
    return jax.shard_map(
        functools.partial(per_device, shape), mesh=mesh, in_specs=in_specs, out_specs=out_specs, check_vma=False
    )
```

```python
import functools
import math

import jax
import jax.numpy as jnp
from jax import lax
from jax.experimental import pallas as pl
from jax.experimental.pallas import tpu as pltpu
from jax.sharding import PartitionSpec as P

HEAD = 64
EMB = 256
EPS = 1e-06
LOG2E = 1.4426950408889634
BF = jnp.bfloat16
F32 = jnp.float32
VMEM = 16 * 1024 * 1024
SMALL = pl.CostEstimate(flops=1, bytes_accessed=1, transcendentals=0)


def time_features(timestep):
    half_emb = EMB // 2
    frequency = jnp.exp(-math.log(10000.0) * jnp.arange(half_emb, dtype=F32) / half_emb)
    phases = timestep.astype(F32)[0] * frequency
    return jnp.stack([jnp.cos(phases), jnp.sin(phases)])


def contract(a, b, a_dim, b_dim):
    return lax.dot_general(a, b, (((a_dim,), (b_dim,)), ((), ())), preferred_element_type=F32)


def columns(x, size):
    if x.shape[1] == size:
        return x[...]
    return x[:, pl.ds(pl.multiple_of(lax.axis_index("rows") * size, 128), size)]


def multiply(x_all, w_all, down_t, up, put):
    seq = x_all.shape[0]
    step = math.gcd(512, seq) if seq > 512 else seq
    for s in range(0, seq, step):
        x = x_all[pl.ds(s, step), :]
        low = contract(x, down_t[...], 1, 1).astype(BF)
        qkv = jnp.dot(x, w_all[...], preferred_element_type=F32)
        qkv = qkv + 0.5 * jnp.dot(low, up, preferred_element_type=F32)
        put(s, step, qkv.astype(BF).T, low.T)


def qkv_kernel(n, x_from, w_from, *refs):
    down_t, up_in = refs[-6:-4]
    r, d = lax.axis_index("rows"), lax.axis_index("dp")
    up = columns(up_in, refs[-2].shape[0])
    x_all, w_all, qkv_t, low_t = refs[-4:]
    at = 0
    for i, rows in x_from:
        x_all[pl.ds(at, rows), :] = refs[i][...]
        at += rows
    for i, to, j, group, other, row in w_from:
        rows, cols = refs[i].shape
        holder, part = r ^ j, 0
        if group == 2:
            holder = r ^ (j + (lax.rem(lax.div(d, 2), 2) ^ other))
        elif group == 4:
            share = lax.rem(d, 4) ^ other
            holder, part = r ^ (j + lax.rem(share, 2)), lax.div(share, 2)
        held_rows = w_all.shape[0] // n
        base = pl.multiple_of(holder * held_rows + part * (held_rows // 2) + row, 16)
        w_all[pl.ds(base, rows), pl.ds(to, cols)] = refs[i][...]

    def put(start, rows, qkv, low):
        qkv_t[:, pl.ds(start, rows)] = qkv
        low_t[:, pl.ds(start, rows)] = low

    multiply(x_all, w_all, down_t, up, put)


def qkv_call(n, arrays, x_from, w_from, down_t, up, seq, cols):
    rank, width = down_t.shape
    return pl.pallas_call(
        functools.partial(qkv_kernel, n, x_from, w_from),
        out_shape=[
            in_vmem((seq, width), BF),
            in_vmem((width, cols), BF),
            in_vmem((cols, seq), BF),
            in_vmem((rank, seq), BF),
        ],
        in_specs=whole_vmem(len(arrays) + 2),
        out_specs=whole_vmem(4),
        compiler_params=pltpu.CompilerParams(vmem_limit_bytes=VMEM),
        cost_estimate=SMALL,
        name="qkv",
    )(*vmem(arrays), down_t, up)


def last_qkv_kernel(tok, places, last_places, *refs):
    w_all, first_qkv, first_low, down_t, up_in, x_all, qkv_t, low_t = refs[-8:]
    at = 0
    for x in refs[:-8]:
        rows = x.shape[0]
        x_all[pl.ds(at, rows), :] = x[...]
        at += rows
    for i, place in enumerate(places):
        qkv_t[:, pl.ds(place * tok, tok)] = first_qkv[:, pl.ds(i * tok, tok)]
        low_t[:, pl.ds(place * tok, tok)] = first_low[:, pl.ds(i * tok, tok)]

    def put(start, rows, qkv, low):
        for at in range(start, start + rows, tok):
            place = last_places[at // tok] * tok
            qkv_t[:, pl.ds(place, tok)] = qkv[:, at - start : at - start + tok]
            low_t[:, pl.ds(place, tok)] = low[:, at - start : at - start + tok]

    multiply(x_all, w_all, down_t, columns(up_in, qkv_t.shape[0]), put)


def last_qkv_call(tok, places, last_places, xs, w_all, first_qkv, first_low, down_t, up):
    rank, width = down_t.shape
    cols = w_all.shape[1]
    seq = (len(places) + len(last_places)) * tok
    return pl.pallas_call(
        functools.partial(last_qkv_kernel, tok, places, last_places),
        out_shape=[
            in_vmem((len(last_places) * tok, width), BF),
            in_vmem((cols, seq), BF),
            in_vmem((rank, seq), BF),
        ],
        in_specs=whole_vmem(len(xs) + 5),
        out_specs=whole_vmem(3),
        compiler_params=pltpu.CompilerParams(vmem_limit_bytes=VMEM),
        cost_estimate=SMALL,
        name="last_qkv",
    )(*vmem(xs), *vmem([w_all, first_qkv, first_low]), down_t, up)


def gate(xs, blocks, *deps):
    xs = [x if isinstance(x, list) else [x] for x in xs]
    flat = [(i, x) for i, parts in enumerate(xs) for x in parts]
    wanted = [(i, sum(sizes[:k]), rows) for i, sizes in enumerate(blocks) for k, rows in enumerate(sizes)]

    def kernel(*refs):
        outs = refs[len(flat) + len(deps) :]
        for (i, at, rows), out in zip(wanted, outs):
            start = 0
            for (owner, _), x in zip(flat, refs):
                if owner == i:
                    low, high = max(at, start), min(at + rows, start + x.shape[0])
                    if low < high:
                        out[pl.ds(low - at, high - low), :] = x[pl.ds(low - start, high - low), :]
                    start += x.shape[0]

    return pl.pallas_call(
        kernel,
        out_shape=[in_vmem((rows, xs[i][0].shape[1]), xs[i][0].dtype) for i, _, rows in wanted],
        in_specs=whole_vmem(len(flat) + len(deps)),
        out_specs=whole_vmem(len(wanted)),
        compiler_params=pltpu.CompilerParams(vmem_limit_bytes=VMEM),
        cost_estimate=SMALL,
        name="gate",
    )(*vmem([x for _, x in flat]), *vmem(deps))


def in_vmem(shape, dtype):
    return pltpu.VMEM(shape, dtype)


def vmem(xs):
    return [pltpu.with_memory_space_constraint(x, pltpu.VMEM) for x in xs]


def hbm(xs):
    return [pltpu.with_memory_space_constraint(x, pltpu.HBM) for x in xs]


def whole_vmem(count):
    return [pl.BlockSpec(memory_space=pltpu.VMEM)] * count


def qkv_call(n, arrays, x_from, w_from, down_t, up, seq, cols):
    rank, width = down_t.shape
    return pl.pallas_call(
        functools.partial(qkv_kernel, n, x_from, w_from),
        out_shape=[
            in_vmem((seq, width), BF),
            in_vmem((width, cols), BF),
            in_vmem((cols, seq), BF),
            in_vmem((rank, seq), BF),
        ],
        in_specs=whole_vmem(len(arrays) + 2),
        out_specs=whole_vmem(4),
        compiler_params=pltpu.CompilerParams(vmem_limit_bytes=VMEM),
        cost_estimate=SMALL,
        name="qkv",
    )(*vmem(arrays), down_t, up)


def token_grads(low_grad_t, grad_t, w_all, down_t, at, rows):
    grad = grad_t[:, pl.ds(at, rows)].T
    part = contract(grad, w_all[...], 1, 1)
    return part + contract(low_grad_t[:, pl.ds(at, rows)], down_t[...], 0, 0)


def attention_kernel(heads, tok, c_from, first, outs, *refs):
    refs = list(refs)
    scale = refs.pop(0)
    cots = [[refs.pop(0) for _ in range(count)] for count, _ in c_from]
    qkv_t, low_t, w_all, down_t, up_in = (refs.pop(0) for _ in range(5))
    parts = [refs.pop(0) for _ in range(outs)]
    grad_t, pack, cot_t = refs

    cols, seq = qkv_t.shape
    up = columns(up_in, cols)
    step = math.gcd(512, seq)
    width = cot_t.shape[0]
    start = lax.rem(lax.axis_index("rows"), 2) * width
    for j, (blocks, (_, choose)) in enumerate(zip(cots, c_from)):
        if not choose:
            block = jnp.concatenate([x[...] for x in blocks], axis=0)
        elif width % 128 == 0:
            block = blocks[0][:, pl.ds(pl.multiple_of(start, 128), width)]
        else:
            block = jnp.where(start == 0, blocks[0][:, pl.ds(0, width)], blocks[0][:, pl.ds(width, width)])
        cot_t[:, pl.ds(j * tok, tok)] = block.T

    for h in range(heads):
        o = 3 * HEAD * h
        kf = qkv_t[pl.ds(o + HEAD, HEAD), :].astype(F32)
        k_inv = lax.rsqrt(jnp.sum(kf * kf, 0, keepdims=True) + EPS)
        k_unit = kf * k_inv
        k_low = k_unit.astype(BF)
        v = qkv_t[pl.ds(o + 2 * HEAD, HEAD), :]
        sc = scale[h]
        gk = gv = None
        for s in range(0, seq, step):
            qf = qkv_t[pl.ds(o, HEAD), pl.ds(s, step)].astype(F32)
            q_inv = lax.rsqrt(jnp.sum(qf * qf, 0, keepdims=True) + EPS)
            q_unit = qf * q_inv
            q_low = q_unit.astype(BF)
            g = cot_t[pl.ds(HEAD * h, HEAD), pl.ds(s, step)]
            e = jnp.exp2(contract(k_low, q_low, 0, 0) * (sc * LOG2E))
            share = 1.0 / jnp.sum(e, 0, keepdims=True)
            grad_probs = contract(v, g, 0, 0)
            delta = jnp.sum(e * grad_probs, 0, keepdims=True) * share
            attention = e * share
            grad_scores = (attention * (grad_probs - delta)).astype(BF)
            gv_s = jnp.dot(attention.astype(BF), g.T, preferred_element_type=F32)
            gk_s = jnp.dot(grad_scores, q_low.T, preferred_element_type=F32)
            gq = sc * jnp.dot(k_low, grad_scores, preferred_element_type=F32)
            gq = q_inv * (gq - q_unit * jnp.sum(q_unit * gq, 0, keepdims=True))
            grad_t[pl.ds(o, HEAD), pl.ds(s, step)] = gq.astype(BF)
            gv = gv_s if gv is None else gv + gv_s
            gk = gk_s if gk is None else gk + gk_s
        gk = sc * gk.T
        gk = k_inv * (gk - k_unit * jnp.sum(k_unit * gk, 0, keepdims=True))
        grad_t[pl.ds(o + HEAD, HEAD), :] = gk.astype(BF)
        grad_t[pl.ds(o + 2 * HEAD, HEAD), :] = gv.astype(BF).T

    rank = up.shape[0]
    pack[:, pl.ds(seq, cols)] = (0.5 * contract(low_t[...], grad_t[...], 1, 1)).astype(BF)
    low_grad_t = pack.at[:, pl.ds(0, seq)]
    low_grad_t[...] = (0.5 * jnp.dot(up, grad_t[...], preferred_element_type=F32)).astype(BF)
    for p in range(0, outs, 4):
        count = min(4, outs - p)
        part = token_grads(low_grad_t, grad_t, w_all, down_t, (first + p) * tok, count * tok)
        for i in range(count):
            out = parts[p + i]
            out[...] = part[i * tok : (i + 1) * tok].astype(out.dtype)


def attention_call(scale, cots, c_from, qkv_t, low_t, w_all, down_t, up, tok, first, dtypes):
    cols, seq = qkv_t.shape
    rank, width = down_t.shape
    smem = pl.BlockSpec(memory_space=pltpu.SMEM)
    outs = len(dtypes)
    return pl.pallas_call(
        functools.partial(attention_kernel, cols // (3 * HEAD), tok, c_from, first, outs),
        out_shape=[in_vmem((tok, width), t) for t in dtypes]
        + [in_vmem((cols, seq), BF), in_vmem((rank, seq + cols), BF)],
        in_specs=[smem] + whole_vmem(len(cots) + 5),
        out_specs=whole_vmem(outs + 2),
        scratch_shapes=[pltpu.VMEM((cols // 3, seq), BF)],
        compiler_params=pltpu.CompilerParams(vmem_limit_bytes=VMEM),
        cost_estimate=SMALL,
        name="attention_grads",
    )(scale, *vmem(cots), qkv_t, low_t, w_all, down_t, up)


def other_half(x, blocks, dep):
    half = x.shape[1] // 2
    starts = [sum(blocks[:i]) for i in range(len(blocks))]
    if half % 128:
        col = (lax.axis_index("rows") ^ 1) % 2 * half
        return [lax.dynamic_slice(x, (at, col), (rows, half)) for at, rows in zip(starts, blocks)]

    def kernel(x, dep, *outs):
        core = lax.rem(lax.axis_index("rows") ^ 1, 2)
        for at, rows, out in zip(starts, blocks, outs):
            out[...] = x[pl.ds(at, rows), pl.ds(pl.multiple_of(core * half, 128), half)]

    return pl.pallas_call(
        kernel,
        out_shape=[in_vmem((rows, half), x.dtype) for rows in blocks],
        in_specs=whole_vmem(2),
        out_specs=whole_vmem(len(blocks)),
        compiler_params=pltpu.CompilerParams(vmem_limit_bytes=VMEM),
        cost_estimate=SMALL,
        name="other_half",
    )(*vmem([x, dep]))


def add(a, b):
    def kernel(a, b, out):
        out[...] = (a[...] + b[...].astype(F32)).astype(BF)

    return pl.pallas_call(
        kernel,
        out_shape=in_vmem(a.shape, BF),
        in_specs=whole_vmem(2),
        out_specs=whole_vmem(1)[0],
        compiler_params=pltpu.CompilerParams(vmem_limit_bytes=VMEM),
        cost_estimate=SMALL,
        name="add",
    )(*vmem([a, b]))


def own_kernel(deps, grad_t, pack, w_all, down_t, *refs):
    mine, rest = refs[deps], refs[deps + 1 :]
    tok = mine.shape[0]
    part = token_grads(pack, grad_t, w_all, down_t, 0, 2 * tok)
    mine[...] = part[:tok]
    part = part[tok:].astype(BF)
    at = 0
    for out in rest:
        out[...] = part[at : at + out.shape[0]]
        at += out.shape[0]


def own_call(grad_t, pack, w_all, down_t, tok, blocks, deps):
    width = down_t.shape[1]
    return pl.pallas_call(
        functools.partial(own_kernel, len(deps)),
        out_shape=[in_vmem((tok, width), F32)] + [in_vmem((rows, width), BF) for rows in blocks],
        in_specs=whole_vmem(4 + len(deps)),
        out_specs=whole_vmem(1 + len(blocks)),
        compiler_params=pltpu.CompilerParams(vmem_limit_bytes=VMEM),
        cost_estimate=SMALL,
        name="own_grads",
    )(grad_t, pack, w_all, down_t, *vmem(deps))


def adapter_kernel(tok, places, *refs):
    packs, (first_x, last_x, down_grad_t, up_grad) = refs[:-4], refs[-4:]
    r = lax.axis_index("rows")
    total = None
    for j, pack in enumerate(packs):
        blocks = [pack[:, pl.ds((q ^ j) * tok, tok)] for q in range(len(packs))]
        term = jnp.concatenate(blocks, axis=1).astype(F32)
        total = term if total is None else total + term
    total = total.astype(BF)
    grad = None
    for x, held in zip((first_x, last_x), places):
        part = jnp.concatenate([total[:, p * tok : (p + 1) * tok] for p in held], axis=1)
        term = jnp.dot(part, x[...], preferred_element_type=F32)
        grad = term if grad is None else grad + term
    down_grad_t[...] = grad
    cols = up_grad.shape[1] // len(packs)
    for j, pack in enumerate(packs):
        if cols % 128 == 0:
            up_grad[:, pl.ds(pl.multiple_of((r ^ j) * cols, 128), cols)] = pack[:, pl.ds(len(packs) * tok, cols)].astype(F32)


def adapter_call(packs, first_x, last_x, places, rank, all_cols, tok):
    down_grad_t, up_grad = pl.pallas_call(
        functools.partial(adapter_kernel, tok, places),
        out_shape=[
            jax.ShapeDtypeStruct((rank, first_x.shape[1]), F32),
            jax.ShapeDtypeStruct((rank, all_cols), F32),
        ],
        in_specs=whole_vmem(len(packs) + 2),
        out_specs=whole_vmem(2),
        compiler_params=pltpu.CompilerParams(vmem_limit_bytes=VMEM),
        cost_estimate=SMALL,
        name="adapter_grads",
    )(*vmem(packs), *vmem([first_x, last_x]))
    cols = all_cols // len(packs)
    if cols % 128:
        for j, pack in enumerate(packs):
            up_grad = lax.dynamic_update_slice(up_grad, pack[:, len(packs) * tok :].astype(F32), (0, (lax.axis_index("rows") ^ j) * cols))
    return down_grad_t, up_grad


def scale_kernel(tokens, gain, inv_rms, mine, *refs):
    blocks, (total, token_gain, scale, slope) = refs[:-4], refs[-4:]
    at = 0
    for block in blocks:
        rows = pl.ds(at, block.shape[0])
        total[rows, :] = mine[rows, :] + block[...].astype(F32)
        at += block.shape[0]
    x = tokens[...].astype(F32)
    inv = inv_rms[...]
    token_gain[...] = x * gain[...]
    scale[...] = inv * gain[...]
    slope[...] = x * (inv * inv * inv * (1.0 / x.shape[1]))


def scale_call(tokens, gain, inv_rms, mine, blocks):
    return pl.pallas_call(
        scale_kernel,
        out_shape=[in_vmem(tokens.shape, F32)] * 4,
        in_specs=whole_vmem(4 + len(blocks)),
        out_specs=whole_vmem(4),
        compiler_params=pltpu.CompilerParams(vmem_limit_bytes=VMEM),
        cost_estimate=SMALL,
        name="scale",
    )(tokens, gain, inv_rms, mine, *vmem(blocks))


def final_kernel(total, token_gain, scale, slope, *refs):
    terms, (out, made, sems) = refs[:-3], refs[-3:]
    count = sems.shape[0]
    rows = made.shape[0] // count
    copies = []
    for i in range(count):
        block = pl.ds(i * rows, rows)
        grad = total[block, :]
        for x in terms:
            grad = grad + x[block, :].astype(F32)
        moment = jnp.sum(grad * token_gain[block, :], -1, keepdims=True)
        made[block, :] = (grad * scale[block, :] - slope[block, :] * moment).astype(BF)
        copies.append(pltpu.make_async_copy(made.at[block], out.at[block], sems.at[i]))
        copies[-1].start()
    for c in copies:
        c.wait()


def final_call(held, terms):
    shape = held[0].shape
    count = 4 if shape[0] % 64 == 0 else 1
    return pl.pallas_call(
        final_kernel,
        out_shape=jax.ShapeDtypeStruct(shape, BF),
        in_specs=whole_vmem(4 + len(terms)),
        out_specs=pl.BlockSpec(memory_space=pltpu.HBM),
        scratch_shapes=[pltpu.VMEM(shape, BF), pltpu.SemaphoreType.DMA((count,))],
        compiler_params=pltpu.CompilerParams(vmem_limit_bytes=VMEM),
        cost_estimate=SMALL,
        name="input_grads",
    )(*vmem(held), *vmem(terms))


def shares_kernel(chips, pair_cols, weight, *refs):
    r, d = lax.axis_index("rows"), lax.axis_index("dp")
    outs, sems = refs[:-1], refs[-1]
    cols = pair_cols + outs[0].shape[1]
    copies = []
    for i, j in enumerate(chips):
        half = outs[2 * i].shape[0]
        row = pl.multiple_of(lax.div(lax.rem(d, 4), 2) * half, 16)
        col = pl.multiple_of((r ^ (j + lax.rem(d, 2))) * cols + pair_cols, 128)
        copies.append((weight.at[pl.ds(row, half), pl.ds(col, cols - pair_cols)], outs[2 * i]))
        col = pl.multiple_of((r ^ (j + lax.rem(lax.div(d, 2), 2))) * cols, 128)
        copies.append((weight.at[:, pl.ds(col, pair_cols)], outs[2 * i + 1]))
    copies = [pltpu.make_async_copy(a, b, sems.at[i]) for i, (a, b) in enumerate(copies)]
    for c in copies:
        c.start()
    for c in copies:
        c.wait()


def shares_call(weight, chips, cols, pair_cols):
    rows = weight.shape[0]
    count = 2 * len(chips)
    return pl.pallas_call(
        functools.partial(shares_kernel, chips, pair_cols),
        out_shape=[in_vmem((rows // 2, cols - pair_cols), BF), in_vmem((rows, pair_cols), BF)] * len(chips),
        in_specs=[pl.BlockSpec(memory_space=pltpu.HBM)],
        out_specs=whole_vmem(count),
        scratch_shapes=[pltpu.SemaphoreType.DMA((count,))],
        compiler_params=pltpu.CompilerParams(vmem_limit_bytes=VMEM),
        cost_estimate=SMALL,
        name="shares",
    )(*hbm([weight]))


def prepare_kernel(chips, head_cols, sizes, features, gain_map, tokens, core_tokens, cot, *refs):
    count, outs = len(sizes), len(sizes) + len(chips)
    normed, core_normed, gain, inv_rms = refs[count : count + 4]
    cut = refs[count + 4 : count + 4 + outs]
    map_in, tokens_in, core_in, sems = refs[count + 4 + outs :]
    r = lax.axis_index("rows")
    copies = [(tokens, tokens_in), (core_tokens, core_in), (gain_map, map_in)]
    for x, size, out in zip(refs, sizes, cut):
        copies.append((x.at[:, pl.ds(pl.multiple_of(r * size, 128), size)] if size else x, out))
    for j, out in zip(chips, cut[count:]):
        chip = lax.div(r ^ j, 2) * (2 * head_cols)
        copies.append((cot.at[:, pl.ds(pl.multiple_of(chip, 128), 2 * head_cols)], out))
    copies = [pltpu.make_async_copy(a, b, sems.at[i]) for i, (a, b) in enumerate(copies)]
    for c in copies:
        c.start()
    half = features.shape[1]
    col = features[...].T
    for c in copies[:3]:
        c.wait()
    total = jnp.sum(col[:, :1] * map_in[:half, :], 0, keepdims=True)
    total = total + jnp.sum(col[:, 1:] * map_in[half:, :], 0, keepdims=True)
    gain[...] = 1.0 + total
    for x, out in ((tokens_in, normed), (core_in, core_normed)):
        x = x[...].astype(F32)
        inv = lax.rsqrt(jnp.mean(x * x, -1, keepdims=True) + EPS)
        if out is normed:
            inv_rms[...] = inv
        out[...] = (x * inv * gain[...]).astype(BF)
    for c in copies[3:]:
        c.wait()


def prepare_call(features, gain_map, tokens, core_tokens, cot, chips, head_cols, arrays):
    tok, width = tokens.shape
    shapes = [((tok, width), BF), ((tok, width), BF), ((1, width), F32), ((tok, 1), F32)]
    shapes += [((x.shape[0], size or x.shape[1]), BF) for x, size in arrays]
    shapes += [((tok, 2 * head_cols), BF)] * len(chips)
    copies = 3 + len(arrays) + len(chips)
    return pl.pallas_call(
        functools.partial(prepare_kernel, chips, head_cols, [size for _, size in arrays]),
        out_shape=[in_vmem(*shape) for shape in shapes],
        in_specs=whole_vmem(1) + [pl.BlockSpec(memory_space=pl.ANY)] * (4 + len(arrays)),
        out_specs=whole_vmem(len(shapes)),
        scratch_shapes=[
            pltpu.VMEM(gain_map.shape, F32),
            pltpu.VMEM((tok, width), BF),
            pltpu.VMEM((tok, width), BF),
            pltpu.SemaphoreType.DMA((copies,)),
        ],
        compiler_params=pltpu.CompilerParams(vmem_limit_bytes=VMEM),
        cost_estimate=SMALL,
        name="prepare",
    )(features, gain_map, tokens, core_tokens, cot, *[x for x, _ in arrays])


def per_device(
    mesh_shape,
    tokens,
    timestep,
    timestep_gain_map,
    query_key_value_weight,
    adapter_down_weight,
    adapter_up_weight,
    head_score_scale,
    heads_output_grad,
):
    dp, n = mesh_shape
    axes = ("dp", "rows")
    r, d = lax.axis_index("rows"), lax.axis_index("dp")

    def send(x, target):
        perm = []
        for a in range(dp):
            for b in range(n):
                a2, b2 = target(a, b)
                perm.append((a * n + b, a2 * n + b2))
        return lax.ppermute(x, axes, perm)

    def to_row(x, j):
        return send(x, lambda a, b: (a, b ^ j))

    tok, width = tokens.shape
    weight, cot_all = query_key_value_weight, heads_output_grad
    k_rows = weight.shape[0]
    cols = weight.shape[1] // n
    head_cols = cot_all.shape[1] // n
    chips = list(range(2, n, 2))

    pair_cols = cols // 2 if cols % 256 == 0 else cols
    half = k_rows // 2
    pair, quad = [], []
    if pair_cols < cols:
        pieces = shares_call(weight, chips, cols, pair_cols)
        quad, pair = list(pieces[0::2]), list(pieces[1::2])
    else:
        pair = [lax.dynamic_slice(weight, (0, (r ^ (j + d // 2 % 2)) * cols), (k_rows, cols)) for j in chips]
    quad = [send(x, lambda a, b, j=j: (a, b ^ (j + a % 2))) for x, j in zip(quad, chips)]
    pair = [send(x, lambda a, b, j=j: (a, b ^ (j + a // 2 % 2))) for x, j in zip(pair, chips)]

    core_weight, core_tokens, core_cot = (to_row(x, 1) for x in (weight, tokens, cot_all))

    def mine(x, size):
        if size % 128 == 0 and x is weight:
            return hbm([x])[0], size
        return (x, size) if size % 128 == 0 else (lax.dynamic_slice(x, (0, r * size), (x.shape[0], size)), 0)

    own_map, own_tokens, own_cot = hbm([timestep_gain_map, tokens, cot_all])
    normed, core_normed, gain, inv_rms, own_w, core_w, own_cot, core_cot, *chip_cot = prepare_call(
        time_features(timestep), own_map, own_tokens, core_tokens, own_cot, chips, head_cols,
        [mine(weight, cols), mine(core_weight, cols), mine(cot_all, head_cols), mine(core_cot, head_cols)],
    )
    arrays = [own_w, core_w, normed, core_normed]
    w_from, x_from = [(0, 0, 0, 1, 0, 0), (1, 0, 1, 1, 0, 0)], [(2, tok), (3, tok)]
    def exchange(x, other):
        return send(x, lambda a, b: (a ^ other, b))

    early = []
    for j, x in zip(chips, quad):
        held = [x, exchange(x, 1), exchange(x, 2)]
        for other, x in enumerate(held):
            w_from.append((len(arrays), pair_cols, j, 4, other, 0))
            arrays.append(x)
        early.append(held[1])
        cut = (half * 3 // 4, half // 4)
        for at, x in zip((0, cut[0]), gate([held[2]], [cut])):
            early.append(exchange(x, 1))
            w_from.append((len(arrays), pair_cols, j, 4, 3, at))
            arrays.append(early[-1])
    for j, x in zip(chips, pair):
        w_from += [(len(arrays), 0, j, 2, 0, 0), (len(arrays) + 1, 0, j, 2, 1, 0)]
        arrays += [x, exchange(x, 2)]

    relay_rows = (tok * 5 // 8, tok * 3 // 8) if tok % 128 == 0 else (tok,)
    chip_normed = [to_row(normed, j) for j in chips]
    later = list(gate(chip_normed, [relay_rows] * len(chips), *early))
    for x in chip_normed:
        x_from.append((len(arrays), x.shape[0]))
        arrays.append(x)

    rank = adapter_up_weight.shape[0]
    down_t = adapter_down_weight.T
    up = adapter_up_weight
    if cols % 128:
        up = lax.dynamic_slice(up, (0, r * cols), (rank, cols))
    places, last_places = (0, 1, *chips), tuple(j + 1 for j in chips)
    first_x, w_all, first_qkv, first_low = qkv_call(
        n, arrays, tuple(x_from), tuple(w_from), down_t, up, len(places) * tok, cols
    )
    last_x, qkv_t, low_t = last_qkv_call(
        tok, places, last_places, [to_row(x, 1) for x in later], w_all, first_qkv, first_low, down_t, up
    )

    cots, c_from = [own_cot, core_cot], [(1, False), (1, False)]
    blocks = (tok * 3 // 4, tok // 4) if tok % 64 == 0 else (tok,)
    for j, x in zip(chips, chip_cot):
        x = to_row(x, j)
        c_from += [(1, True), (len(blocks), False)]
        cots += [x] + [to_row(y, 1) for y in other_half(x, blocks, first_low)]

    *others, grad_t, pack = attention_call(
        head_score_scale, cots, tuple(c_from), qkv_t, low_t, w_all, down_t, up, tok, 2, (F32, BF) * len(chips)
    )

    totals = [add(others[2 * i], to_row(others[2 * i + 1], 1)) for i in range(len(chips))]
    sums = [to_row(x, j) for x, j in zip(totals, chips)]
    packs = {0: pack, 1: to_row(pack, 1)}
    for j in chips:
        packs[j] = to_row(pack, j)
    blocks = (tok * 7 // 8, tok // 8) if tok % 128 == 0 else (tok,)
    mine, *core_part = own_call(grad_t, pack, w_all, down_t, tok, blocks, totals + [packs[j] for j in chips])
    core_part = [to_row(x, 1) for x in core_part]

    for j in chips:
        packs[j ^ 1] = to_row(packs[j], 1)
    down_grad_t, up_grad = adapter_call(
        [packs[j] for j in range(n)], first_x, last_x, (places, last_places), rank, n * cols, tok
    )

    input_grad = final_call(scale_call(tokens, gain, inv_rms, mine, core_part), sums)
    return (input_grad, down_grad_t.T, up_grad)


def solution(mesh):
    in_specs = (
        P(("dp", "rows"), None),
        P("dp"),
        P(),
        P("rows", None),
        P(),
        P(),
        P("rows"),
        P(("dp", "rows"), None),
    )
    out_specs = (P(("dp", "rows"), None), P("dp", None), P("dp", None))
    shape = (mesh.shape["dp"], mesh.shape["rows"])
    return jax.shard_map(
        functools.partial(per_device, shape), mesh=mesh, in_specs=in_specs, out_specs=out_specs, check_vma=False
    )
```

```python
import functools
import math

import jax
import jax.numpy as jnp
from jax import lax
from jax.experimental import pallas as pl
from jax.experimental.pallas import tpu as pltpu
from jax.sharding import PartitionSpec as P

HEAD = 64
EMB = 256
EPS = 1e-06
LOG2E = 1.4426950408889634
BF = jnp.bfloat16
F32 = jnp.float32
VMEM = 16 * 1024 * 1024
SMALL = pl.CostEstimate(flops=1, bytes_accessed=1, transcendentals=0)


def time_features(timestep):
    half_emb = EMB // 2
    frequency = jnp.exp(-math.log(10000.0) * jnp.arange(half_emb, dtype=F32) / half_emb)
    phases = timestep.astype(F32)[0] * frequency
    return jnp.stack([jnp.cos(phases), jnp.sin(phases)])


def contract(a, b, a_dim, b_dim):
    return lax.dot_general(a, b, (((a_dim,), (b_dim,)), ((), ())), preferred_element_type=F32)


def columns(x, size):
    if x.shape[1] == size:
        return x[...]
    return x[:, pl.ds(pl.multiple_of(lax.axis_index("rows") * size, 128), size)]


def multiply(x_all, w_all, down_t, up, put):
    seq = x_all.shape[0]
    step = math.gcd(512, seq) if seq > 512 else seq
    for s in range(0, seq, step):
        x = x_all[pl.ds(s, step), :]
        low = contract(x, down_t[...], 1, 1).astype(BF)
        qkv = jnp.dot(x, w_all[...], preferred_element_type=F32)
        qkv = qkv + 0.5 * jnp.dot(low, up, preferred_element_type=F32)
        put(s, step, qkv.astype(BF).T, low.T)


def qkv_kernel(n, x_from, w_from, *refs):
    down_t, up_in = refs[-6:-4]
    r, d = lax.axis_index("rows"), lax.axis_index("dp")
    up = columns(up_in, refs[-2].shape[0])
    x_all, w_all, qkv_t, low_t = refs[-4:]
    at = 0
    for i, rows in x_from:
        x_all[pl.ds(at, rows), :] = refs[i][...]
        at += rows
    for i, to, j, group, other, row in w_from:
        rows, cols = refs[i].shape
        holder, part = r ^ j, 0
        if group == 2:
            holder = r ^ (j + (lax.rem(lax.div(d, 2), 2) ^ other))
        elif group == 4:
            share = lax.rem(d, 4) ^ other
            holder, part = r ^ (j + lax.rem(share, 2)), lax.div(share, 2)
        held_rows = w_all.shape[0] // n
        base = pl.multiple_of(holder * held_rows + part * (held_rows // 2) + row, 16)
        w_all[pl.ds(base, rows), pl.ds(to, cols)] = refs[i][...]

    def put(start, rows, qkv, low):
        qkv_t[:, pl.ds(start, rows)] = qkv
        low_t[:, pl.ds(start, rows)] = low

    multiply(x_all, w_all, down_t, up, put)


def qkv_call(n, arrays, x_from, w_from, down_t, up, seq, cols):
    rank, width = down_t.shape
    return pl.pallas_call(
        functools.partial(qkv_kernel, n, x_from, w_from),
        out_shape=[
            in_vmem((seq, width), BF),
            in_vmem((width, cols), BF),
            in_vmem((cols, seq), BF),
            in_vmem((rank, seq), BF),
        ],
        in_specs=whole_vmem(len(arrays) + 2),
        out_specs=whole_vmem(4),
        compiler_params=pltpu.CompilerParams(vmem_limit_bytes=VMEM),
        cost_estimate=SMALL,
        name="qkv",
    )(*vmem(arrays), down_t, up)


def last_qkv_kernel(tok, places, last_places, *refs):
    w_all, first_qkv, first_low, down_t, up_in, x_all, qkv_t, low_t = refs[-8:]
    at = 0
    for x in refs[:-8]:
        rows = x.shape[0]
        x_all[pl.ds(at, rows), :] = x[...]
        at += rows
    for i, place in enumerate(places):
        qkv_t[:, pl.ds(place * tok, tok)] = first_qkv[:, pl.ds(i * tok, tok)]
        low_t[:, pl.ds(place * tok, tok)] = first_low[:, pl.ds(i * tok, tok)]

    def put(start, rows, qkv, low):
        for at in range(start, start + rows, tok):
            place = last_places[at // tok] * tok
            qkv_t[:, pl.ds(place, tok)] = qkv[:, at - start : at - start + tok]
            low_t[:, pl.ds(place, tok)] = low[:, at - start : at - start + tok]

    multiply(x_all, w_all, down_t, columns(up_in, qkv_t.shape[0]), put)


def last_qkv_call(tok, places, last_places, xs, w_all, first_qkv, first_low, down_t, up):
    rank, width = down_t.shape
    cols = w_all.shape[1]
    seq = (len(places) + len(last_places)) * tok
    return pl.pallas_call(
        functools.partial(last_qkv_kernel, tok, places, last_places),
        out_shape=[
            in_vmem((len(last_places) * tok, width), BF),
            in_vmem((cols, seq), BF),
            in_vmem((rank, seq), BF),
        ],
        in_specs=whole_vmem(len(xs) + 5),
        out_specs=whole_vmem(3),
        compiler_params=pltpu.CompilerParams(vmem_limit_bytes=VMEM),
        cost_estimate=SMALL,
        name="last_qkv",
    )(*vmem(xs), *vmem([w_all, first_qkv, first_low]), down_t, up)


def gate(xs, blocks, *deps):
    xs = [x if isinstance(x, list) else [x] for x in xs]
    flat = [(i, x) for i, parts in enumerate(xs) for x in parts]
    wanted = [(i, sum(sizes[:k]), rows) for i, sizes in enumerate(blocks) for k, rows in enumerate(sizes)]

    def kernel(*refs):
        outs = refs[len(flat) + len(deps) :]
        for (i, at, rows), out in zip(wanted, outs):
            start = 0
            for (owner, _), x in zip(flat, refs):
                if owner == i:
                    low, high = max(at, start), min(at + rows, start + x.shape[0])
                    if low < high:
                        out[pl.ds(low - at, high - low), :] = x[pl.ds(low - start, high - low), :]
                    start += x.shape[0]

    return pl.pallas_call(
        kernel,
        out_shape=[in_vmem((rows, xs[i][0].shape[1]), xs[i][0].dtype) for i, _, rows in wanted],
        in_specs=whole_vmem(len(flat) + len(deps)),
        out_specs=whole_vmem(len(wanted)),
        compiler_params=pltpu.CompilerParams(vmem_limit_bytes=VMEM),
        cost_estimate=SMALL,
        name="gate",
    )(*vmem([x for _, x in flat]), *vmem(deps))


def in_vmem(shape, dtype):
    return pltpu.VMEM(shape, dtype)


def vmem(xs):
    return [pltpu.with_memory_space_constraint(x, pltpu.VMEM) for x in xs]


def hbm(xs):
    return [pltpu.with_memory_space_constraint(x, pltpu.HBM) for x in xs]


def whole_vmem(count):
    return [pl.BlockSpec(memory_space=pltpu.VMEM)] * count


def qkv_call(n, arrays, x_from, w_from, down_t, up, seq, cols):
    rank, width = down_t.shape
    return pl.pallas_call(
        functools.partial(qkv_kernel, n, x_from, w_from),
        out_shape=[
            in_vmem((seq, width), BF),
            in_vmem((width, cols), BF),
            in_vmem((cols, seq), BF),
            in_vmem((rank, seq), BF),
        ],
        in_specs=whole_vmem(len(arrays) + 2),
        out_specs=whole_vmem(4),
        compiler_params=pltpu.CompilerParams(vmem_limit_bytes=VMEM),
        cost_estimate=SMALL,
        name="qkv",
    )(*vmem(arrays), down_t, up)


def token_grads(low_grad_t, grad_t, w_all, down_t, at, rows):
    low = contract(low_grad_t[:, pl.ds(at, rows)], down_t[...], 0, 0)
    return low + contract(grad_t[:, pl.ds(at, rows)], w_all[...], 0, 1)


def attention_kernel(heads, tok, c_from, first, outs, *refs):
    refs = list(refs)
    scale = refs.pop(0)
    cots = [[refs.pop(0) for _ in range(count)] for count, _ in c_from]
    qkv_t, low_t, w_all, down_t, up_in = (refs.pop(0) for _ in range(5))
    parts = [refs.pop(0) for _ in range(outs)]
    grad_t, pack, cot_t = refs

    cols, seq = qkv_t.shape
    up = columns(up_in, cols)
    step = math.gcd(512, seq)
    width = cot_t.shape[0]
    start = lax.rem(lax.axis_index("rows"), 2) * width
    for j, (blocks, (_, choose)) in enumerate(zip(cots, c_from)):
        if not choose:
            block = jnp.concatenate([x[...] for x in blocks], axis=0)
        elif width % 128 == 0:
            block = blocks[0][:, pl.ds(pl.multiple_of(start, 128), width)]
        else:
            block = jnp.where(start == 0, blocks[0][:, pl.ds(0, width)], blocks[0][:, pl.ds(width, width)])
        cot_t[:, pl.ds(j * tok, tok)] = block.T

    for h in range(heads):
        o = 3 * HEAD * h
        kf = qkv_t[pl.ds(o + HEAD, HEAD), :].astype(F32)
        k_inv = lax.rsqrt(jnp.sum(kf * kf, 0, keepdims=True) + EPS)
        k_unit = kf * k_inv
        k_low = k_unit.astype(BF)
        v = qkv_t[pl.ds(o + 2 * HEAD, HEAD), :]
        sc = scale[h]
        gk = gv = None
        for s in range(0, seq, step):
            qf = qkv_t[pl.ds(o, HEAD), pl.ds(s, step)].astype(F32)
            q_inv = lax.rsqrt(jnp.sum(qf * qf, 0, keepdims=True) + EPS)
            q_unit = qf * q_inv
            q_low = q_unit.astype(BF)
            g = cot_t[pl.ds(HEAD * h, HEAD), pl.ds(s, step)]
            e = jnp.exp2(contract(k_low, q_low, 0, 0) * (sc * LOG2E))
            share = 1.0 / jnp.sum(e, 0, keepdims=True)
            grad_probs = contract(v, g, 0, 0)
            delta = jnp.sum(e * grad_probs, 0, keepdims=True) * share
            attention = e * share
            grad_scores = (attention * (grad_probs - delta)).astype(BF)
            gv_s = jnp.dot(attention.astype(BF), g.T, preferred_element_type=F32)
            gk_s = jnp.dot(grad_scores, q_low.T, preferred_element_type=F32)
            gq = sc * jnp.dot(k_low, grad_scores, preferred_element_type=F32)
            gq = q_inv * (gq - q_unit * jnp.sum(q_unit * gq, 0, keepdims=True))
            grad_t[pl.ds(o, HEAD), pl.ds(s, step)] = gq.astype(BF)
            gv = gv_s if gv is None else gv + gv_s
            gk = gk_s if gk is None else gk + gk_s
        gk = sc * gk.T
        gk = k_inv * (gk - k_unit * jnp.sum(k_unit * gk, 0, keepdims=True))
        grad_t[pl.ds(o + HEAD, HEAD), :] = gk.astype(BF)
        grad_t[pl.ds(o + 2 * HEAD, HEAD), :] = gv.astype(BF).T

    rank = up.shape[0]
    pack[:, pl.ds(seq, cols)] = (0.5 * contract(low_t[...], grad_t[...], 1, 1)).astype(BF)
    low_grad_t = pack.at[:, pl.ds(0, seq)]
    low_grad_t[...] = (0.5 * jnp.dot(up, grad_t[...], preferred_element_type=F32)).astype(BF)
    for p in range(0, outs, 4):
        count = min(4, outs - p)
        part = token_grads(low_grad_t, grad_t, w_all, down_t, (first + p) * tok, count * tok)
        for i in range(count):
            out = parts[p + i]
            out[...] = part[i * tok : (i + 1) * tok].astype(out.dtype)


def attention_call(scale, cots, c_from, qkv_t, low_t, w_all, down_t, up, tok, first, dtypes):
    cols, seq = qkv_t.shape
    rank, width = down_t.shape
    smem = pl.BlockSpec(memory_space=pltpu.SMEM)
    outs = len(dtypes)
    return pl.pallas_call(
        functools.partial(attention_kernel, cols // (3 * HEAD), tok, c_from, first, outs),
        out_shape=[in_vmem((tok, width), t) for t in dtypes]
        + [in_vmem((cols, seq), BF), in_vmem((rank, seq + cols), BF)],
        in_specs=[smem] + whole_vmem(len(cots) + 5),
        out_specs=whole_vmem(outs + 2),
        scratch_shapes=[pltpu.VMEM((cols // 3, seq), BF)],
        compiler_params=pltpu.CompilerParams(vmem_limit_bytes=VMEM),
        cost_estimate=SMALL,
        name="attention_grads",
    )(scale, *vmem(cots), qkv_t, low_t, w_all, down_t, up)


def other_half(x, blocks, dep):
    half = x.shape[1] // 2
    starts = [sum(blocks[:i]) for i in range(len(blocks))]
    if half % 128:
        col = (lax.axis_index("rows") ^ 1) % 2 * half
        return [lax.dynamic_slice(x, (at, col), (rows, half)) for at, rows in zip(starts, blocks)]

    def kernel(x, dep, *outs):
        core = lax.rem(lax.axis_index("rows") ^ 1, 2)
        for at, rows, out in zip(starts, blocks, outs):
            out[...] = x[pl.ds(at, rows), pl.ds(pl.multiple_of(core * half, 128), half)]

    return pl.pallas_call(
        kernel,
        out_shape=[in_vmem((rows, half), x.dtype) for rows in blocks],
        in_specs=whole_vmem(2),
        out_specs=whole_vmem(len(blocks)),
        compiler_params=pltpu.CompilerParams(vmem_limit_bytes=VMEM),
        cost_estimate=SMALL,
        name="other_half",
    )(*vmem([x, dep]))


def add(a, b):
    def kernel(a, b, out):
        out[...] = (a[...] + b[...].astype(F32)).astype(BF)

    return pl.pallas_call(
        kernel,
        out_shape=in_vmem(a.shape, BF),
        in_specs=whole_vmem(2),
        out_specs=whole_vmem(1)[0],
        compiler_params=pltpu.CompilerParams(vmem_limit_bytes=VMEM),
        cost_estimate=SMALL,
        name="add",
    )(*vmem([a, b]))


def own_kernel(deps, grad_t, pack, w_all, down_t, *refs):
    mine, rest = refs[deps], refs[deps + 1 :]
    tok = mine.shape[0]
    part = token_grads(pack, grad_t, w_all, down_t, 0, 2 * tok)
    mine[...] = part[:tok]
    part = part[tok:].astype(BF)
    at = 0
    for out in rest:
        out[...] = part[at : at + out.shape[0]]
        at += out.shape[0]


def own_call(grad_t, pack, w_all, down_t, tok, blocks, deps):
    width = down_t.shape[1]
    return pl.pallas_call(
        functools.partial(own_kernel, len(deps)),
        out_shape=[in_vmem((tok, width), F32)] + [in_vmem((rows, width), BF) for rows in blocks],
        in_specs=whole_vmem(4 + len(deps)),
        out_specs=whole_vmem(1 + len(blocks)),
        compiler_params=pltpu.CompilerParams(vmem_limit_bytes=VMEM),
        cost_estimate=SMALL,
        name="own_grads",
    )(grad_t, pack, w_all, down_t, *vmem(deps))


def adapter_kernel(tok, places, *refs):
    packs, (first_x, last_x, down_grad_t, up_grad) = refs[:-4], refs[-4:]
    r = lax.axis_index("rows")
    total = None
    for j, pack in enumerate(packs):
        blocks = [pack[:, pl.ds((q ^ j) * tok, tok)] for q in range(len(packs))]
        term = jnp.concatenate(blocks, axis=1).astype(F32)
        total = term if total is None else total + term
    total = total.astype(BF)
    grad = None
    for x, held in zip((first_x, last_x), places):
        part = jnp.concatenate([total[:, p * tok : (p + 1) * tok] for p in held], axis=1)
        term = jnp.dot(part, x[...], preferred_element_type=F32)
        grad = term if grad is None else grad + term
    down_grad_t[...] = grad
    cols = up_grad.shape[1] // len(packs)
    for j, pack in enumerate(packs):
        if cols % 128 == 0:
            up_grad[:, pl.ds(pl.multiple_of((r ^ j) * cols, 128), cols)] = pack[:, pl.ds(len(packs) * tok, cols)].astype(F32)


def adapter_call(packs, first_x, last_x, places, rank, all_cols, tok):
    down_grad_t, up_grad = pl.pallas_call(
        functools.partial(adapter_kernel, tok, places),
        out_shape=[
            jax.ShapeDtypeStruct((rank, first_x.shape[1]), F32),
            jax.ShapeDtypeStruct((rank, all_cols), F32),
        ],
        in_specs=whole_vmem(len(packs) + 2),
        out_specs=whole_vmem(2),
        compiler_params=pltpu.CompilerParams(vmem_limit_bytes=VMEM),
        cost_estimate=SMALL,
        name="adapter_grads",
    )(*vmem(packs), *vmem([first_x, last_x]))
    cols = all_cols // len(packs)
    if cols % 128:
        for j, pack in enumerate(packs):
            up_grad = lax.dynamic_update_slice(up_grad, pack[:, len(packs) * tok :].astype(F32), (0, (lax.axis_index("rows") ^ j) * cols))
    return down_grad_t, up_grad


def scale_kernel(tokens, gain, inv_rms, mine, *refs):
    blocks, (total, token_gain, scale, slope) = refs[:-4], refs[-4:]
    at = 0
    for block in blocks:
        rows = pl.ds(at, block.shape[0])
        total[rows, :] = mine[rows, :] + block[...].astype(F32)
        at += block.shape[0]
    x = tokens[...].astype(F32)
    inv = inv_rms[...]
    token_gain[...] = x * gain[...]
    scale[...] = inv * gain[...]
    slope[...] = x * (inv * inv * inv * (1.0 / x.shape[1]))


def scale_call(tokens, gain, inv_rms, mine, blocks):
    return pl.pallas_call(
        scale_kernel,
        out_shape=[in_vmem(tokens.shape, F32)] * 4,
        in_specs=whole_vmem(4 + len(blocks)),
        out_specs=whole_vmem(4),
        compiler_params=pltpu.CompilerParams(vmem_limit_bytes=VMEM),
        cost_estimate=SMALL,
        name="scale",
    )(tokens, gain, inv_rms, mine, *vmem(blocks))


def final_kernel(total, token_gain, scale, slope, *refs):
    terms, (out, made, sems) = refs[:-3], refs[-3:]
    count = sems.shape[0]
    rows = made.shape[0] // count
    copies = []
    for i in range(count):
        block = pl.ds(i * rows, rows)
        grad = total[block, :]
        for x in terms:
            grad = grad + x[block, :].astype(F32)
        moment = jnp.sum(grad * token_gain[block, :], -1, keepdims=True)
        made[block, :] = (grad * scale[block, :] - slope[block, :] * moment).astype(BF)
        copies.append(pltpu.make_async_copy(made.at[block], out.at[block], sems.at[i]))
        copies[-1].start()
    for c in copies:
        c.wait()


def final_call(held, terms):
    shape = held[0].shape
    count = 4 if shape[0] % 64 == 0 else 1
    return pl.pallas_call(
        final_kernel,
        out_shape=jax.ShapeDtypeStruct(shape, BF),
        in_specs=whole_vmem(4 + len(terms)),
        out_specs=pl.BlockSpec(memory_space=pltpu.HBM),
        scratch_shapes=[pltpu.VMEM(shape, BF), pltpu.SemaphoreType.DMA((count,))],
        compiler_params=pltpu.CompilerParams(vmem_limit_bytes=VMEM),
        cost_estimate=SMALL,
        name="input_grads",
    )(*vmem(held), *vmem(terms))


def shares_kernel(chips, pair_cols, weight, *refs):
    r, d = lax.axis_index("rows"), lax.axis_index("dp")
    outs, sems = refs[:-1], refs[-1]
    cols = pair_cols + outs[0].shape[1]
    copies = []
    for i, j in enumerate(chips):
        half = outs[2 * i].shape[0]
        row = pl.multiple_of(lax.div(lax.rem(d, 4), 2) * half, 16)
        col = pl.multiple_of((r ^ (j + lax.rem(d, 2))) * cols + pair_cols, 128)
        copies.append((weight.at[pl.ds(row, half), pl.ds(col, cols - pair_cols)], outs[2 * i]))
        col = pl.multiple_of((r ^ (j + lax.rem(lax.div(d, 2), 2))) * cols, 128)
        copies.append((weight.at[:, pl.ds(col, pair_cols)], outs[2 * i + 1]))
    copies = [pltpu.make_async_copy(a, b, sems.at[i]) for i, (a, b) in enumerate(copies)]
    for c in copies:
        c.start()
    for c in copies:
        c.wait()


def shares_call(weight, chips, cols, pair_cols):
    rows = weight.shape[0]
    count = 2 * len(chips)
    return pl.pallas_call(
        functools.partial(shares_kernel, chips, pair_cols),
        out_shape=[in_vmem((rows // 2, cols - pair_cols), BF), in_vmem((rows, pair_cols), BF)] * len(chips),
        in_specs=[pl.BlockSpec(memory_space=pltpu.HBM)],
        out_specs=whole_vmem(count),
        scratch_shapes=[pltpu.SemaphoreType.DMA((count,))],
        compiler_params=pltpu.CompilerParams(vmem_limit_bytes=VMEM),
        cost_estimate=SMALL,
        name="shares",
    )(*hbm([weight]))


def prepare_kernel(chips, head_cols, sizes, features, gain_map, tokens, core_tokens, cot, *refs):
    count, outs = len(sizes), len(sizes) + len(chips)
    normed, core_normed, gain, inv_rms = refs[count : count + 4]
    cut = refs[count + 4 : count + 4 + outs]
    map_in, tokens_in, core_in, sems = refs[count + 4 + outs :]
    r = lax.axis_index("rows")
    copies = [(tokens, tokens_in), (core_tokens, core_in), (gain_map, map_in)]
    for x, size, out in zip(refs, sizes, cut):
        copies.append((x.at[:, pl.ds(pl.multiple_of(r * size, 128), size)] if size else x, out))
    for j, out in zip(chips, cut[count:]):
        chip = lax.div(r ^ j, 2) * (2 * head_cols)
        copies.append((cot.at[:, pl.ds(pl.multiple_of(chip, 128), 2 * head_cols)], out))
    copies = [pltpu.make_async_copy(a, b, sems.at[i]) for i, (a, b) in enumerate(copies)]
    for c in copies:
        c.start()
    half = features.shape[1]
    col = features[...].T
    for c in copies[:3]:
        c.wait()
    total = jnp.sum(col[:, :1] * map_in[:half, :], 0, keepdims=True)
    total = total + jnp.sum(col[:, 1:] * map_in[half:, :], 0, keepdims=True)
    gain[...] = 1.0 + total
    for x, out in ((tokens_in, normed), (core_in, core_normed)):
        x = x[...].astype(F32)
        inv = lax.rsqrt(jnp.mean(x * x, -1, keepdims=True) + EPS)
        if out is normed:
            inv_rms[...] = inv
        out[...] = (x * inv * gain[...]).astype(BF)
    for c in copies[3:]:
        c.wait()


def prepare_call(features, gain_map, tokens, core_tokens, cot, chips, head_cols, arrays):
    tok, width = tokens.shape
    shapes = [((tok, width), BF), ((tok, width), BF), ((1, width), F32), ((tok, 1), F32)]
    shapes += [((x.shape[0], size or x.shape[1]), BF) for x, size in arrays]
    shapes += [((tok, 2 * head_cols), BF)] * len(chips)
    copies = 3 + len(arrays) + len(chips)
    return pl.pallas_call(
        functools.partial(prepare_kernel, chips, head_cols, [size for _, size in arrays]),
        out_shape=[in_vmem(*shape) for shape in shapes],
        in_specs=whole_vmem(1) + [pl.BlockSpec(memory_space=pl.ANY)] * (4 + len(arrays)),
        out_specs=whole_vmem(len(shapes)),
        scratch_shapes=[
            pltpu.VMEM(gain_map.shape, F32),
            pltpu.VMEM((tok, width), BF),
            pltpu.VMEM((tok, width), BF),
            pltpu.SemaphoreType.DMA((copies,)),
        ],
        compiler_params=pltpu.CompilerParams(vmem_limit_bytes=VMEM),
        cost_estimate=SMALL,
        name="prepare",
    )(features, gain_map, tokens, core_tokens, cot, *[x for x, _ in arrays])


def per_device(
    mesh_shape,
    tokens,
    timestep,
    timestep_gain_map,
    query_key_value_weight,
    adapter_down_weight,
    adapter_up_weight,
    head_score_scale,
    heads_output_grad,
):
    dp, n = mesh_shape
    axes = ("dp", "rows")
    r, d = lax.axis_index("rows"), lax.axis_index("dp")

    def send(x, target):
        perm = []
        for a in range(dp):
            for b in range(n):
                a2, b2 = target(a, b)
                perm.append((a * n + b, a2 * n + b2))
        return lax.ppermute(x, axes, perm)

    def to_row(x, j):
        return send(x, lambda a, b: (a, b ^ j))

    tok, width = tokens.shape
    weight, cot_all = query_key_value_weight, heads_output_grad
    k_rows = weight.shape[0]
    cols = weight.shape[1] // n
    head_cols = cot_all.shape[1] // n
    chips = list(range(2, n, 2))

    pair_cols = cols // 2 if cols % 256 == 0 else cols
    half = k_rows // 2
    pair, quad = [], []
    if pair_cols < cols:
        pieces = shares_call(weight, chips, cols, pair_cols)
        quad, pair = list(pieces[0::2]), list(pieces[1::2])
    else:
        pair = [lax.dynamic_slice(weight, (0, (r ^ (j + d // 2 % 2)) * cols), (k_rows, cols)) for j in chips]
    quad = [send(x, lambda a, b, j=j: (a, b ^ (j + a % 2))) for x, j in zip(quad, chips)]
    pair = [send(x, lambda a, b, j=j: (a, b ^ (j + a // 2 % 2))) for x, j in zip(pair, chips)]

    core_weight, core_tokens, core_cot = (to_row(x, 1) for x in (weight, tokens, cot_all))

    def mine(x, size):
        if size % 128 == 0 and x is weight:
            return hbm([x])[0], size
        return (x, size) if size % 128 == 0 else (lax.dynamic_slice(x, (0, r * size), (x.shape[0], size)), 0)

    own_map, own_tokens, own_cot = hbm([timestep_gain_map, tokens, cot_all])
    normed, core_normed, gain, inv_rms, own_w, core_w, own_cot, core_cot, *chip_cot = prepare_call(
        time_features(timestep), own_map, own_tokens, core_tokens, own_cot, chips, head_cols,
        [mine(weight, cols), mine(core_weight, cols), mine(cot_all, head_cols), mine(core_cot, head_cols)],
    )
    arrays = [own_w, core_w, normed, core_normed]
    w_from, x_from = [(0, 0, 0, 1, 0, 0), (1, 0, 1, 1, 0, 0)], [(2, tok), (3, tok)]
    def exchange(x, other):
        return send(x, lambda a, b: (a ^ other, b))

    early = []
    for j, x in zip(chips, quad):
        held = [x, exchange(x, 1), exchange(x, 2)]
        for other, x in enumerate(held):
            w_from.append((len(arrays), pair_cols, j, 4, other, 0))
            arrays.append(x)
        early.append(held[1])
        cut = (half * 3 // 4, half // 4)
        for at, x in zip((0, cut[0]), gate([held[2]], [cut])):
            early.append(exchange(x, 1))
            w_from.append((len(arrays), pair_cols, j, 4, 3, at))
            arrays.append(early[-1])
    for j, x in zip(chips, pair):
        w_from += [(len(arrays), 0, j, 2, 0, 0), (len(arrays) + 1, 0, j, 2, 1, 0)]
        arrays += [x, exchange(x, 2)]

    relay_rows = (tok * 5 // 8, tok * 3 // 8) if tok % 128 == 0 else (tok,)
    chip_normed = [to_row(normed, j) for j in chips]
    later = list(gate(chip_normed, [relay_rows] * len(chips), *early))
    for x in chip_normed:
        x_from.append((len(arrays), x.shape[0]))
        arrays.append(x)

    rank = adapter_up_weight.shape[0]
    down_t = adapter_down_weight.T
    up = adapter_up_weight
    if cols % 128:
        up = lax.dynamic_slice(up, (0, r * cols), (rank, cols))
    places, last_places = (0, 1, *chips), tuple(j + 1 for j in chips)
    first_x, w_all, first_qkv, first_low = qkv_call(
        n, arrays, tuple(x_from), tuple(w_from), down_t, up, len(places) * tok, cols
    )
    last_x, qkv_t, low_t = last_qkv_call(
        tok, places, last_places, [to_row(x, 1) for x in later], w_all, first_qkv, first_low, down_t, up
    )

    cots, c_from = [own_cot, core_cot], [(1, False), (1, False)]
    blocks = (tok * 3 // 4, tok // 4) if tok % 64 == 0 else (tok,)
    for j, x in zip(chips, chip_cot):
        x = to_row(x, j)
        c_from += [(1, True), (len(blocks), False)]
        cots += [x] + [to_row(y, 1) for y in other_half(x, blocks, first_low)]

    *others, grad_t, pack = attention_call(
        head_score_scale, cots, tuple(c_from), qkv_t, low_t, w_all, down_t, up, tok, 2, (F32, BF) * len(chips)
    )

    totals = [add(others[2 * i], to_row(others[2 * i + 1], 1)) for i in range(len(chips))]
    sums = [to_row(x, j) for x, j in zip(totals, chips)]
    packs = {0: pack, 1: to_row(pack, 1)}
    for j in chips:
        packs[j] = to_row(pack, j)
    blocks = (tok * 7 // 8, tok // 8) if tok % 128 == 0 else (tok,)
    mine, *core_part = own_call(grad_t, pack, w_all, down_t, tok, blocks, totals + [packs[j] for j in chips])
    core_part = [to_row(x, 1) for x in core_part]

    for j in chips:
        packs[j ^ 1] = to_row(packs[j], 1)
    down_grad_t, up_grad = adapter_call(
        [packs[j] for j in range(n)], first_x, last_x, (places, last_places), rank, n * cols, tok
    )

    input_grad = final_call(scale_call(tokens, gain, inv_rms, mine, core_part), sums)
    return (input_grad, down_grad_t.T, up_grad)


def solution(mesh):
    in_specs = (
        P(("dp", "rows"), None),
        P("dp"),
        P(),
        P("rows", None),
        P(),
        P(),
        P("rows"),
        P(("dp", "rows"), None),
    )
    out_specs = (P(("dp", "rows"), None), P("dp", None), P("dp", None))
    shape = (mesh.shape["dp"], mesh.shape["rows"])
    return jax.shard_map(
        functools.partial(per_device, shape), mesh=mesh, in_specs=in_specs, out_specs=out_specs, check_vma=False
    )
```

```python
import functools
import math

import jax
import jax.numpy as jnp
from jax import lax
from jax.experimental import pallas as pl
from jax.experimental.pallas import tpu as pltpu
from jax.sharding import PartitionSpec as P

HEAD = 64
EMB = 256
EPS = 1e-06
LOG2E = 1.4426950408889634
BF = jnp.bfloat16
F32 = jnp.float32
VMEM = 16 * 1024 * 1024
SMALL = pl.CostEstimate(flops=1, bytes_accessed=1, transcendentals=0)


def time_features(timestep):
    half_emb = EMB // 2
    frequency = jnp.exp(-math.log(10000.0) * jnp.arange(half_emb, dtype=F32) / half_emb)
    phases = timestep.astype(F32)[0] * frequency
    return jnp.stack([jnp.cos(phases), jnp.sin(phases)])


def contract(a, b, a_dim, b_dim):
    return lax.dot_general(a, b, (((a_dim,), (b_dim,)), ((), ())), preferred_element_type=F32)


def columns(x, size):
    if x.shape[1] == size:
        return x[...]
    return x[:, pl.ds(pl.multiple_of(lax.axis_index("rows") * size, 128), size)]


def multiply(x_all, w_all, down_t, up, put):
    seq = x_all.shape[0]
    step = math.gcd(512, seq) if seq > 512 else seq
    for s in range(0, seq, step):
        x = x_all[pl.ds(s, step), :]
        low = contract(x, down_t[...], 1, 1).astype(BF)
        qkv = jnp.dot(x, w_all[...], preferred_element_type=F32)
        qkv = qkv + 0.5 * jnp.dot(low, up, preferred_element_type=F32)
        put(s, step, qkv.astype(BF).T, low.T)


def qkv_kernel(n, x_from, w_from, *refs):
    down_t, up_in = refs[-6:-4]
    r, d = lax.axis_index("rows"), lax.axis_index("dp")
    up = columns(up_in, refs[-2].shape[0])
    x_all, w_all, qkv_t, low_t = refs[-4:]
    at = 0
    for i, rows in x_from:
        x_all[pl.ds(at, rows), :] = refs[i][...]
        at += rows
    for i, to, j, group, other, row in w_from:
        rows, cols = refs[i].shape
        holder, part = r ^ j, 0
        if group == 2:
            holder = r ^ (j + (lax.rem(lax.div(d, 2), 2) ^ other))
        elif group == 4:
            share = lax.rem(d, 4) ^ other
            holder, part = r ^ (j + lax.rem(share, 2)), lax.div(share, 2)
        held_rows = w_all.shape[0] // n
        base = pl.multiple_of(holder * held_rows + part * (held_rows // 2) + row, 16)
        w_all[pl.ds(base, rows), pl.ds(to, cols)] = refs[i][...]

    def put(start, rows, qkv, low):
        qkv_t[:, pl.ds(start, rows)] = qkv
        low_t[:, pl.ds(start, rows)] = low

    multiply(x_all, w_all, down_t, up, put)


def qkv_call(n, arrays, x_from, w_from, down_t, up, seq, cols):
    rank, width = down_t.shape
    return pl.pallas_call(
        functools.partial(qkv_kernel, n, x_from, w_from),
        out_shape=[
            in_vmem((seq, width), BF),
            in_vmem((width, cols), BF),
            in_vmem((cols, seq), BF),
            in_vmem((rank, seq), BF),
        ],
        in_specs=whole_vmem(len(arrays) + 2),
        out_specs=whole_vmem(4),
        compiler_params=pltpu.CompilerParams(vmem_limit_bytes=VMEM),
        cost_estimate=SMALL,
        name="qkv",
    )(*vmem(arrays), down_t, up)


def last_qkv_kernel(tok, places, last_places, *refs):
    w_all, first_qkv, first_low, down_t, up_in, x_all, qkv_t, low_t = refs[-8:]
    at = 0
    for x in refs[:-8]:
        rows = x.shape[0]
        x_all[pl.ds(at, rows), :] = x[...]
        at += rows
    for i, place in enumerate(places):
        qkv_t[:, pl.ds(place * tok, tok)] = first_qkv[:, pl.ds(i * tok, tok)]
        low_t[:, pl.ds(place * tok, tok)] = first_low[:, pl.ds(i * tok, tok)]

    def put(start, rows, qkv, low):
        for at in range(start, start + rows, tok):
            place = last_places[at // tok] * tok
            qkv_t[:, pl.ds(place, tok)] = qkv[:, at - start : at - start + tok]
            low_t[:, pl.ds(place, tok)] = low[:, at - start : at - start + tok]

    multiply(x_all, w_all, down_t, columns(up_in, qkv_t.shape[0]), put)


def last_qkv_call(tok, places, last_places, xs, w_all, first_qkv, first_low, down_t, up):
    rank, width = down_t.shape
    cols = w_all.shape[1]
    seq = (len(places) + len(last_places)) * tok
    return pl.pallas_call(
        functools.partial(last_qkv_kernel, tok, places, last_places),
        out_shape=[
            in_vmem((len(last_places) * tok, width), BF),
            in_vmem((cols, seq), BF),
            in_vmem((rank, seq), BF),
        ],
        in_specs=whole_vmem(len(xs) + 5),
        out_specs=whole_vmem(3),
        compiler_params=pltpu.CompilerParams(vmem_limit_bytes=VMEM),
        cost_estimate=SMALL,
        name="last_qkv",
    )(*vmem(xs), *vmem([w_all, first_qkv, first_low]), down_t, up)


def gate(xs, blocks, *deps):
    xs = [x if isinstance(x, list) else [x] for x in xs]
    flat = [(i, x) for i, parts in enumerate(xs) for x in parts]
    wanted = [(i, sum(sizes[:k]), rows) for i, sizes in enumerate(blocks) for k, rows in enumerate(sizes)]

    def kernel(*refs):
        outs = refs[len(flat) + len(deps) :]
        for (i, at, rows), out in zip(wanted, outs):
            start = 0
            for (owner, _), x in zip(flat, refs):
                if owner == i:
                    low, high = max(at, start), min(at + rows, start + x.shape[0])
                    if low < high:
                        out[pl.ds(low - at, high - low), :] = x[pl.ds(low - start, high - low), :]
                    start += x.shape[0]

    return pl.pallas_call(
        kernel,
        out_shape=[in_vmem((rows, xs[i][0].shape[1]), xs[i][0].dtype) for i, _, rows in wanted],
        in_specs=whole_vmem(len(flat) + len(deps)),
        out_specs=whole_vmem(len(wanted)),
        compiler_params=pltpu.CompilerParams(vmem_limit_bytes=VMEM),
        cost_estimate=SMALL,
        name="gate",
    )(*vmem([x for _, x in flat]), *vmem(deps))


def in_vmem(shape, dtype):
    return pltpu.VMEM(shape, dtype)


def vmem(xs):
    return [pltpu.with_memory_space_constraint(x, pltpu.VMEM) for x in xs]


def hbm(xs):
    return [pltpu.with_memory_space_constraint(x, pltpu.HBM) for x in xs]


def whole_vmem(count):
    return [pl.BlockSpec(memory_space=pltpu.VMEM)] * count


def qkv_call(n, arrays, x_from, w_from, down_t, up, seq, cols):
    rank, width = down_t.shape
    return pl.pallas_call(
        functools.partial(qkv_kernel, n, x_from, w_from),
        out_shape=[
            in_vmem((seq, width), BF),
            in_vmem((width, cols), BF),
            in_vmem((cols, seq), BF),
            in_vmem((rank, seq), BF),
        ],
        in_specs=whole_vmem(len(arrays) + 2),
        out_specs=whole_vmem(4),
        compiler_params=pltpu.CompilerParams(vmem_limit_bytes=VMEM),
        cost_estimate=SMALL,
        name="qkv",
    )(*vmem(arrays), down_t, up)


def token_grads(low_grad_t, grad_t, w_all, down_t, at, rows):
    low = contract(low_grad_t[:, pl.ds(at, rows)], down_t[...], 0, 0)
    return low + contract(grad_t[:, pl.ds(at, rows)], w_all[...], 0, 1)


def attention_kernel(heads, tok, c_from, first, outs, *refs):
    refs = list(refs)
    scale = refs.pop(0)
    cots = [[refs.pop(0) for _ in range(count)] for count, _ in c_from]
    qkv_t, low_t, w_all, down_t, up_in = (refs.pop(0) for _ in range(5))
    parts = [refs.pop(0) for _ in range(outs)]
    grad_t, pack, cot_t = refs

    cols, seq = qkv_t.shape
    up = columns(up_in, cols)
    step = math.gcd(512, seq)
    width = cot_t.shape[0]
    start = lax.rem(lax.axis_index("rows"), 2) * width
    for j, (blocks, (_, choose)) in enumerate(zip(cots, c_from)):
        if not choose:
            block = jnp.concatenate([x[...] for x in blocks], axis=0)
        elif width % 128 == 0:
            block = blocks[0][:, pl.ds(pl.multiple_of(start, 128), width)]
        else:
            block = jnp.where(start == 0, blocks[0][:, pl.ds(0, width)], blocks[0][:, pl.ds(width, width)])
        cot_t[:, pl.ds(j * tok, tok)] = block.T

    for h in range(heads):
        o = 3 * HEAD * h
        kf = qkv_t[pl.ds(o + HEAD, HEAD), :].astype(F32)
        k_inv = lax.rsqrt(jnp.sum(kf * kf, 0, keepdims=True) + EPS)
        k_unit = kf * k_inv
        k_low = k_unit.astype(BF)
        v = qkv_t[pl.ds(o + 2 * HEAD, HEAD), :]
        sc = scale[h]
        gk = gv = None
        for s in range(0, seq, step):
            qf = qkv_t[pl.ds(o, HEAD), pl.ds(s, step)].astype(F32)
            q_inv = lax.rsqrt(jnp.sum(qf * qf, 0, keepdims=True) + EPS)
            q_unit = qf * q_inv
            q_low = q_unit.astype(BF)
            g = cot_t[pl.ds(HEAD * h, HEAD), pl.ds(s, step)]
            e = jnp.exp2(contract(k_low, q_low, 0, 0) * (sc * LOG2E))
            share = 1.0 / jnp.sum(e, 0, keepdims=True)
            grad_probs = contract(v, g, 0, 0)
            delta = jnp.sum(e * grad_probs, 0, keepdims=True) * share
            attention = e * share
            grad_scores = (attention * (grad_probs - delta)).astype(BF)
            gv_s = jnp.dot(attention.astype(BF), g.T, preferred_element_type=F32)
            gk_s = jnp.dot(grad_scores, q_low.T, preferred_element_type=F32)
            gq = sc * jnp.dot(k_low, grad_scores, preferred_element_type=F32)
            gq = q_inv * (gq - q_unit * jnp.sum(q_unit * gq, 0, keepdims=True))
            grad_t[pl.ds(o, HEAD), pl.ds(s, step)] = gq.astype(BF)
            gv = gv_s if gv is None else gv + gv_s
            gk = gk_s if gk is None else gk + gk_s
        gk = sc * gk.T
        gk = k_inv * (gk - k_unit * jnp.sum(k_unit * gk, 0, keepdims=True))
        grad_t[pl.ds(o + HEAD, HEAD), :] = gk.astype(BF)
        grad_t[pl.ds(o + 2 * HEAD, HEAD), :] = gv.astype(BF).T

    rank = up.shape[0]
    pack[:, pl.ds(seq, cols)] = (0.5 * contract(low_t[...], grad_t[...], 1, 1)).astype(BF)
    low_grad_t = pack.at[:, pl.ds(0, seq)]
    low_grad_t[...] = (0.5 * jnp.dot(up, grad_t[...], preferred_element_type=F32)).astype(BF)
    for p in range(0, outs, 4):
        count = min(4, outs - p)
        part = token_grads(low_grad_t, grad_t, w_all, down_t, (first + p) * tok, count * tok)
        for i in range(count):
            out = parts[p + i]
            out[...] = part[i * tok : (i + 1) * tok].astype(out.dtype)


def attention_call(scale, cots, c_from, qkv_t, low_t, w_all, down_t, up, tok, first, dtypes):
    cols, seq = qkv_t.shape
    rank, width = down_t.shape
    smem = pl.BlockSpec(memory_space=pltpu.SMEM)
    outs = len(dtypes)
    return pl.pallas_call(
        functools.partial(attention_kernel, cols // (3 * HEAD), tok, c_from, first, outs),
        out_shape=[in_vmem((tok, width), t) for t in dtypes]
        + [in_vmem((cols, seq), BF), in_vmem((rank, seq + cols), BF)],
        in_specs=[smem] + whole_vmem(len(cots) + 5),
        out_specs=whole_vmem(outs + 2),
        scratch_shapes=[pltpu.VMEM((cols // 3, seq), BF)],
        compiler_params=pltpu.CompilerParams(vmem_limit_bytes=VMEM),
        cost_estimate=SMALL,
        name="attention_grads",
    )(scale, *vmem(cots), qkv_t, low_t, w_all, down_t, up)


def other_half(x, blocks, dep):
    half = x.shape[1] // 2
    starts = [sum(blocks[:i]) for i in range(len(blocks))]
    if half % 128:
        col = (lax.axis_index("rows") ^ 1) % 2 * half
        return [lax.dynamic_slice(x, (at, col), (rows, half)) for at, rows in zip(starts, blocks)]

    def kernel(x, dep, *outs):
        core = lax.rem(lax.axis_index("rows") ^ 1, 2)
        for at, rows, out in zip(starts, blocks, outs):
            out[...] = x[pl.ds(at, rows), pl.ds(pl.multiple_of(core * half, 128), half)]

    return pl.pallas_call(
        kernel,
        out_shape=[in_vmem((rows, half), x.dtype) for rows in blocks],
        in_specs=whole_vmem(2),
        out_specs=whole_vmem(len(blocks)),
        compiler_params=pltpu.CompilerParams(vmem_limit_bytes=VMEM),
        cost_estimate=SMALL,
        name="other_half",
    )(*vmem([x, dep]))


def add(a, b):
    def kernel(a, b, out):
        out[...] = (a[...] + b[...].astype(F32)).astype(BF)

    return pl.pallas_call(
        kernel,
        out_shape=in_vmem(a.shape, BF),
        in_specs=whole_vmem(2),
        out_specs=whole_vmem(1)[0],
        compiler_params=pltpu.CompilerParams(vmem_limit_bytes=VMEM),
        cost_estimate=SMALL,
        name="add",
    )(*vmem([a, b]))


def own_kernel(deps, grad_t, pack, w_all, down_t, *refs):
    mine, rest = refs[deps], refs[deps + 1 :]
    tok = mine.shape[0]
    part = token_grads(pack, grad_t, w_all, down_t, 0, 2 * tok)
    mine[...] = part[:tok]
    part = part[tok:].astype(BF)
    at = 0
    for out in rest:
        out[...] = part[at : at + out.shape[0]]
        at += out.shape[0]


def own_call(grad_t, pack, w_all, down_t, tok, blocks, deps):
    width = down_t.shape[1]
    return pl.pallas_call(
        functools.partial(own_kernel, len(deps)),
        out_shape=[in_vmem((tok, width), F32)] + [in_vmem((rows, width), BF) for rows in blocks],
        in_specs=whole_vmem(4 + len(deps)),
        out_specs=whole_vmem(1 + len(blocks)),
        compiler_params=pltpu.CompilerParams(vmem_limit_bytes=VMEM),
        cost_estimate=SMALL,
        name="own_grads",
    )(grad_t, pack, w_all, down_t, *vmem(deps))


def adapter_kernel(tok, places, *refs):
    packs, (first_x, last_x, down_grad_t, up_grad) = refs[:-4], refs[-4:]
    r = lax.axis_index("rows")
    total = None
    for j, pack in enumerate(packs):
        blocks = [pack[:, pl.ds((q ^ j) * tok, tok)] for q in range(len(packs))]
        term = jnp.concatenate(blocks, axis=1).astype(F32)
        total = term if total is None else total + term
    total = total.astype(BF)
    grad = None
    for x, held in zip((first_x, last_x), places):
        part = jnp.concatenate([total[:, p * tok : (p + 1) * tok] for p in held], axis=1)
        term = jnp.dot(part, x[...], preferred_element_type=F32)
        grad = term if grad is None else grad + term
    down_grad_t[...] = grad
    cols = up_grad.shape[1] // len(packs)
    for j, pack in enumerate(packs):
        if cols % 128 == 0:
            up_grad[:, pl.ds(pl.multiple_of((r ^ j) * cols, 128), cols)] = pack[:, pl.ds(len(packs) * tok, cols)].astype(F32)


def adapter_call(packs, first_x, last_x, places, rank, all_cols, tok):
    down_grad_t, up_grad = pl.pallas_call(
        functools.partial(adapter_kernel, tok, places),
        out_shape=[
            jax.ShapeDtypeStruct((rank, first_x.shape[1]), F32),
            jax.ShapeDtypeStruct((rank, all_cols), F32),
        ],
        in_specs=whole_vmem(len(packs) + 2),
        out_specs=whole_vmem(2),
        compiler_params=pltpu.CompilerParams(vmem_limit_bytes=VMEM),
        cost_estimate=SMALL,
        name="adapter_grads",
    )(*vmem(packs), *vmem([first_x, last_x]))
    cols = all_cols // len(packs)
    if cols % 128:
        for j, pack in enumerate(packs):
            up_grad = lax.dynamic_update_slice(up_grad, pack[:, len(packs) * tok :].astype(F32), (0, (lax.axis_index("rows") ^ j) * cols))
    return down_grad_t, up_grad


def scale_kernel(tokens, gain, inv_rms, mine, *refs):
    blocks, (total, token_gain, scale, slope) = refs[:-4], refs[-4:]
    at = 0
    for block in blocks:
        rows = pl.ds(at, block.shape[0])
        total[rows, :] = mine[rows, :] + block[...].astype(F32)
        at += block.shape[0]
    x = tokens[...].astype(F32)
    inv = inv_rms[...]
    token_gain[...] = x * gain[...]
    scale[...] = inv * gain[...]
    slope[...] = x * (inv * inv * inv * (1.0 / x.shape[1]))


def scale_call(tokens, gain, inv_rms, mine, blocks):
    return pl.pallas_call(
        scale_kernel,
        out_shape=[in_vmem(tokens.shape, F32)] * 4,
        in_specs=whole_vmem(4 + len(blocks)),
        out_specs=whole_vmem(4),
        compiler_params=pltpu.CompilerParams(vmem_limit_bytes=VMEM),
        cost_estimate=SMALL,
        name="scale",
    )(tokens, gain, inv_rms, mine, *vmem(blocks))


def final_kernel(total, token_gain, scale, slope, *refs):
    terms, (out, made, sems) = refs[:-3], refs[-3:]
    count = sems.shape[0]
    rows = made.shape[0] // count
    copies = []
    for i in range(count):
        block = pl.ds(i * rows, rows)
        grad = total[block, :]
        for x in terms:
            grad = grad + x[block, :].astype(F32)
        moment = jnp.sum(grad * token_gain[block, :], -1, keepdims=True)
        made[block, :] = (grad * scale[block, :] - slope[block, :] * moment).astype(BF)
        copies.append(pltpu.make_async_copy(made.at[block], out.at[block], sems.at[i]))
        copies[-1].start()
    for c in copies:
        c.wait()


def final_call(held, terms):
    shape = held[0].shape
    count = 4 if shape[0] % 64 == 0 else 1
    return pl.pallas_call(
        final_kernel,
        out_shape=jax.ShapeDtypeStruct(shape, BF),
        in_specs=whole_vmem(4 + len(terms)),
        out_specs=pl.BlockSpec(memory_space=pltpu.HBM),
        scratch_shapes=[pltpu.VMEM(shape, BF), pltpu.SemaphoreType.DMA((count,))],
        compiler_params=pltpu.CompilerParams(vmem_limit_bytes=VMEM),
        cost_estimate=SMALL,
        name="input_grads",
    )(*vmem(held), *vmem(terms))


def shares_kernel(chips, pair_cols, weight, *refs):
    r, d = lax.axis_index("rows"), lax.axis_index("dp")
    outs, sems = refs[:-1], refs[-1]
    cols = pair_cols + outs[0].shape[1]
    copies = []
    for i, j in enumerate(chips):
        half = outs[2 * i].shape[0]
        row = pl.multiple_of(lax.div(lax.rem(d, 4), 2) * half, 16)
        col = pl.multiple_of((r ^ (j + lax.rem(d, 2))) * cols + pair_cols, 128)
        copies.append((weight.at[pl.ds(row, half), pl.ds(col, cols - pair_cols)], outs[2 * i]))
        col = pl.multiple_of((r ^ (j + lax.rem(lax.div(d, 2), 2))) * cols, 128)
        copies.append((weight.at[:, pl.ds(col, pair_cols)], outs[2 * i + 1]))
    copies = [pltpu.make_async_copy(a, b, sems.at[i]) for i, (a, b) in enumerate(copies)]
    for c in copies:
        c.start()
    for c in copies:
        c.wait()


def shares_call(weight, chips, cols, pair_cols):
    rows = weight.shape[0]
    count = 2 * len(chips)
    return pl.pallas_call(
        functools.partial(shares_kernel, chips, pair_cols),
        out_shape=[in_vmem((rows // 2, cols - pair_cols), BF), in_vmem((rows, pair_cols), BF)] * len(chips),
        in_specs=[pl.BlockSpec(memory_space=pltpu.HBM)],
        out_specs=whole_vmem(count),
        scratch_shapes=[pltpu.SemaphoreType.DMA((count,))],
        compiler_params=pltpu.CompilerParams(vmem_limit_bytes=VMEM),
        cost_estimate=SMALL,
        name="shares",
    )(*hbm([weight]))


def own_columns(weight, cols):
    def kernel(x, out, sem):
        start = pl.multiple_of(lax.axis_index("rows") * cols, 128)
        copy = pltpu.make_async_copy(x.at[:, pl.ds(start, cols)], out, sem)
        copy.start()
        copy.wait()

    return pl.pallas_call(
        kernel,
        out_shape=in_vmem((weight.shape[0], cols), BF),
        in_specs=[pl.BlockSpec(memory_space=pltpu.HBM)],
        out_specs=whole_vmem(1)[0],
        scratch_shapes=[pltpu.SemaphoreType.DMA],
        compiler_params=pltpu.CompilerParams(vmem_limit_bytes=VMEM),
        cost_estimate=SMALL,
        name="own_columns",
    )(*hbm([weight]))


def prepare_kernel(chips, head_cols, sizes, features, gain_map, tokens, core_tokens, cot, *refs):
    count, outs = len(sizes), len(sizes) + len(chips)
    normed, core_normed, gain, inv_rms = refs[count : count + 4]
    cut = refs[count + 4 : count + 4 + outs]
    map_in, tokens_in, core_in, sems = refs[count + 4 + outs :]
    r = lax.axis_index("rows")
    half = features.shape[1]
    copies = [(tokens, tokens_in), (core_tokens, core_in)]
    copies += [(gain_map.at[pl.ds(at, half)], map_in.at[pl.ds(at, half)]) for at in (0, half)]
    for x, size, out in zip(refs, sizes, cut):
        copies.append((x.at[:, pl.ds(pl.multiple_of(r * size, 128), size)] if size else x, out))
    for j, out in zip(chips, cut[count:]):
        chip = lax.div(r ^ j, 2) * (2 * head_cols)
        copies.append((cot.at[:, pl.ds(pl.multiple_of(chip, 128), 2 * head_cols)], out))
    copies = [pltpu.make_async_copy(a, b, sems.at[i]) for i, (a, b) in enumerate(copies)]
    for c in copies:
        c.start()
    col = features[...].T
    held = []
    for c, x in zip(copies[:2], (tokens_in, core_in)):
        c.wait()
        x = x[...].astype(F32)
        held.append(lax.rsqrt(jnp.mean(x * x, -1, keepdims=True) + EPS))
    inv_rms[...] = held[0]
    copies[2].wait()
    total = jnp.sum(col[:, :1] * map_in[:half, :], 0, keepdims=True)
    copies[3].wait()
    total = total + jnp.sum(col[:, 1:] * map_in[half:, :], 0, keepdims=True)
    gain[...] = 1.0 + total
    for x, inv, out in ((tokens_in, held[0], normed), (core_in, held[1], core_normed)):
        out[...] = (x[...].astype(F32) * inv * gain[...]).astype(BF)
    for c in copies[4:]:
        c.wait()


def prepare_call(features, gain_map, tokens, core_tokens, cot, chips, head_cols, arrays):
    tok, width = tokens.shape
    shapes = [((tok, width), BF), ((tok, width), BF), ((1, width), F32), ((tok, 1), F32)]
    shapes += [((x.shape[0], size or x.shape[1]), BF) for x, size in arrays]
    shapes += [((tok, 2 * head_cols), BF)] * len(chips)
    copies = 4 + len(arrays) + len(chips)
    return pl.pallas_call(
        functools.partial(prepare_kernel, chips, head_cols, [size for _, size in arrays]),
        out_shape=[in_vmem(*shape) for shape in shapes],
        in_specs=whole_vmem(1) + [pl.BlockSpec(memory_space=pl.ANY)] * (4 + len(arrays)),
        out_specs=whole_vmem(len(shapes)),
        scratch_shapes=[
            pltpu.VMEM(gain_map.shape, F32),
            pltpu.VMEM((tok, width), BF),
            pltpu.VMEM((tok, width), BF),
            pltpu.SemaphoreType.DMA((copies,)),
        ],
        compiler_params=pltpu.CompilerParams(vmem_limit_bytes=VMEM),
        cost_estimate=SMALL,
        name="prepare",
    )(features, gain_map, tokens, core_tokens, cot, *[x for x, _ in arrays])


def per_device(
    mesh_shape,
    tokens,
    timestep,
    timestep_gain_map,
    query_key_value_weight,
    adapter_down_weight,
    adapter_up_weight,
    head_score_scale,
    heads_output_grad,
):
    dp, n = mesh_shape
    axes = ("dp", "rows")
    r, d = lax.axis_index("rows"), lax.axis_index("dp")

    def send(x, target):
        perm = []
        for a in range(dp):
            for b in range(n):
                a2, b2 = target(a, b)
                perm.append((a * n + b, a2 * n + b2))
        return lax.ppermute(x, axes, perm)

    def to_row(x, j):
        return send(x, lambda a, b: (a, b ^ j))

    tok, width = tokens.shape
    weight, cot_all = query_key_value_weight, heads_output_grad
    k_rows = weight.shape[0]
    cols = weight.shape[1] // n
    head_cols = cot_all.shape[1] // n
    chips = list(range(2, n, 2))

    pair_cols = cols // 2 if cols % 256 == 0 else cols
    half = k_rows // 2
    pair, quad = [], []
    if pair_cols < cols:
        pieces = shares_call(weight, chips, cols, pair_cols)
        quad, pair = list(pieces[0::2]), list(pieces[1::2])
    else:
        pair = [lax.dynamic_slice(weight, (0, (r ^ (j + d // 2 % 2)) * cols), (k_rows, cols)) for j in chips]
    quad = [send(x, lambda a, b, j=j: (a, b ^ (j + a % 2))) for x, j in zip(quad, chips)]
    pair = [send(x, lambda a, b, j=j: (a, b ^ (j + a // 2 % 2))) for x, j in zip(pair, chips)]

    core_weight, core_tokens, core_cot = (to_row(x, 1) for x in (weight, tokens, cot_all))

    def mine(x, size):
        if size % 128 == 0 and x is weight:
            return hbm([x])[0], size
        return (x, size) if size % 128 == 0 else (lax.dynamic_slice(x, (0, r * size), (x.shape[0], size)), 0)

    own_map, own_tokens, own_cot = hbm([timestep_gain_map, tokens, cot_all])
    normed, core_normed, gain, inv_rms, core_w, own_cot, core_cot, *chip_cot = prepare_call(
        time_features(timestep), own_map, own_tokens, core_tokens, own_cot, chips, head_cols,
        [mine(core_weight, cols), mine(cot_all, head_cols), mine(core_cot, head_cols)],
    )
    own_w = own_columns(weight, cols) if cols % 128 == 0 else mine(weight, cols)[0]
    arrays = [own_w, core_w, normed, core_normed]
    w_from, x_from = [(0, 0, 0, 1, 0, 0), (1, 0, 1, 1, 0, 0)], [(2, tok), (3, tok)]
    def exchange(x, other):
        return send(x, lambda a, b: (a ^ other, b))

    early = []
    for j, x in zip(chips, quad):
        held = [x, exchange(x, 1), exchange(x, 2)]
        for other, x in enumerate(held):
            w_from.append((len(arrays), pair_cols, j, 4, other, 0))
            arrays.append(x)
        early.append(held[1])
        cut = (half * 3 // 4, half // 4)
        for at, x in zip((0, cut[0]), gate([held[2]], [cut])):
            early.append(exchange(x, 1))
            w_from.append((len(arrays), pair_cols, j, 4, 3, at))
            arrays.append(early[-1])
    for j, x in zip(chips, pair):
        w_from += [(len(arrays), 0, j, 2, 0, 0), (len(arrays) + 1, 0, j, 2, 1, 0)]
        arrays += [x, exchange(x, 2)]

    relay_rows = (tok * 5 // 8, tok * 3 // 8) if tok % 128 == 0 else (tok,)
    chip_normed = [to_row(normed, j) for j in chips]
    later = list(gate(chip_normed, [relay_rows] * len(chips), *early, own_w))
    for x in chip_normed:
        x_from.append((len(arrays), x.shape[0]))
        arrays.append(x)

    rank = adapter_up_weight.shape[0]
    down_t = adapter_down_weight.T
    up = adapter_up_weight
    if cols % 128:
        up = lax.dynamic_slice(up, (0, r * cols), (rank, cols))
    places, last_places = (0, 1, *chips), tuple(j + 1 for j in chips)
    first_x, w_all, first_qkv, first_low = qkv_call(
        n, arrays, tuple(x_from), tuple(w_from), down_t, up, len(places) * tok, cols
    )
    last_x, qkv_t, low_t = last_qkv_call(
        tok, places, last_places, [to_row(x, 1) for x in later], w_all, first_qkv, first_low, down_t, up
    )

    cots, c_from = [own_cot, core_cot], [(1, False), (1, False)]
    blocks = (tok * 3 // 4, tok // 4) if tok % 64 == 0 else (tok,)
    for j, x in zip(chips, chip_cot):
        x = to_row(x, j)
        c_from += [(1, True), (len(blocks), False)]
        cots += [x] + [to_row(y, 1) for y in other_half(x, blocks, first_low)]

    *others, grad_t, pack = attention_call(
        head_score_scale, cots, tuple(c_from), qkv_t, low_t, w_all, down_t, up, tok, 2, (F32, BF) * len(chips)
    )

    totals = [add(others[2 * i], to_row(others[2 * i + 1], 1)) for i in range(len(chips))]
    sums = [to_row(x, j) for x, j in zip(totals, chips)]
    packs = {0: pack, 1: to_row(pack, 1)}
    for j in chips:
        packs[j] = to_row(pack, j)
    blocks = (tok * 7 // 8, tok // 8) if tok % 128 == 0 else (tok,)
    mine, *core_part = own_call(grad_t, pack, w_all, down_t, tok, blocks, totals + [packs[j] for j in chips])
    core_part = [to_row(x, 1) for x in core_part]

    for j in chips:
        packs[j ^ 1] = to_row(packs[j], 1)
    down_grad_t, up_grad = adapter_call(
        [packs[j] for j in range(n)], first_x, last_x, (places, last_places), rank, n * cols, tok
    )

    input_grad = final_call(scale_call(tokens, gain, inv_rms, mine, core_part), sums)
    return (input_grad, down_grad_t.T, up_grad)


def solution(mesh):
    in_specs = (
        P(("dp", "rows"), None),
        P("dp"),
        P(),
        P("rows", None),
        P(),
        P(),
        P("rows"),
        P(("dp", "rows"), None),
    )
    out_specs = (P(("dp", "rows"), None), P("dp", None), P("dp", None))
    shape = (mesh.shape["dp"], mesh.shape["rows"])
    return jax.shard_map(
        functools.partial(per_device, shape), mesh=mesh, in_specs=in_specs, out_specs=out_specs, check_vma=False
    )
```

```python
import functools
import math

import jax
import jax.numpy as jnp
from jax import lax
from jax.experimental import pallas as pl
from jax.experimental.pallas import tpu as pltpu
from jax.sharding import PartitionSpec as P

HEAD = 64
EMB = 256
EPS = 1e-06
LOG2E = 1.4426950408889634
BF = jnp.bfloat16
F32 = jnp.float32
VMEM = 16 * 1024 * 1024
SMALL = pl.CostEstimate(flops=1, bytes_accessed=1, transcendentals=0)


def time_features(timestep):
    half_emb = EMB // 2
    frequency = jnp.exp(-math.log(10000.0) * jnp.arange(half_emb, dtype=F32) / half_emb)
    phases = timestep.astype(F32)[0] * frequency
    return jnp.stack([jnp.cos(phases), jnp.sin(phases)])


def contract(a, b, a_dim, b_dim):
    return lax.dot_general(a, b, (((a_dim,), (b_dim,)), ((), ())), preferred_element_type=F32)


def columns(x, size):
    if x.shape[1] == size:
        return x[...]
    return x[:, pl.ds(pl.multiple_of(lax.axis_index("rows") * size, 128), size)]


def multiply(x_all, w_all, down_t, up, put):
    seq = x_all.shape[0]
    step = math.gcd(512, seq) if seq > 512 else seq
    for s in range(0, seq, step):
        x = x_all[pl.ds(s, step), :]
        low = contract(x, down_t[...], 1, 1).astype(BF)
        qkv = jnp.dot(x, w_all[...], preferred_element_type=F32)
        qkv = qkv + 0.5 * jnp.dot(low, up, preferred_element_type=F32)
        put(s, step, qkv.astype(BF).T, low.T)


def qkv_kernel(n, x_from, w_from, *refs):
    down_t, up_in = refs[-6:-4]
    r, d = lax.axis_index("rows"), lax.axis_index("dp")
    up = columns(up_in, refs[-2].shape[0])
    x_all, w_all, qkv_t, low_t = refs[-4:]
    at = 0
    for i, rows in x_from:
        x_all[pl.ds(at, rows), :] = refs[i][...]
        at += rows
    for i, to, j, group, other, row in w_from:
        rows, cols = refs[i].shape
        holder, part = r ^ j, 0
        if group == 2:
            holder = r ^ (j + (lax.rem(lax.div(d, 2), 2) ^ other))
        elif group == 4:
            share = lax.rem(d, 4) ^ other
            holder, part = r ^ (j + lax.rem(share, 2)), lax.div(share, 2)
        held_rows = w_all.shape[0] // n
        base = pl.multiple_of(holder * held_rows + part * (held_rows // 2) + row, 16)
        w_all[pl.ds(base, rows), pl.ds(to, cols)] = refs[i][...]

    def put(start, rows, qkv, low):
        qkv_t[:, pl.ds(start, rows)] = qkv
        low_t[:, pl.ds(start, rows)] = low

    multiply(x_all, w_all, down_t, up, put)


def qkv_call(n, arrays, x_from, w_from, down_t, up, seq, cols):
    rank, width = down_t.shape
    return pl.pallas_call(
        functools.partial(qkv_kernel, n, x_from, w_from),
        out_shape=[
            in_vmem((seq, width), BF),
            in_vmem((width, cols), BF),
            in_vmem((cols, seq), BF),
            in_vmem((rank, seq), BF),
        ],
        in_specs=whole_vmem(len(arrays) + 2),
        out_specs=whole_vmem(4),
        compiler_params=pltpu.CompilerParams(vmem_limit_bytes=VMEM),
        cost_estimate=SMALL,
        name="qkv",
    )(*vmem(arrays), down_t, up)


def last_qkv_kernel(tok, places, last_places, *refs):
    w_all, first_qkv, first_low, down_t, up_in, x_all, qkv_t, low_t = refs[-8:]
    at = 0
    for x in refs[:-8]:
        rows = x.shape[0]
        x_all[pl.ds(at, rows), :] = x[...]
        at += rows
    for i, place in enumerate(places):
        qkv_t[:, pl.ds(place * tok, tok)] = first_qkv[:, pl.ds(i * tok, tok)]
        low_t[:, pl.ds(place * tok, tok)] = first_low[:, pl.ds(i * tok, tok)]

    def put(start, rows, qkv, low):
        for at in range(start, start + rows, tok):
            place = last_places[at // tok] * tok
            qkv_t[:, pl.ds(place, tok)] = qkv[:, at - start : at - start + tok]
            low_t[:, pl.ds(place, tok)] = low[:, at - start : at - start + tok]

    multiply(x_all, w_all, down_t, columns(up_in, qkv_t.shape[0]), put)


def last_qkv_call(tok, places, last_places, xs, w_all, first_qkv, first_low, down_t, up):
    rank, width = down_t.shape
    cols = w_all.shape[1]
    seq = (len(places) + len(last_places)) * tok
    return pl.pallas_call(
        functools.partial(last_qkv_kernel, tok, places, last_places),
        out_shape=[
            in_vmem((len(last_places) * tok, width), BF),
            in_vmem((cols, seq), BF),
            in_vmem((rank, seq), BF),
        ],
        in_specs=whole_vmem(len(xs) + 5),
        out_specs=whole_vmem(3),
        compiler_params=pltpu.CompilerParams(vmem_limit_bytes=VMEM),
        cost_estimate=SMALL,
        name="last_qkv",
    )(*vmem(xs), *vmem([w_all, first_qkv, first_low]), down_t, up)


def gate(xs, blocks, *deps):
    xs = [x if isinstance(x, list) else [x] for x in xs]
    flat = [(i, x) for i, parts in enumerate(xs) for x in parts]
    wanted = [(i, sum(sizes[:k]), rows) for i, sizes in enumerate(blocks) for k, rows in enumerate(sizes)]

    def kernel(*refs):
        outs = refs[len(flat) + len(deps) :]
        for (i, at, rows), out in zip(wanted, outs):
            start = 0
            for (owner, _), x in zip(flat, refs):
                if owner == i:
                    low, high = max(at, start), min(at + rows, start + x.shape[0])
                    if low < high:
                        out[pl.ds(low - at, high - low), :] = x[pl.ds(low - start, high - low), :]
                    start += x.shape[0]

    return pl.pallas_call(
        kernel,
        out_shape=[in_vmem((rows, xs[i][0].shape[1]), xs[i][0].dtype) for i, _, rows in wanted],
        in_specs=whole_vmem(len(flat) + len(deps)),
        out_specs=whole_vmem(len(wanted)),
        compiler_params=pltpu.CompilerParams(vmem_limit_bytes=VMEM),
        cost_estimate=SMALL,
        name="gate",
    )(*vmem([x for _, x in flat]), *vmem(deps))


def in_vmem(shape, dtype):
    return pltpu.VMEM(shape, dtype)


def vmem(xs):
    return [pltpu.with_memory_space_constraint(x, pltpu.VMEM) for x in xs]


def hbm(xs):
    return [pltpu.with_memory_space_constraint(x, pltpu.HBM) for x in xs]


def whole_vmem(count):
    return [pl.BlockSpec(memory_space=pltpu.VMEM)] * count


def qkv_call(n, arrays, x_from, w_from, down_t, up, seq, cols):
    rank, width = down_t.shape
    return pl.pallas_call(
        functools.partial(qkv_kernel, n, x_from, w_from),
        out_shape=[
            in_vmem((seq, width), BF),
            in_vmem((width, cols), BF),
            in_vmem((cols, seq), BF),
            in_vmem((rank, seq), BF),
        ],
        in_specs=whole_vmem(len(arrays) + 2),
        out_specs=whole_vmem(4),
        compiler_params=pltpu.CompilerParams(vmem_limit_bytes=VMEM),
        cost_estimate=SMALL,
        name="qkv",
    )(*vmem(arrays), down_t, up)


def token_grads(low_grad_t, grad_t, w_all, down_t, at, rows):
    low = contract(low_grad_t[:, pl.ds(at, rows)], down_t[...], 0, 0)
    return low + contract(grad_t[:, pl.ds(at, rows)], w_all[...], 0, 1)


def attention_kernel(heads, tok, c_from, first, outs, *refs):
    refs = list(refs)
    scale = refs.pop(0)
    cots = [[refs.pop(0) for _ in range(count)] for count, _ in c_from]
    qkv_t, low_t, w_all, down_t, up_in = (refs.pop(0) for _ in range(5))
    parts = [refs.pop(0) for _ in range(outs)]
    grad_t, pack, cot_t = refs

    cols, seq = qkv_t.shape
    up = columns(up_in, cols)
    step = math.gcd(512, seq)
    width = cot_t.shape[0]
    start = lax.rem(lax.axis_index("rows"), 2) * width
    for j, (blocks, (_, choose)) in enumerate(zip(cots, c_from)):
        if not choose:
            block = jnp.concatenate([x[...] for x in blocks], axis=0)
        elif width % 128 == 0:
            block = blocks[0][:, pl.ds(pl.multiple_of(start, 128), width)]
        else:
            block = jnp.where(start == 0, blocks[0][:, pl.ds(0, width)], blocks[0][:, pl.ds(width, width)])
        cot_t[:, pl.ds(j * tok, tok)] = block.T

    for h in range(heads):
        o = 3 * HEAD * h
        kf = qkv_t[pl.ds(o + HEAD, HEAD), :].astype(F32)
        k_inv = lax.rsqrt(jnp.sum(kf * kf, 0, keepdims=True) + EPS)
        k_unit = kf * k_inv
        k_low = k_unit.astype(BF)
        v = qkv_t[pl.ds(o + 2 * HEAD, HEAD), :]
        sc = scale[h]
        gk = gv = None
        for s in range(0, seq, step):
            qf = qkv_t[pl.ds(o, HEAD), pl.ds(s, step)].astype(F32)
            q_inv = lax.rsqrt(jnp.sum(qf * qf, 0, keepdims=True) + EPS)
            q_unit = qf * q_inv
            q_low = q_unit.astype(BF)
            g = cot_t[pl.ds(HEAD * h, HEAD), pl.ds(s, step)]
            e = jnp.exp2(contract(k_low, q_low, 0, 0) * (sc * LOG2E))
            share = 1.0 / jnp.sum(e, 0, keepdims=True)
            grad_probs = contract(v, g, 0, 0)
            delta = jnp.sum(e * grad_probs, 0, keepdims=True) * share
            attention = e * share
            grad_scores = (attention * (grad_probs - delta)).astype(BF)
            gv_s = contract(attention.astype(BF), g, 1, 1)
            gk_s = contract(grad_scores, q_low, 1, 1)
            gq = sc * jnp.dot(k_low, grad_scores, preferred_element_type=F32)
            gq = q_inv * (gq - q_unit * jnp.sum(q_unit * gq, 0, keepdims=True))
            grad_t[pl.ds(o, HEAD), pl.ds(s, step)] = gq.astype(BF)
            gv = gv_s if gv is None else gv + gv_s
            gk = gk_s if gk is None else gk + gk_s
        gk = sc * gk.T
        gk = k_inv * (gk - k_unit * jnp.sum(k_unit * gk, 0, keepdims=True))
        grad_t[pl.ds(o + HEAD, HEAD), :] = gk.astype(BF)
        grad_t[pl.ds(o + 2 * HEAD, HEAD), :] = gv.astype(BF).T

    rank = up.shape[0]
    pack[:, pl.ds(seq, cols)] = (0.5 * contract(low_t[...], grad_t[...], 1, 1)).astype(BF)
    low_grad_t = pack.at[:, pl.ds(0, seq)]
    low_grad_t[...] = (0.5 * jnp.dot(up, grad_t[...], preferred_element_type=F32)).astype(BF)
    for p in range(0, outs, 4):
        count = min(4, outs - p)
        part = token_grads(low_grad_t, grad_t, w_all, down_t, (first + p) * tok, count * tok)
        for i in range(count):
            out = parts[p + i]
            out[...] = part[i * tok : (i + 1) * tok].astype(out.dtype)


def attention_call(scale, cots, c_from, qkv_t, low_t, w_all, down_t, up, tok, first, dtypes):
    cols, seq = qkv_t.shape
    rank, width = down_t.shape
    smem = pl.BlockSpec(memory_space=pltpu.SMEM)
    outs = len(dtypes)
    return pl.pallas_call(
        functools.partial(attention_kernel, cols // (3 * HEAD), tok, c_from, first, outs),
        out_shape=[in_vmem((tok, width), t) for t in dtypes]
        + [in_vmem((cols, seq), BF), in_vmem((rank, seq + cols), BF)],
        in_specs=[smem] + whole_vmem(len(cots) + 5),
        out_specs=whole_vmem(outs + 2),
        scratch_shapes=[pltpu.VMEM((cols // 3, seq), BF)],
        compiler_params=pltpu.CompilerParams(vmem_limit_bytes=VMEM),
        cost_estimate=SMALL,
        name="attention_grads",
    )(scale, *vmem(cots), qkv_t, low_t, w_all, down_t, up)


def other_half(x, blocks, dep):
    half = x.shape[1] // 2
    starts = [sum(blocks[:i]) for i in range(len(blocks))]
    if half % 128:
        col = (lax.axis_index("rows") ^ 1) % 2 * half
        return [lax.dynamic_slice(x, (at, col), (rows, half)) for at, rows in zip(starts, blocks)]

    def kernel(x, dep, *outs):
        core = lax.rem(lax.axis_index("rows") ^ 1, 2)
        for at, rows, out in zip(starts, blocks, outs):
            out[...] = x[pl.ds(at, rows), pl.ds(pl.multiple_of(core * half, 128), half)]

    return pl.pallas_call(
        kernel,
        out_shape=[in_vmem((rows, half), x.dtype) for rows in blocks],
        in_specs=whole_vmem(2),
        out_specs=whole_vmem(len(blocks)),
        compiler_params=pltpu.CompilerParams(vmem_limit_bytes=VMEM),
        cost_estimate=SMALL,
        name="other_half",
    )(*vmem([x, dep]))


def add(a, b):
    def kernel(a, b, out):
        out[...] = (a[...] + b[...].astype(F32)).astype(BF)

    return pl.pallas_call(
        kernel,
        out_shape=in_vmem(a.shape, BF),
        in_specs=whole_vmem(2),
        out_specs=whole_vmem(1)[0],
        compiler_params=pltpu.CompilerParams(vmem_limit_bytes=VMEM),
        cost_estimate=SMALL,
        name="add",
    )(*vmem([a, b]))


def own_kernel(deps, grad_t, pack, w_all, down_t, *refs):
    mine, rest = refs[deps], refs[deps + 1 :]
    tok = mine.shape[0]
    part = token_grads(pack, grad_t, w_all, down_t, 0, 2 * tok)
    mine[...] = part[:tok]
    part = part[tok:].astype(BF)
    at = 0
    for out in rest:
        out[...] = part[at : at + out.shape[0]]
        at += out.shape[0]


def own_call(grad_t, pack, w_all, down_t, tok, blocks, deps):
    width = down_t.shape[1]
    return pl.pallas_call(
        functools.partial(own_kernel, len(deps)),
        out_shape=[in_vmem((tok, width), F32)] + [in_vmem((rows, width), BF) for rows in blocks],
        in_specs=whole_vmem(4 + len(deps)),
        out_specs=whole_vmem(1 + len(blocks)),
        compiler_params=pltpu.CompilerParams(vmem_limit_bytes=VMEM),
        cost_estimate=SMALL,
        name="own_grads",
    )(grad_t, pack, w_all, down_t, *vmem(deps))


def adapter_kernel(tok, places, *refs):
    packs, (first_x, last_x, down_grad_t, up_grad) = refs[:-4], refs[-4:]
    r = lax.axis_index("rows")
    total = None
    for j, pack in enumerate(packs):
        blocks = [pack[:, pl.ds((q ^ j) * tok, tok)] for q in range(len(packs))]
        term = jnp.concatenate(blocks, axis=1).astype(F32)
        total = term if total is None else total + term
    total = total.astype(BF)
    grad = None
    for x, held in zip((first_x, last_x), places):
        part = jnp.concatenate([total[:, p * tok : (p + 1) * tok] for p in held], axis=1)
        term = jnp.dot(part, x[...], preferred_element_type=F32)
        grad = term if grad is None else grad + term
    down_grad_t[...] = grad
    cols = up_grad.shape[1] // len(packs)
    for j, pack in enumerate(packs):
        if cols % 128 == 0:
            up_grad[:, pl.ds(pl.multiple_of((r ^ j) * cols, 128), cols)] = pack[:, pl.ds(len(packs) * tok, cols)].astype(F32)


def adapter_call(packs, first_x, last_x, places, rank, all_cols, tok):
    down_grad_t, up_grad = pl.pallas_call(
        functools.partial(adapter_kernel, tok, places),
        out_shape=[
            jax.ShapeDtypeStruct((rank, first_x.shape[1]), F32),
            jax.ShapeDtypeStruct((rank, all_cols), F32),
        ],
        in_specs=whole_vmem(len(packs) + 2),
        out_specs=whole_vmem(2),
        compiler_params=pltpu.CompilerParams(vmem_limit_bytes=VMEM),
        cost_estimate=SMALL,
        name="adapter_grads",
    )(*vmem(packs), *vmem([first_x, last_x]))
    cols = all_cols // len(packs)
    if cols % 128:
        for j, pack in enumerate(packs):
            up_grad = lax.dynamic_update_slice(up_grad, pack[:, len(packs) * tok :].astype(F32), (0, (lax.axis_index("rows") ^ j) * cols))
    return down_grad_t, up_grad


def scale_kernel(tokens, gain, inv_rms, mine, *refs):
    blocks, (total, token_gain, scale, slope) = refs[:-4], refs[-4:]
    at = 0
    for block in blocks:
        rows = pl.ds(at, block.shape[0])
        total[rows, :] = mine[rows, :] + block[...].astype(F32)
        at += block.shape[0]
    x = tokens[...].astype(F32)
    inv = inv_rms[...]
    token_gain[...] = x * gain[...]
    scale[...] = inv * gain[...]
    slope[...] = x * (inv * inv * inv * (1.0 / x.shape[1]))


def scale_call(tokens, gain, inv_rms, mine, blocks):
    return pl.pallas_call(
        scale_kernel,
        out_shape=[in_vmem(tokens.shape, F32)] * 4,
        in_specs=whole_vmem(4 + len(blocks)),
        out_specs=whole_vmem(4),
        compiler_params=pltpu.CompilerParams(vmem_limit_bytes=VMEM),
        cost_estimate=SMALL,
        name="scale",
    )(tokens, gain, inv_rms, mine, *vmem(blocks))


def final_kernel(total, token_gain, scale, slope, *refs):
    terms, (out, made, sems) = refs[:-3], refs[-3:]
    count = sems.shape[0]
    rows = made.shape[0] // count
    copies = []
    for i in range(count):
        block = pl.ds(i * rows, rows)
        grad = total[block, :]
        for x in terms:
            grad = grad + x[block, :].astype(F32)
        moment = jnp.sum(grad * token_gain[block, :], -1, keepdims=True)
        made[block, :] = (grad * scale[block, :] - slope[block, :] * moment).astype(BF)
        copies.append(pltpu.make_async_copy(made.at[block], out.at[block], sems.at[i]))
        copies[-1].start()
    for c in copies:
        c.wait()


def final_call(held, terms):
    shape = held[0].shape
    count = 4 if shape[0] % 64 == 0 else 1
    return pl.pallas_call(
        final_kernel,
        out_shape=jax.ShapeDtypeStruct(shape, BF),
        in_specs=whole_vmem(4 + len(terms)),
        out_specs=pl.BlockSpec(memory_space=pltpu.HBM),
        scratch_shapes=[pltpu.VMEM(shape, BF), pltpu.SemaphoreType.DMA((count,))],
        compiler_params=pltpu.CompilerParams(vmem_limit_bytes=VMEM),
        cost_estimate=SMALL,
        name="input_grads",
    )(*vmem(held), *vmem(terms))


def shares_kernel(chips, pair_cols, weight, *refs):
    r, d = lax.axis_index("rows"), lax.axis_index("dp")
    outs, sems = refs[:-1], refs[-1]
    cols = pair_cols + outs[0].shape[1]
    copies = []
    for i, j in enumerate(chips):
        half = outs[2 * i].shape[0]
        row = pl.multiple_of(lax.div(lax.rem(d, 4), 2) * half, 16)
        col = pl.multiple_of((r ^ (j + lax.rem(d, 2))) * cols + pair_cols, 128)
        copies.append((weight.at[pl.ds(row, half), pl.ds(col, cols - pair_cols)], outs[2 * i]))
        col = pl.multiple_of((r ^ (j + lax.rem(lax.div(d, 2), 2))) * cols, 128)
        copies.append((weight.at[:, pl.ds(col, pair_cols)], outs[2 * i + 1]))
    copies = [pltpu.make_async_copy(a, b, sems.at[i]) for i, (a, b) in enumerate(copies)]
    for c in copies:
        c.start()
    for c in copies:
        c.wait()


def shares_call(weight, chips, cols, pair_cols):
    rows = weight.shape[0]
    count = 2 * len(chips)
    return pl.pallas_call(
        functools.partial(shares_kernel, chips, pair_cols),
        out_shape=[in_vmem((rows // 2, cols - pair_cols), BF), in_vmem((rows, pair_cols), BF)] * len(chips),
        in_specs=[pl.BlockSpec(memory_space=pltpu.HBM)],
        out_specs=whole_vmem(count),
        scratch_shapes=[pltpu.SemaphoreType.DMA((count,))],
        compiler_params=pltpu.CompilerParams(vmem_limit_bytes=VMEM),
        cost_estimate=SMALL,
        name="shares",
    )(*hbm([weight]))


def prepare_kernel(chips, head_cols, sizes, features, gain_map, tokens, core_tokens, cot, *refs):
    count, outs = len(sizes), len(sizes) + len(chips)
    normed, core_normed, gain, inv_rms = refs[count : count + 4]
    cut = refs[count + 4 : count + 4 + outs]
    map_in, tokens_in, core_in, sems = refs[count + 4 + outs :]
    r = lax.axis_index("rows")
    copies = [(tokens, tokens_in), (core_tokens, core_in), (gain_map, map_in)]
    for x, size, out in zip(refs, sizes, cut):
        copies.append((x.at[:, pl.ds(pl.multiple_of(r * size, 128), size)] if size else x, out))
    for j, out in zip(chips, cut[count:]):
        chip = lax.div(r ^ j, 2) * (2 * head_cols)
        copies.append((cot.at[:, pl.ds(pl.multiple_of(chip, 128), 2 * head_cols)], out))
    copies = [pltpu.make_async_copy(a, b, sems.at[i]) for i, (a, b) in enumerate(copies)]
    for c in copies:
        c.start()
    half = features.shape[1]
    col = features[...].T
    for c in copies[:3]:
        c.wait()
    total = jnp.sum(col[:, :1] * map_in[:half, :], 0, keepdims=True)
    total = total + jnp.sum(col[:, 1:] * map_in[half:, :], 0, keepdims=True)
    gain[...] = 1.0 + total
    for x, out in ((tokens_in, normed), (core_in, core_normed)):
        x = x[...].astype(F32)
        inv = lax.rsqrt(jnp.mean(x * x, -1, keepdims=True) + EPS)
        if out is normed:
            inv_rms[...] = inv
        out[...] = (x * inv * gain[...]).astype(BF)
    for c in copies[3:]:
        c.wait()


def prepare_call(features, gain_map, tokens, core_tokens, cot, chips, head_cols, arrays):
    tok, width = tokens.shape
    shapes = [((tok, width), BF), ((tok, width), BF), ((1, width), F32), ((tok, 1), F32)]
    shapes += [((x.shape[0], size or x.shape[1]), BF) for x, size in arrays]
    shapes += [((tok, 2 * head_cols), BF)] * len(chips)
    copies = 3 + len(arrays) + len(chips)
    return pl.pallas_call(
        functools.partial(prepare_kernel, chips, head_cols, [size for _, size in arrays]),
        out_shape=[in_vmem(*shape) for shape in shapes],
        in_specs=whole_vmem(1) + [pl.BlockSpec(memory_space=pl.ANY)] * (4 + len(arrays)),
        out_specs=whole_vmem(len(shapes)),
        scratch_shapes=[
            pltpu.VMEM(gain_map.shape, F32),
            pltpu.VMEM((tok, width), BF),
            pltpu.VMEM((tok, width), BF),
            pltpu.SemaphoreType.DMA((copies,)),
        ],
        compiler_params=pltpu.CompilerParams(vmem_limit_bytes=VMEM),
        cost_estimate=SMALL,
        name="prepare",
    )(features, gain_map, tokens, core_tokens, cot, *[x for x, _ in arrays])


def per_device(
    mesh_shape,
    tokens,
    timestep,
    timestep_gain_map,
    query_key_value_weight,
    adapter_down_weight,
    adapter_up_weight,
    head_score_scale,
    heads_output_grad,
):
    dp, n = mesh_shape
    axes = ("dp", "rows")
    r, d = lax.axis_index("rows"), lax.axis_index("dp")

    def send(x, target):
        perm = []
        for a in range(dp):
            for b in range(n):
                a2, b2 = target(a, b)
                perm.append((a * n + b, a2 * n + b2))
        return lax.ppermute(x, axes, perm)

    def to_row(x, j):
        return send(x, lambda a, b: (a, b ^ j))

    tok, width = tokens.shape
    weight, cot_all = query_key_value_weight, heads_output_grad
    k_rows = weight.shape[0]
    cols = weight.shape[1] // n
    head_cols = cot_all.shape[1] // n
    chips = list(range(2, n, 2))

    pair_cols = cols // 2 if cols % 256 == 0 else cols
    half = k_rows // 2
    pair, quad = [], []
    if pair_cols < cols:
        pieces = shares_call(weight, chips, cols, pair_cols)
        quad, pair = list(pieces[0::2]), list(pieces[1::2])
    else:
        pair = [lax.dynamic_slice(weight, (0, (r ^ (j + d // 2 % 2)) * cols), (k_rows, cols)) for j in chips]
    quad = [send(x, lambda a, b, j=j: (a, b ^ (j + a % 2))) for x, j in zip(quad, chips)]
    pair = [send(x, lambda a, b, j=j: (a, b ^ (j + a // 2 % 2))) for x, j in zip(pair, chips)]

    core_weight, core_tokens, core_cot = (to_row(x, 1) for x in (weight, tokens, cot_all))

    def mine(x, size):
        if size % 128 == 0 and x is weight:
            return hbm([x])[0], size
        return (x, size) if size % 128 == 0 else (lax.dynamic_slice(x, (0, r * size), (x.shape[0], size)), 0)

    own_map, own_tokens, own_cot = hbm([timestep_gain_map, tokens, cot_all])
    normed, core_normed, gain, inv_rms, own_w, core_w, own_cot, core_cot, *chip_cot = prepare_call(
        time_features(timestep), own_map, own_tokens, core_tokens, own_cot, chips, head_cols,
        [mine(weight, cols), mine(core_weight, cols), mine(cot_all, head_cols), mine(core_cot, head_cols)],
    )
    arrays = [own_w, core_w, normed, core_normed]
    w_from, x_from = [(0, 0, 0, 1, 0, 0), (1, 0, 1, 1, 0, 0)], [(2, tok), (3, tok)]
    def exchange(x, other):
        return send(x, lambda a, b: (a ^ other, b))

    early = []
    for j, x in zip(chips, quad):
        held = [x, exchange(x, 1), exchange(x, 2)]
        for other, x in enumerate(held):
            w_from.append((len(arrays), pair_cols, j, 4, other, 0))
            arrays.append(x)
        early.append(held[1])
        cut = (half * 3 // 4, half // 4)
        for at, x in zip((0, cut[0]), gate([held[2]], [cut])):
            early.append(exchange(x, 1))
            w_from.append((len(arrays), pair_cols, j, 4, 3, at))
            arrays.append(early[-1])
    for j, x in zip(chips, pair):
        w_from += [(len(arrays), 0, j, 2, 0, 0), (len(arrays) + 1, 0, j, 2, 1, 0)]
        arrays += [x, exchange(x, 2)]

    relay_rows = (tok * 5 // 8, tok * 3 // 8) if tok % 128 == 0 else (tok,)
    chip_normed = [to_row(normed, j) for j in chips]
    later = list(gate(chip_normed, [relay_rows] * len(chips), *early))
    for x in chip_normed:
        x_from.append((len(arrays), x.shape[0]))
        arrays.append(x)

    rank = adapter_up_weight.shape[0]
    down_t = adapter_down_weight.T
    up = adapter_up_weight
    if cols % 128:
        up = lax.dynamic_slice(up, (0, r * cols), (rank, cols))
    places, last_places = (0, 1, *chips), tuple(j + 1 for j in chips)
    first_x, w_all, first_qkv, first_low = qkv_call(
        n, arrays, tuple(x_from), tuple(w_from), down_t, up, len(places) * tok, cols
    )
    last_x, qkv_t, low_t = last_qkv_call(
        tok, places, last_places, [to_row(x, 1) for x in later], w_all, first_qkv, first_low, down_t, up
    )

    cots, c_from = [own_cot, core_cot], [(1, False), (1, False)]
    blocks = (tok * 3 // 4, tok // 4) if tok % 64 == 0 else (tok,)
    for j, x in zip(chips, chip_cot):
        x = to_row(x, j)
        c_from += [(1, True), (len(blocks), False)]
        cots += [x] + [to_row(y, 1) for y in other_half(x, blocks, first_low)]

    *others, grad_t, pack = attention_call(
        head_score_scale, cots, tuple(c_from), qkv_t, low_t, w_all, down_t, up, tok, 2, (F32, BF) * len(chips)
    )

    totals = [add(others[2 * i], to_row(others[2 * i + 1], 1)) for i in range(len(chips))]
    sums = [to_row(x, j) for x, j in zip(totals, chips)]
    packs = {0: pack, 1: to_row(pack, 1)}
    for j in chips:
        packs[j] = to_row(pack, j)
    blocks = (tok * 7 // 8, tok // 8) if tok % 128 == 0 else (tok,)
    mine, *core_part = own_call(grad_t, pack, w_all, down_t, tok, blocks, totals + [packs[j] for j in chips])
    core_part = [to_row(x, 1) for x in core_part]

    for j in chips:
        packs[j ^ 1] = to_row(packs[j], 1)
    down_grad_t, up_grad = adapter_call(
        [packs[j] for j in range(n)], first_x, last_x, (places, last_places), rank, n * cols, tok
    )

    input_grad = final_call(scale_call(tokens, gain, inv_rms, mine, core_part), sums)
    return (input_grad, down_grad_t.T, up_grad)


def solution(mesh):
    in_specs = (
        P(("dp", "rows"), None),
        P("dp"),
        P(),
        P("rows", None),
        P(),
        P(),
        P("rows"),
        P(("dp", "rows"), None),
    )
    out_specs = (P(("dp", "rows"), None), P("dp", None), P("dp", None))
    shape = (mesh.shape["dp"], mesh.shape["rows"])
    return jax.shard_map(
        functools.partial(per_device, shape), mesh=mesh, in_specs=in_specs, out_specs=out_specs, check_vma=False
    )
```
